32 devices in a mesh: dp: 8 (over y, x, core), head: 4 (over z).
Axes of the slice: x: 2, y: 2, z: 4, core: 2. Of those that a mesh axis runs over, the one named last changes fastest.
Arguments:
- images: bfloat16 [160, 200, 768], P(('dp', 'head')), may hold values from -6 to 6
- mask_ids: int32 [160, 75], P(('dp', 'head')), may hold values from 1 to 196, as said below
- rel_index: int32 [200, 200], replicated, may hold values from 0 to 731, as said below
- out_grad: bfloat16 [160, 200, 768], P(('dp', 'head')), may hold values from -6 to 6
- mask_token: float32 [768], replicated, may hold values from -4 to 4
- attn_gain: float32 [768], replicated, may hold values from 0.5 to 1.5
- attn_shift: float32 [768], replicated, may hold values from -1.5 to 1.5
- qkv_weight: bfloat16 [3, 768, 768], P(None, None, 'head'), may hold values from -0.21875 to 0.21875
- qv_bias: float32 [2, 768], P(None, 'head'), may hold values from -1.5 to 1.5
- rel_table: float32 [732, 12], P(None, 'head'), may hold values from -4 to 4
- out_weight: bfloat16 [768, 768], P('head'), may hold values from -1.75 to 1.75
- out_bias: float32 [768], replicated, may hold values from -1.5 to 1.5
- attn_scale: float32 [768], replicated, may hold values from 0.5 to 1.5
- ffn_gain: float32 [768], replicated, may hold values from 0.5 to 1.5
- ffn_shift: float32 [768], replicated, may hold values from -1.5 to 1.5
- up_weight: bfloat16 [768, 3072], P(None, ('dp', 'head')), may hold values from -0.21875 to 0.21875
- up_bias: bfloat16 [3072], P(('dp', 'head')), may hold values from -1.5 to 1.5
- down_weight: bfloat16 [3072, 768], P(('dp', 'head')), may hold values from -0.109375 to 0.109375
- down_bias: float32 [768], replicated, may hold values from -1.5 to 1.5
- ffn_scale: float32 [768], replicated, may hold values from 0.5 to 1.5
Outputs:
- output: bfloat16 [160, 200, 768], P(('dp', 'head'))
- images_grad: bfloat16 [160, 200, 768], P(('dp', 'head'))
- mask_token_grad: float32 [768], replicated
- attn_gain_grad: float32 [768], replicated
- attn_shift_grad: float32 [768], replicated
- qkv_weight_grad: float32 [3, 768, 768], P(None, None, 'head')
- qv_bias_grad: float32 [2, 768], P(None, 'head')
- rel_table_grad: float32 [732, 12], P(None, 'head')
- out_weight_grad: float32 [768, 768], P('head')
- out_bias_grad: float32 [768], replicated
- attn_scale_grad: float32 [768], replicated
- ffn_gain_grad: float32 [768], replicated
- ffn_shift_grad: float32 [768], replicated
- up_weight_grad: float32 [768, 3072], P(None, ('dp', 'head'))
- up_bias_grad: float32 [3072], P(('dp', 'head'))
- down_weight_grad: float32 [3072, 768], P(('dp', 'head'))
- down_bias_grad: float32 [768], replicated
- ffn_scale_grad: float32 [768], replicated
The draws below stay inside these ranges and needn't reach their ends.
Inputs may be any that keep to these rules, and one draw needn't show every extreme that they name: `mask_ids`: each image's 75 ids are distinct patch positions, from 1 to 196. Rows and columns 1 to 196 stand for the patches of a 14 by 14 grid in some order, and there rel_index[q, k] = (dy + 13) * 27 + dx + 13 with (dy, dx) the grid offset of q's patch from k's; row 0 holds 729, column 0 below it 732 - 2, entry [0, 0] holds 731; entries of padding rows and columns are any table rows.
All inputs are finite; a program needn't handle non-finite values.
Results may differ from the reference program's by a relative error of at most 0.015.
Values may be sent and summed in bfloat16 or wider, within the bound.
No kernel may reach another device: no remote copies, remote signals or barrier semaphores. Data moves between devices by JAX's collectives and lax.ppermute only.
A program may use at most 192 MiB of HBM per device.

```python
import jax
import jax.numpy as jnp
from jax import lax

HEADS = 12
HEAD_DIM = 64
D = 768
FF = 3072
GRID = 14
SEQ = 200
VALID = 197
NREL = 732
NMASK = 75
IMG_DEV = 5
IMAGES = 160


def shuffle_one(subkey):
    return jax.random.permutation(subkey, GRID * GRID)


def draw_rel_index(key, part):
    shuffled = jax.random.permutation(jax.random.fold_in(key, 11), GRID * GRID)
    grid_rows = shuffled // GRID
    grid_cols = shuffled % GRID
    rel_rows = grid_rows[:, None] - grid_rows[None, :] + GRID - 1
    rel_cols = grid_cols[:, None] - grid_cols[None, :] + GRID - 1
    inside = rel_rows * (2 * GRID - 1) + rel_cols
    distinct = (2 * GRID - 1) ** 2
    filler = jax.random.randint(jax.random.fold_in(key, 12), (SEQ, SEQ), 0, distinct + 3)
    indices = filler.at[1:VALID, 1:VALID].set(inside)
    indices = indices.at[0, :].set(distinct)
    indices = indices.at[:, 0].set(distinct + 1)
    indices = indices.at[0, 0].set(distinct + 2)
    return indices.astype(jnp.int32)


def draw_mask_ids(key, part):
    subkeys = jax.random.split(jax.random.fold_in(key, 21), IMAGES)
    picks = jax.vmap(shuffle_one)(subkeys)
    drawn = picks[:, :NMASK] + 1
    middle_pick = jax.random.permutation(jax.random.fold_in(key, 22), GRID * GRID - 2)[:NMASK - 2] + 2
    with_ends = jnp.concatenate([jnp.array([1, GRID * GRID], dtype=jnp.int32), middle_pick.astype(jnp.int32)])
    return drawn.astype(jnp.int32).at[0].set(with_ends)


def steps_of(own_key, extent, cuts, smallest, largest):
    factor_of, own = 1.0, jax.random.fold_in(own_key, 6)
    for dim, shards_of in cuts:
        heights = jnp.exp(jax.random.uniform(jax.random.fold_in(own, dim), (shards_of,), jnp.float32, smallest / len(cuts), largest / len(cuts)))
        factor_of = factor_of * jnp.repeat(heights, extent[dim] // shards_of).reshape([-1 if axis == dim else 1 for axis in range(len(extent))])
    return factor_of


def scatter_about(stream_key, extent, spread, bound, cuts=(), kind=jnp.bfloat16):
    values = jax.random.normal(stream_key, extent, jnp.float32) * spread
    if len(cuts) > 0:
        values = steps_of(stream_key, extent, cuts, -0.22, 0.18) * values
    return jnp.clip(values, min=-bound, max=bound).astype(kind)


def setup_inputs(seed: int = 0) -> dict:
    key_of = jax.random.split(jax.random.key(seed), 21)
    return {
        "images": scatter_about(key_of[0], (IMAGES, SEQ, D), 1.0, 6.0, ((0, 32),)),
        "mask_ids": draw_mask_ids(jax.random.fold_in(key_of[20], 71), 0),
        "rel_index": draw_rel_index(jax.random.fold_in(key_of[20], 71), 0),
        "out_grad": scatter_about(key_of[3], (IMAGES, SEQ, D), 1.0, 6.0, ((0, 32),)),
        "mask_token": scatter_about(key_of[4], (D,), 1.0, 4.0, (), jnp.float32),
        "attn_gain": jnp.clip(1.0 + 0.1 * jax.random.normal(key_of[5], (D,), jnp.float32), 0.5, 1.5),
        "attn_shift": scatter_about(key_of[6], (D,), 0.3, 1.5, (), jnp.float32),
        "qkv_weight": scatter_about(key_of[7], (3, D, D), D ** -0.5, 0.21875, ((2, 4),)),
        "qv_bias": scatter_about(key_of[8], (2, D), 0.3, 1.5, ((1, 4),), jnp.float32),
        "rel_table": scatter_about(key_of[9], (NREL, HEADS), 1.0, 4.0, ((1, 4),), jnp.float32),
        "out_weight": scatter_about(key_of[10], (D, D), (max(D // 64, 1)) ** -0.5, 1.75, ((0, 4),)),
        "out_bias": scatter_about(key_of[11], (D,), 0.3, 1.5, (), jnp.float32),
        "attn_scale": jnp.clip(jax.random.uniform(key_of[12], (D,), jnp.float32, 0.5, 1.5), 0.5, 1.5),
        "ffn_gain": jnp.clip(1.0 + 0.1 * jax.random.normal(key_of[13], (D,), jnp.float32), 0.5, 1.5),
        "ffn_shift": scatter_about(key_of[14], (D,), 0.3, 1.5, (), jnp.float32),
        "up_weight": scatter_about(key_of[15], (D, FF), D ** -0.5, 0.21875, ((1, 32),)),
        "up_bias": scatter_about(key_of[16], (FF,), 0.3, 1.5, ((0, 32),)),
        "down_weight": scatter_about(key_of[17], (FF, D), FF ** -0.5, 0.109375, ((0, 32),)),
        "down_bias": scatter_about(key_of[18], (D,), 0.3, 1.5, (), jnp.float32),
        "ffn_scale": jnp.clip(jax.random.uniform(key_of[19], (D,), jnp.float32, 0.5, 1.5), 0.5, 1.5),
    }


EPS = 1e-06
NEG = -1000000000.0
HIGH = lax.Precision.HIGHEST

@jax.custom_vjp
def low(v):
    return lax.optimization_barrier(v.astype(jnp.bfloat16)).astype(jnp.float32)

@jax.custom_vjp
def low_back(v):
    return v

def low_keep(v):
    return (low(v), None)

def low_pass(kept, grad):
    return (grad,)

def back_keep(v):
    return (v, None)

def back_low(kept, grad):
    return (low(grad),)
low.defvjp(low_keep, low_pass)
low_back.defvjp(back_keep, back_low)

def layer_norm(rows, gain, shift):
    row_mean = lax.optimization_barrier(jnp.mean(rows, axis=-1, keepdims=True))
    centered = rows - row_mean
    variance = lax.optimization_barrier(jnp.mean(centered * centered, axis=-1, keepdims=True))
    return centered * lax.rsqrt(variance + EPS) * gain + shift

def block_forward(params, images, masked, keep, flat_index):
    mask_token, attn_gain, attn_shift, qkv_weight, qv_bias, rel_table, out_weight, out_bias, attn_scale, ffn_gain, ffn_shift, up_weight, up_bias, down_weight, down_bias, ffn_scale = params
    count_img = images.shape[0]
    shape_heads = (count_img, SEQ, HEADS, HEAD_DIM)
    hidden = jnp.where(masked[:, :, None], mask_token, images)
    normed_one = low(layer_norm(hidden, attn_gain, attn_shift))
    projected = jnp.einsum('bsd,jde->jbse', normed_one, qkv_weight, precision=HIGH)
    queries = low(low_back((projected[0] + qv_bias[0]) * HEAD_DIM ** (-0.5))).reshape(shape_heads)
    key_vecs = low(low_back(projected[1])).reshape(shape_heads)
    values_in = low(low_back(projected[2] + qv_bias[1])).reshape(shape_heads)
    rel_bias = jnp.take(rel_table, flat_index, axis=0).reshape(SEQ, SEQ, HEADS).transpose(2, 0, 1)
    scores = low_back(jnp.einsum('bqhd,bkhd->bhqk', queries, key_vecs, precision=HIGH) + rel_bias[None])
    scores = jnp.where(keep, scores, NEG)
    attn_probs = low(jax.nn.softmax(scores, axis=-1))
    attended = low(low_back(jnp.einsum('bhqk,bkhd->bqhd', attn_probs, values_in, precision=HIGH)))
    attended = attended.reshape(count_img, SEQ, HEADS * HEAD_DIM)
    branch = low_back(jnp.einsum('bse,ed->bsd', attended, out_weight, precision=HIGH) + out_bias)
    middle = hidden + attn_scale * branch
    normed_two = low(layer_norm(middle, ffn_gain, ffn_shift))
    pre_act = low_back(jnp.einsum('bsd,df->bsf', normed_two, up_weight, precision=HIGH) + up_bias)
    activated = low(jax.nn.gelu(pre_act, approximate=False))
    mlp_out = low_back(jnp.einsum('bsf,fd->bsd', activated, down_weight, precision=HIGH) + down_bias)
    return middle + ffn_scale * mlp_out

def reference(images, mask_ids, rel_index, out_grad, mask_token, attn_gain, attn_shift, qkv_weight, qv_bias, rel_table, out_weight, out_bias, attn_scale, ffn_gain, ffn_shift, up_weight, up_bias, down_weight, down_bias, ffn_scale):
    params = tuple((value.astype(jnp.float32) for value in (mask_token, attn_gain, attn_shift, qkv_weight, qv_bias, rel_table, out_weight, out_bias, attn_scale, ffn_gain, ffn_shift, up_weight, up_bias, down_weight, down_bias, ffn_scale)))
    positions = jnp.arange(SEQ, dtype=jnp.int32)
    masked = jnp.any(mask_ids[:, :, None] == positions[None, None, :], axis=1)
    keep = positions < VALID
    flat_index = rel_index.reshape(-1).astype(jnp.int32)
    blocks = IMAGES // IMG_DEV
    block_images = images.astype(jnp.float32).reshape(blocks, IMG_DEV, SEQ, D)
    block_masked = masked.reshape(blocks, IMG_DEV, SEQ)
    block_grads = out_grad.astype(jnp.float32).reshape(blocks, IMG_DEV, SEQ, D)

    def accumulate(totals, block_data):
        these_images, these_masked, these_grads = block_data

        def forward_only(values, inputs):
            return block_forward(values, inputs, these_masked, keep, flat_index)
        result, pullback = jax.vjp(forward_only, params, these_images)
        param_grads, input_grads = pullback(these_grads)
        return (jax.tree.map(jnp.add, totals, param_grads), (result.astype(jnp.bfloat16), input_grads.astype(jnp.bfloat16)))
    start_totals = jax.tree.map(jnp.zeros_like, params)
    totals, outputs = lax.scan(accumulate, start_totals, (block_images, block_masked, block_grads))
    output = outputs[0].reshape(IMAGES, SEQ, D)
    images_grad = outputs[1].reshape(IMAGES, SEQ, D)
    return (output, images_grad, totals[0], totals[1], totals[2], totals[3], totals[4], totals[5], totals[6], totals[7], totals[8], totals[9], totals[10], totals[11], totals[12], totals[13], totals[14], totals[15])
```

```python
from functools import partial

import jax
import jax.numpy as jnp
from jax import lax
from jax.experimental import pallas as pl
from jax.experimental.pallas import tpu as pltpu
from jax.sharding import PartitionSpec as P

HEAD_DIM = 64
SEQ = 200
VALID = 197
ROWS = 208
D = 768
HALF = 384
TABLE = 768
REACH = 384
CENTRE = 364
EPS = 1e-06
NEG = -1000000000.0
BOTH = ("dp", "head")
BF = jnp.bfloat16
F32 = jnp.float32
MIB = 1 << 20


def nn(a, b):
    return lax.dot_general(a, b, (((1,), (0,)), ((), ())), preferred_element_type=F32)


def nt(a, b):
    return lax.dot_general(a, b, (((1,), (1,)), ((), ())), preferred_element_type=F32)


def tn(a, b):
    return lax.dot_general(a, b, (((0,), (0,)), ((), ())), preferred_element_type=F32)


def norm_stats(rows):
    row_mean = jnp.mean(rows, axis=-1, keepdims=True)
    centered = rows - row_mean
    inv_std = lax.rsqrt(jnp.mean(centered * centered, axis=-1, keepdims=True) + EPS)
    return centered * inv_std, inv_std


def norm_back(grad_normed, normal, inv_std, gain):
    scaled = grad_normed * gain
    return inv_std * (
        scaled
        - jnp.mean(scaled, axis=-1, keepdims=True)
        - normal * jnp.mean(scaled * normal, axis=-1, keepdims=True)
    )


def swap_halves(core, value):
    low, high = value[:, :HALF], value[:, HALF:]
    first = core == 0
    return jnp.where(first, low, high), jnp.where(first, high, low)


def column_sum(value):
    return jnp.sum(value, axis=0, keepdims=True)


def split_two(value):
    high = value.astype(BF)
    return high, (value - high.astype(F32)).astype(BF)


def call(kernel, name, grid, in_specs, out_specs, out_shape, scratch=(), prefetch=0, vmem=48, flops=0, moved=0, aliases=None):
    return pl.pallas_call(
        kernel,
        name=name,
        grid_spec=pltpu.PrefetchScalarGridSpec(
            num_scalar_prefetch=prefetch,
            grid=grid,
            in_specs=in_specs,
            out_specs=out_specs,
            scratch_shapes=list(scratch),
        ),
        out_shape=out_shape,
        input_output_aliases=aliases or {},
        compiler_params=pltpu.CompilerParams(vmem_limit_bytes=vmem * MIB),
        cost_estimate=pl.CostEstimate(flops=int(flops), bytes_accessed=int(moved), transcendentals=0),
    )


def whole(shape):
    count = len(shape)
    return pl.BlockSpec(shape, lambda *_: (0,) * count)


def rows_of(width):
    return pl.BlockSpec((ROWS, width), lambda i, *_: (i, 0))


def image_of(width):
    return pl.BlockSpec((1, SEQ, width), lambda i, *_: (i, 0, 0))


def like(shape, dtype):
    return jax.ShapeDtypeStruct(shape, dtype)


def start_kernel(place, images, masked, out_grad, token, gain, shift, ffn_scale, normed, grad_mlp, sums):
    step = pl.program_id(0)
    hidden = jnp.where(masked[0] > 0.0, token[...], images[0].astype(F32))
    normal, _ = norm_stats(hidden)
    rows = normal * gain[...] + shift[...]
    low, high = swap_halves(place[0], rows)
    normed[0:SEQ, 0:HALF] = low.astype(BF)
    normed[0:SEQ, HALF:D] = high.astype(BF)
    normed[SEQ:ROWS, :] = jnp.zeros((ROWS - SEQ, D), BF)
    scaled = (out_grad[0].astype(F32) * ffn_scale[...]).astype(BF)
    grad_mlp[0:SEQ, :] = scaled
    grad_mlp[SEQ:ROWS, :] = jnp.zeros((ROWS - SEQ, D), BF)

    @pl.when(step == 0)
    def _():
        sums[...] = jnp.zeros_like(sums)

    sums[0:1, :] += column_sum(scaled.astype(F32))


def start(place, images, masked, out_grad, token, gain, shift, ffn_scale):
    count = images.shape[0]
    return call(
        start_kernel,
        "start",
        (count,),
        [image_of(D), image_of(1), image_of(D)] + [whole((1, D))] * 4,
        [rows_of(D), rows_of(D), whole((8, D))],
        [like((count * ROWS, D), BF), like((count * ROWS, D), BF), like((8, D), F32)],
        prefetch=1,
        flops=count * SEQ * D * 30,
        moved=count * SEQ * D * 8,
    )(place, images, masked, out_grad, token, gain, shift, ffn_scale)


def bias_kernel(spots_down, spots_across, edge_rows, table_ref, table_turned, bias, picked):
    heads = table_ref.shape[0]
    down = spots_down[...]
    across = spots_across[...]
    ones_down = (down == lax.broadcasted_iota(jnp.int32, (ROWS, REACH), 1)).astype(BF)
    ones_across = (across == lax.broadcasted_iota(jnp.int32, (REACH, ROWS), 0)).astype(BF)
    reach = lax.broadcasted_iota(jnp.int32, (ROWS, TABLE), 1)
    turned_high, turned_low = split_two(table_turned[...])
    for edge in range(SEQ - VALID):
        hot = (edge_rows[:, edge : edge + 1] == reach).astype(BF)
        picked[edge] = nn(hot, turned_high) + nn(hot, turned_low)
    key = lax.broadcasted_iota(jnp.int32, (ROWS, ROWS), 0)
    query = lax.broadcasted_iota(jnp.int32, (ROWS, ROWS), 1)
    for head in range(heads):
        line = table_ref[head : head + 1, :]
        spread = []
        for chunk in range(REACH // 128):
            turned = pltpu.roll(jnp.broadcast_to(line, (8, TABLE)), (TABLE - CENTRE + chunk * 128) % TABLE, 1)
            turned = jnp.broadcast_to(turned[0:1], (128, TABLE))
            spread.append(pltpu.roll(turned, 0, 1, stride=1, stride_axis=0)[:, :REACH])
        spread = jnp.concatenate(spread, axis=0)
        high, low = split_two(spread)
        middle = nn(nn(ones_down, high).astype(BF), ones_across)
        middle += nn(nn(ones_down, low).astype(BF), ones_across)
        value = jnp.where(key == 0, line[:, 730:731], middle)
        value = jnp.where(query == 0, jnp.where(key == 0, line[:, 731:732], line[:, 729:730]), value)
        for edge in range(SEQ - VALID):
            value = jnp.where(query == VALID + edge, picked[edge][:, head : head + 1], value)
        bias[head] = jnp.where(key >= VALID, NEG, value)


def bias_of(spots_down, spots_across, edge_rows, table, table_turned):
    heads = table.shape[0]
    return call(
        bias_kernel,
        "bias",
        (1,),
        [
            whole(spots_down.shape),
            whole(spots_across.shape),
            whole(edge_rows.shape),
            whole(table.shape),
            whole(table_turned.shape),
        ],
        whole((heads, ROWS, ROWS)),
        like((heads, ROWS, ROWS), F32),
        scratch=[pltpu.VMEM((SEQ - VALID, ROWS, 128), F32)],
        flops=heads * 4 * ROWS * REACH * REACH,
        moved=heads * ROWS * ROWS * 4,
    )(spots_down, spots_across, edge_rows, table, table_turned)


def table_kernel(spots_down, spots_across, edge_rows, grad_a, grad_b, out):
    each = grad_a.shape[0]
    down = spots_down[...]
    across = spots_across[...]
    ones_turned = ((REACH - 1) - across == lax.broadcasted_iota(jnp.int32, (REACH, ROWS), 0)).astype(BF)
    ones_turned = jnp.where(across >= 0, ones_turned, jnp.zeros_like(ones_turned))
    ones_down = (down == lax.broadcasted_iota(jnp.int32, (ROWS, REACH), 1)).astype(BF)
    reach = lax.broadcasted_iota(jnp.int32, (ROWS, TABLE), 1)
    line = lax.broadcasted_iota(jnp.int32, (1, TABLE), 1)
    key = lax.broadcasted_iota(jnp.int32, (ROWS, 1), 0)
    for head in range(2 * each):
        grads = grad_a if head < each else grad_b
        grad = grads[head % each]
        high, low = split_two(grad)
        both = nn(nn(ones_turned, high).astype(BF), ones_down)
        both += nn(nn(ones_turned, low).astype(BF), ones_down)
        total = jnp.zeros((1, TABLE), F32)
        for chunk in range(REACH // 128):
            rows = both[chunk * 128 : chunk * 128 + 128]
            wide = jnp.concatenate([rows, jnp.zeros((128, TABLE - REACH), F32)], axis=1)
            added = column_sum(pltpu.roll(wide, 0, 1, stride=1, stride_axis=0))
            shift = (TABLE - (REACH - 1 - CENTRE) + chunk * 128) % TABLE
            total += pltpu.roll(jnp.broadcast_to(added, (8, TABLE)), shift, 1)[0:1]
        first = grad[:, 0:1]
        total += jnp.where(line == 729, column_sum(jnp.where(key > 0, first, 0.0)), 0.0)
        total += jnp.where(line == 731, grad[0:1, 0:1], 0.0)
        top = lax.broadcasted_iota(jnp.int32, (1, ROWS), 1)
        row = jnp.where((top > 0) & (top < VALID), grad[0:1, :], 0.0)
        total += jnp.where(line == 730, jnp.sum(row, axis=1, keepdims=True), 0.0)
        for edge in range(SEQ - VALID):
            spot = edge_rows[:, edge : edge + 1] == reach
            total += column_sum(jnp.where(spot, grad[:, VALID + edge : VALID + edge + 1], 0.0))
        out[head : head + 1, :] = total


def table_of(spots_down, spots_across, edge_rows, grad_a, grad_b):
    heads = grad_a.shape[0] * 2
    return call(
        table_kernel,
        "table",
        (1,),
        [
            whole(spots_down.shape),
            whole(spots_across.shape),
            whole(edge_rows.shape),
            whole(grad_a.shape),
            whole(grad_b.shape),
        ],
        whole((heads, TABLE)),
        like((heads, TABLE), F32),
        flops=heads * 4 * ROWS * REACH * REACH,
        moved=heads * ROWS * ROWS * 4,
    )(spots_down, spots_across, edge_rows, grad_a, grad_b)


def project_kernel(mine, other, normed, bias, queries, keys, values, weights):
    planes, groups, blocks, part, _ = mine.shape
    heads = blocks // 4
    for plane in range(planes):
        for group in range(groups):
            for block in range(blocks):
                kind, head = divmod(block, heads)
                at = (group * heads + head) * HEAD_DIM + plane * part
                weights[kind, at : at + part, 0:HALF] = mine[plane, group, block]
                weights[kind, at : at + part, HALF:D] = other[plane, group, block]
    scale = HEAD_DIM ** (-0.5)
    queries[...] = ((nt(normed[...], weights[0]) + bias[0:1, :]) * scale).astype(BF)
    keys[...] = nt(normed[...], weights[1]).astype(BF)
    values[...] = (nt(normed[...], weights[2]) + bias[1:2, :]).astype(BF)


def project(mine, other, normed, bias):
    total = normed.shape[0]
    return call(
        project_kernel,
        "project",
        (1,),
        [whole(mine.shape), whole(other.shape), whole(normed.shape), whole(bias.shape)],
        [whole((total, HALF))] * 3 + [whole((4, HALF, D))],
        [like((total, HALF), BF)] * 3 + [like((4, HALF, D), BF)],
        flops=2 * total * D * HALF * 3,
        moved=8 * MIB,
    )(mine, other, normed, bias)


def attend_kernel(queries, keys, values, bias, attended, probs):
    lane = lax.broadcasted_iota(jnp.int32, (ROWS, 128), 1)
    for pair in range(HALF // 128):
        cols = slice(pair * 128, pair * 128 + 128)
        query_pair, key_pair = queries[:, cols], keys[:, cols]
        turned = values[:, cols].T
        parts = []
        for side in range(2):
            head = pair * 2 + side
            own = (lane >= 64) if side else (lane < 64)
            scores = nt(key_pair, jnp.where(own, query_pair, jnp.zeros_like(query_pair))) + bias[head]
            top = jnp.max(scores, axis=0, keepdims=True)
            expo = jnp.exp(scores - top)
            soft = (expo * (1.0 / jnp.sum(expo, axis=0, keepdims=True))).astype(BF)
            probs[0, head] = soft
            parts.append(nn(turned[side * 64 : side * 64 + 64, :], soft))
        attended[:, cols] = jnp.concatenate(parts, axis=0).T.astype(BF)


def attend(queries, keys, values, bias):
    total = queries.shape[0]
    count, heads = total // ROWS, bias.shape[0]
    return call(
        attend_kernel,
        "attend",
        (count,),
        [rows_of(HALF)] * 3 + [whole(bias.shape)],
        [rows_of(HALF), pl.BlockSpec((1, heads, ROWS, ROWS), lambda i: (i, 0, 0, 0))],
        [like((total, HALF), BF), like((count, heads, ROWS, ROWS), BF)],
        flops=4 * count * heads * ROWS * ROWS * 256,
        moved=10 * MIB,
    )(queries, keys, values, bias)


def attend_back_kernel(queries, keys, values, grad_att, probs, grad_q, grad_k, grad_v, grad_bias):
    step = pl.program_id(0)
    lane = lax.broadcasted_iota(jnp.int32, (ROWS, 128), 1)
    scale = HEAD_DIM ** (-0.5)

    @pl.when(step == 0)
    def _():
        grad_bias[...] = jnp.zeros_like(grad_bias)

    for pair in range(HALF // 128):
        cols = slice(pair * 128, pair * 128 + 128)
        query_pair, value_pair, grad_pair = queries[:, cols], values[:, cols], grad_att[:, cols]
        turned = keys[:, cols].T
        parts_q, parts_k, parts_v = [], [], []
        for side in range(2):
            head = pair * 2 + side
            own = (lane >= 64) if side else (lane < 64)
            soft = probs[0, head]
            wide = soft.astype(F32)
            grad_probs = nt(value_pair, jnp.where(own, grad_pair, jnp.zeros_like(grad_pair)))
            centre = jnp.sum(wide * grad_probs, axis=0, keepdims=True)
            grad_scores = (wide * (grad_probs - centre)).astype(BF)
            grad_bias[head] += grad_scores.astype(F32)
            parts_v.append(nn(soft, grad_pair))
            parts_k.append(nn(grad_scores, query_pair))
            parts_q.append(nn(turned[side * 64 : side * 64 + 64, :], grad_scores))
        grad_v[:, cols] = jnp.where(lane < 64, parts_v[0], parts_v[1]).astype(BF)
        grad_k[:, cols] = jnp.where(lane < 64, parts_k[0], parts_k[1]).astype(BF)
        grad_q[:, cols] = (jnp.concatenate(parts_q, axis=0).T * scale).astype(BF)


def attend_back(queries, keys, values, grad_att, probs):
    total = queries.shape[0]
    count, heads = probs.shape[:2]
    return call(
        attend_back_kernel,
        "attend_back",
        (count,),
        [rows_of(HALF)] * 4 + [pl.BlockSpec((1, heads, ROWS, ROWS), lambda i: (i, 0, 0, 0))],
        [rows_of(HALF)] * 3 + [whole((heads, ROWS, ROWS))],
        [like((total, HALF), BF)] * 3 + [like((heads, ROWS, ROWS), F32)],
        flops=10 * count * heads * ROWS * ROWS * 256,
        moved=10 * MIB,
    )(queries, keys, values, grad_att, probs)


def branch_kernel(
    place, att_a, att_b, out_a, out_b, images, masked, token, out_bias, attn_scale, gain, shift, branch, normed
):
    mixed = nn(att_a[...], out_a[0]) + nn(att_b[...], out_b[0])
    low, high = swap_halves(place[0], mixed)
    rows = jnp.concatenate([low, high], axis=1) + out_bias[...]
    branch[...] = rows
    hidden = jnp.where(masked[0] > 0.0, token[...], images[0].astype(F32))
    middle = hidden + attn_scale[...] * rows[0:SEQ]
    normal, _ = norm_stats(middle)
    normed[0:SEQ, :] = (normal * gain[...] + shift[...]).astype(BF)
    normed[SEQ:ROWS, :] = jnp.zeros((ROWS - SEQ, D), BF)


def out_weight_spec():
    return pl.BlockSpec((1, HALF, D), lambda i, *_: (3, 0, 0))


def branch_of(place, att_a, att_b, w_a, w_b, images, masked, vectors):
    count = images.shape[0]
    return call(
        branch_kernel,
        "branch",
        (count,),
        [rows_of(HALF), rows_of(HALF), out_weight_spec(), out_weight_spec(), image_of(D), image_of(1)]
        + [whole((1, D))] * len(vectors),
        [rows_of(D), rows_of(D)],
        [like((count * ROWS, D), F32), like((count * ROWS, D), BF)],
        prefetch=1,
        flops=2 * count * ROWS * D * D,
        moved=10 * MIB,
    )(place, att_a, att_b, w_a, w_b, images, masked, *vectors)


def gelu_both(value):
    cdf = 0.5 * (1.0 + lax.erf(value * (0.5**0.5)))
    pdf = jnp.exp(value * value * -0.5) * 0.3989422804014327
    return value * cdf, cdf + value * pdf


def feed_kernel(first, up_m, down_m, up_o, down_o, bias, normed, grad_mlp, *rest):
    if first:
        mlp, grad_normed, out_m, out_o, bias_grad, up, down, act, pre = rest
    else:
        _, _, mlp, grad_normed, out_m, out_o, bias_grad, up, down, act, pre = rest
    step = pl.program_id(0)
    half_steps = pl.num_programs(0) // 2
    slots, part = up_m.shape[0], up_m.shape[1]
    units = slots * part
    mine = step < half_steps

    def pick(up_ref, down_ref):
        for slot in range(slots):
            up[slot * part : slot * part + part, :] = up_ref[slot]
            down[slot * part : slot * part + part, :] = down_ref[slot]

    @pl.when(mine)
    def _():
        pick(up_m, down_m)

    @pl.when(jnp.logical_not(mine))
    def _():
        pick(up_o, down_o)

    if first:

        @pl.when(step == 0)
        def _():
            mlp[...] = jnp.zeros_like(mlp)
            grad_normed[...] = jnp.zeros_like(grad_normed)
    else:

        @pl.when(step == 0)
        def _():
            mlp[...] = rest[0][...]
            grad_normed[...] = rest[1][...]

    tiles = normed.shape[0] // ROWS

    def tile(index, total):
        at = pl.ds(pl.multiple_of(index * ROWS, ROWS), ROWS)
        value = nt(normed[at, :], up[...]) + bias[0]
        active, slope = gelu_both(value)
        act[at, :] = active.astype(BF)
        grad = (nt(grad_mlp[at, :], down[...]) * slope).astype(BF)
        pre[at, :] = grad
        return total + column_sum(grad.astype(F32))

    bias_grad[0] = lax.fori_loop(0, tiles, tile, jnp.zeros((1, units), F32))
    mlp[...] += nn(act[...], down[...])
    grad_normed[...] += nn(pre[...], up[...])
    grad_up = tn(pre[...], normed[...]).astype(BF)
    grad_down = tn(act[...], grad_mlp[...]).astype(BF)

    def put(ref):
        for slot in range(slots):
            ref[slot, 0:part, :] = grad_up[slot * part : slot * part + part, :]
            ref[slot, part : 2 * part, :] = grad_down[slot * part : slot * part + part, :]

    @pl.when(mine)
    def _():
        put(out_m)

    @pl.when(jnp.logical_not(mine))
    def _():
        put(out_o)


def feed(mine, other, bias, normed, grad_mlp, carried):
    total = normed.shape[0]
    slots, twice, _ = mine.shape
    part = twice // 2
    steps = bias.shape[0]
    take = 2 * slots // steps
    last = steps // 2 - 1
    first = carried is None

    def at_mine(place):
        return lambda i: (jnp.minimum(i, last), place, 0)

    def at_other(place):
        return lambda i: (jnp.maximum(i - last - 1, 0), place, 0)

    block = (take, part, D)
    wide = (take, twice, D)
    units = take * part
    in_specs = [
        pl.BlockSpec(block, at_mine(0)),
        pl.BlockSpec(block, at_mine(1)),
        pl.BlockSpec(block, at_other(0)),
        pl.BlockSpec(block, at_other(1)),
        pl.BlockSpec((1, 1, units), lambda i: (i, 0, 0)),
        whole((total, D)),
        whole((total, D)),
    ]
    operands = [mine, mine, other, other, bias, normed, grad_mlp]
    aliases = {}
    if not first:
        in_specs += [whole((total, D))] * 2
        operands += list(carried)
        aliases = {7: 0, 8: 1}
    return call(
        partial(feed_kernel, first),
        "feed",
        (steps,),
        in_specs,
        [
            whole((total, D)),
            whole((total, D)),
            pl.BlockSpec(wide, at_mine(0)),
            pl.BlockSpec(wide, at_other(0)),
            pl.BlockSpec((1, 1, units), lambda i: (i, 0, 0)),
        ],
        [
            like((total, D), F32),
            like((total, D), F32),
            like(mine.shape, BF),
            like(other.shape, BF),
            like(bias.shape, F32),
        ],
        scratch=[
            pltpu.VMEM((units, D), BF),
            pltpu.VMEM((units, D), BF),
            pltpu.VMEM((total, units), BF),
            pltpu.VMEM((total, units), BF),
        ],
        vmem=56,
        flops=12 * total * D * slots * part * 2,
        moved=20 * MIB,
        aliases=aliases,
    )(*operands)


def middle_kernel(
    place,
    mlp_ref,
    grad_normed,
    branch,
    images,
    masked,
    out_grad,
    out_a,
    out_b,
    token,
    attn_scale,
    gain,
    ffn_scale,
    down_bias,
    output,
    grad_middle,
    grad_branch,
    grad_a,
    grad_b,
    sums,
):
    step = pl.program_id(0)

    @pl.when(step == 0)
    def _():
        sums[...] = jnp.zeros_like(sums)

    hidden = jnp.where(masked[0] > 0.0, token[...], images[0].astype(F32))
    side = branch[0:SEQ, :]
    middle = hidden + attn_scale[...] * side
    mlp = mlp_ref[0:SEQ, :] + down_bias[...]
    output[0] = (middle + ffn_scale[...] * mlp).astype(BF)
    grad_out = out_grad[0].astype(F32)
    sums[0:1, :] += column_sum(grad_out * mlp)
    normal, inv_std = norm_stats(middle)
    grad_two = grad_normed[0:SEQ, :]
    sums[1:2, :] += column_sum(grad_two * normal)
    sums[2:3, :] += column_sum(grad_two)
    grad = grad_out + norm_back(grad_two, normal, inv_std, gain[...])
    grad_middle[0:SEQ, :] = grad
    grad_middle[SEQ:ROWS, :] = jnp.zeros((ROWS - SEQ, D), F32)
    sums[3:4, :] += column_sum(grad * side)
    low_branch = (grad * attn_scale[...]).astype(BF)
    sums[4:5, :] += column_sum(low_branch.astype(F32))
    low, high = swap_halves(place[0], low_branch)
    grad_branch[0:SEQ, 0:HALF] = low
    grad_branch[0:SEQ, HALF:D] = high
    grad_branch[SEQ:ROWS, :] = jnp.zeros((ROWS - SEQ, D), BF)
    grad_a[...] = nt(grad_branch[...], out_a[0]).astype(BF)
    grad_b[...] = nt(grad_branch[...], out_b[0]).astype(BF)


def middle_of(place, mlp, grad_normed, branch, images, masked, out_grad, w_a, w_b, vectors):
    count = images.shape[0]
    total = count * ROWS
    return call(
        middle_kernel,
        "middle",
        (count,),
        [rows_of(D)] * 3
        + [image_of(D), image_of(1), image_of(D), out_weight_spec(), out_weight_spec()]
        + [whole((1, D))] * len(vectors),
        [image_of(D), rows_of(D), rows_of(D), rows_of(HALF), rows_of(HALF), whole((8, D))],
        [
            like((count, SEQ, D), BF),
            like((total, D), F32),
            like((total, D), BF),
            like((total, HALF), BF),
            like((total, HALF), BF),
            like((8, D), F32),
        ],
        prefetch=1,
        flops=2 * total * D * D,
        moved=20 * MIB,
    )(place, mlp, grad_normed, branch, images, masked, out_grad, w_a, w_b, *vectors)


def weight_kernel(grad_q, grad_k, grad_v, attended, normed, grad_branch, mine, other, sums):
    planes, groups, blocks, part, _ = mine.shape
    heads = blocks // 4
    for kind, (left, right) in enumerate(
        ((grad_q, normed), (grad_k, normed), (grad_v, normed), (attended, grad_branch))
    ):
        grad = tn(left[...], right[...]).astype(BF)
        for plane in range(planes):
            for group in range(groups):
                for head in range(heads):
                    at = (group * heads + head) * HEAD_DIM + plane * part
                    mine[plane, group, kind * heads + head] = grad[at : at + part, 0:HALF]
                    other[plane, group, kind * heads + head] = grad[at : at + part, HALF:D]
    sums[...] = jnp.zeros_like(sums)
    sums[0:1, :] = column_sum(grad_q[...].astype(F32))
    sums[1:2, :] = column_sum(grad_v[...].astype(F32))


def weights_of(grads, attended, normed, grad_branch, shape):
    total = normed.shape[0]
    return call(
        weight_kernel,
        "weights",
        (1,),
        [whole((total, HALF))] * 4 + [whole((total, D))] * 2,
        [whole(shape), whole(shape), whole((8, HALF))],
        [like(shape, BF), like(shape, BF), like((8, HALF), F32)],
        flops=2 * total * D * HALF * 4,
        moved=10 * MIB,
    )(*grads, attended, normed, grad_branch)


def end_kernel(
    place, qa, ka, va, qb, kb, vb, w_a, w_b, grad_middle, images, masked, token, gain, images_grad, sums
):
    step = pl.program_id(0)

    @pl.when(step == 0)
    def _():
        sums[...] = jnp.zeros_like(sums)

    total = nn(qa[...], w_a[0]) + nn(ka[...], w_a[1]) + nn(va[...], w_a[2])
    total += nn(qb[...], w_b[0]) + nn(kb[...], w_b[1]) + nn(vb[...], w_b[2])
    low, high = swap_halves(place[0], total)
    grad_one = jnp.concatenate([low, high], axis=1)[0:SEQ]
    is_masked = masked[0] > 0.0
    hidden = jnp.where(is_masked, token[...], images[0].astype(F32))
    normal, inv_std = norm_stats(hidden)
    sums[0:1, :] += column_sum(grad_one * normal)
    sums[1:2, :] += column_sum(grad_one)
    grad = grad_middle[0:SEQ, :] + norm_back(grad_one, normal, inv_std, gain[...])
    images_grad[0] = jnp.where(is_masked, 0.0, grad).astype(BF)
    sums[2:3, :] += column_sum(jnp.where(is_masked, grad, 0.0))


def end_of(place, grads_a, grads_b, w_a, w_b, grad_middle, images, masked, vectors):
    count = images.shape[0]
    return call(
        end_kernel,
        "end",
        (count,),
        [rows_of(HALF)] * 6
        + [pl.BlockSpec((3, HALF, D), lambda i, *_: (0, 0, 0))] * 2
        + [rows_of(D), image_of(D), image_of(1)]
        + [whole((1, D))] * len(vectors),
        [image_of(D), whole((8, D))],
        [like((count, SEQ, D), BF), like((8, D), F32)],
        prefetch=1,
        flops=2 * count * ROWS * D * D * 3,
        moved=20 * MIB,
    )(place, *grads_a, *grads_b, w_a, w_b, grad_middle, images, masked, *vectors)


def order_kernel(place, gathered, qkv_grad, out_grad, wide):
    core, plane_here = place[0], place[1]
    _, planes, blocks, part, _ = gathered.shape
    heads = blocks // 4
    for plane in range(planes):
        slot = jnp.bitwise_xor(plane_here, plane)
        for block in range(blocks):
            at = block * HEAD_DIM + plane * part
            for half in range(2):
                from_core = jnp.bitwise_xor(core, half)
                wide[at : at + part, half * HALF : half * HALF + HALF] = gathered[
                    from_core, slot, block
                ].astype(F32)
    size = heads * HEAD_DIM
    for kind in range(3):
        qkv_grad[kind] = wide[kind * size : kind * size + size, :].T
    out_grad[...] = wide[3 * size : 4 * size, :]


def order(place, gathered):
    _, planes, blocks, part, _ = gathered.shape
    size = blocks // 4 * HEAD_DIM
    return call(
        order_kernel,
        "order",
        (1,),
        [whole(gathered.shape)],
        [whole((3, D, size)), whole((size, D))],
        [like((3, D, size), F32), like((size, D), F32)],
        scratch=[pltpu.VMEM((4 * size, D), F32)],
        prefetch=1,
        moved=5 * MIB,
    )(place, gathered)


class Butterfly:
    def __init__(self, mesh):
        self.dp, self.head = mesh.shape["dp"], mesh.shape["head"]
        self.far, self.near = 2, 1
        self.core, self.x, self.y = (self.head << bit for bit in range(3))

    def swap(self, value, mask):
        size = self.dp * self.head
        return lax.ppermute(value, BOTH, [(i, i ^ mask) for i in range(size)])

    def grow(self, value, mask):
        return jnp.stack([value, self.swap(value, mask)])

    def fold(self, value, mask):
        return add_low(value[0], self.swap(value[1], mask))


def add_low(own, come):
    return (own.astype(F32) + come.astype(F32)).astype(own.dtype)


def on_device(
    mesh,
    images,
    mask_ids,
    rel_index,
    out_grad,
    mask_token,
    attn_gain,
    attn_shift,
    qkv_weight,
    qv_bias,
    rel_table,
    out_weight,
    out_bias,
    attn_scale,
    ffn_gain,
    ffn_shift,
    up_weight,
    up_bias,
    down_weight,
    down_bias,
    ffn_scale,
):
    count = images.shape[0]
    heads = rel_table.shape[1]
    blocks = 4 * heads
    table_rows = rel_table.shape[0]
    own_units = up_weight.shape[1]
    positions = jnp.arange(SEQ, dtype=jnp.int32)
    masked = jnp.any(mask_ids[:, :, None] == positions, axis=1).astype(F32)[:, :, None]
    net = Butterfly(mesh)
    butterfly = net.dp == 8 and net.head == 4

    def line(vector):
        return vector.reshape(1, -1)

    stacked = jnp.concatenate([jnp.swapaxes(qkv_weight, 1, 2), out_weight[None]], axis=0)
    stacked = stacked.reshape(blocks, HEAD_DIM, D)
    small = jnp.zeros((8, D), F32)
    small = small.at[0:heads, :table_rows].set(rel_table.T)
    small = small.at[heads : heads + 2, : heads * HEAD_DIM].set(qv_bias)
    small = small.at[heads + 2, :own_units].set(up_bias.astype(F32))
    shares = jnp.stack([up_weight.T, down_weight])

    if butterfly:
        dp_here = lax.axis_index("dp")
        core = dp_here % 2
        plane = (dp_here // 2) % 2 * 2 + dp_here // 4
        place = jnp.stack([core, plane]).astype(jnp.int32)
        part = HEAD_DIM // 4
        own = lax.dynamic_slice(stacked, (0, plane * part, core * HALF), (blocks, part, HALF))
        attn = net.grow(net.grow(own, net.far), net.near)
        small_all = net.grow(net.grow(small, net.far), net.near)
        att_in_a = net.grow(net.grow(attn[0], net.y), net.x)
        att_in_b = net.grow(net.grow(attn[1], net.x), net.y)

        def planes(value):
            return value.reshape((4,) + value.shape[2:])

        def turn(value):
            value = jnp.where(dp_here // 2 % 2 == 1, value[:, :, :, ::-1], value)
            return jnp.where(dp_here // 4 == 1, value[:, :, :, :, ::-1], value)

        def by_slot(value):
            value = turn(value.reshape(2, 2, HALF // HEAD_DIM, 2, 2, part))
            return jnp.stack([value[0], value[1].swapaxes(2, 3)]).reshape(2, 2, HALF)

        def by_place(value):
            value = value.reshape(2, 2, HALF // HEAD_DIM, 2, 2, part)
            return turn(jnp.stack([value[0], value[1].swapaxes(2, 3)])).reshape(2, 2, HALF)

        att_in_a, att_in_b = planes(att_in_a), planes(att_in_b)
        attn_pieces = [(v, net.swap(v, net.core)) for v in (att_in_a, att_in_b)]

        half_units = own_units // 2
        ffn = shares.reshape(2, 2, half_units, D).transpose(1, 0, 2, 3).reshape(2, 2 * half_units, D)
        ffn = net.grow(net.grow(ffn, net.far), net.near).reshape(4, 2, 2 * half_units, D)
        ffn_in_a = net.grow(net.grow(ffn[:, 0], net.y), net.x).reshape(16, 2 * half_units, D)
        ffn_in_b = net.grow(net.grow(ffn[:, 1], net.x), net.y).reshape(16, 2 * half_units, D)
        ffn_pieces = [(v, net.swap(v, net.core)) for v in (ffn_in_a, ffn_in_b)]
        unit_bias = small_all[:, :, heads + 2, :own_units].reshape(4, own_units)
        unit_bias = net.grow(net.grow(net.grow(unit_bias, net.y), net.x), net.core)
        bias_a = unit_bias[..., :half_units].reshape(4, 1, -1)
        bias_b = unit_bias[..., half_units:].transpose(0, 2, 1, 3, 4).reshape(4, 1, -1)
        unit_biases = [bias_a, bias_b]
        small_all = small_all.reshape(4, 8, D)
    else:
        place = jnp.zeros((2,), jnp.int32)
        part = HEAD_DIM // 4
        by_slot = by_place = lambda value: value
        gathered = lax.all_gather(stacked, "head", axis=0, tiled=False)
        gathered = gathered.reshape(2, 2, blocks, 4, part, 2, HALF).transpose(0, 5, 3, 1, 2, 4, 6)
        attn_pieces = [(gathered[i, 0], gathered[i, 1]) for i in range(2)]
        ffn = lax.all_gather(shares, BOTH, axis=1, tiled=True)
        units_all = ffn.shape[1]
        half_units = units_all // 64
        ffn = ffn.reshape(2, 2, 2, 16, half_units, D).transpose(1, 2, 3, 0, 4, 5)
        ffn = ffn.reshape(2, 2, 16, 2 * half_units, D)
        ffn_pieces = [(ffn[i, 0], ffn[i, 1]) for i in range(2)]
        small_all = lax.all_gather(small, "head", axis=0, tiled=False)
        unit_bias = lax.all_gather(up_bias.astype(F32), BOTH, axis=0, tiled=True)
        unit_bias = unit_bias.reshape(2, 4, 1, -1)
        unit_biases = [unit_bias[0], unit_bias[1]]

    groups = small_all.shape[0]
    normed_one, grad_mlp, sums_start = start(
        place, images, masked, out_grad, line(mask_token), line(attn_gain), line(attn_shift), line(ffn_scale)
    )

    column = rel_index[:, 1]
    patch = (positions >= 1) & (positions < VALID)
    corner = jnp.min(jnp.where(patch, column, TABLE))
    spots = jnp.where(patch, column - corner, -1)
    spots = jnp.pad(spots, (0, ROWS - SEQ), constant_values=-1)
    spots_down, spots_across = spots[:, None], spots[None, :]
    edge_rows = jnp.pad(rel_index[VALID:, :].T, ((0, ROWS - SEQ), (0, 8 - (SEQ - VALID))))
    table = small_all[:, :heads].reshape(groups * heads, TABLE)
    table_turned = jnp.pad(table.T, ((0, 0), (0, 128 - groups * heads)))
    bias = bias_of(spots_down, spots_across, edge_rows, table, table_turned)
    each = groups * heads // 2
    qv_all = small_all[:, heads : heads + 2, : heads * HEAD_DIM].reshape(2, groups // 2, 2, heads * HEAD_DIM)
    qv_all = by_slot(qv_all.transpose(0, 2, 1, 3).reshape(2, 2, HALF))

    streams = []
    for half in range(2):
        mine, other = attn_pieces[half]
        queries, keys, values, weights = project(mine, other, normed_one, qv_all[half])
        attended, probs = attend(queries, keys, values, bias[half * each : half * each + each])
        streams.append((queries, keys, values, weights, attended, probs))
    w_a, w_b = streams[0][3], streams[1][3]
    branch, normed_two = branch_of(
        place,
        streams[0][4],
        streams[1][4],
        w_a,
        w_b,
        images,
        masked,
        [line(v) for v in (mask_token, out_bias, attn_scale, ffn_gain, ffn_shift)],
    )

    carried = None
    ffn_grads, unit_grads = [], []
    for half in range(2):
        mine, other = ffn_pieces[half]
        mlp, grad_two, grad_m, grad_o, unit_grad = feed(
            mine, other, unit_biases[half], normed_two, grad_mlp, carried
        )
        carried = (mlp, grad_two)
        ffn_grads.append((grad_m, grad_o))
        unit_grads.append(unit_grad)
    output, grad_middle, grad_branch, grad_att_a, grad_att_b, sums_middle = middle_of(
        place,
        carried[0],
        carried[1],
        branch,
        images,
        masked,
        out_grad,
        w_a,
        w_b,
        [line(v) for v in (mask_token, attn_scale, ffn_gain, ffn_scale, down_bias)],
    )
    back, grad_biases = [None, None], [None, None]
    attn_grads, qv_sums = [None, None], [None, None]
    for half in (1, 0):
        queries, keys, values, _, attended, probs = streams[half]
        grad_att = grad_att_a if half == 0 else grad_att_b
        *grads, grad_biases[half] = attend_back(queries, keys, values, grad_att, probs)
        back[half] = grads
        grad_m, grad_o, qv_sums[half] = weights_of(
            grads, attended, normed_one, grad_branch, attn_pieces[half][0].shape
        )
        attn_grads[half] = (grad_m, grad_o)
    images_grad, sums_end = end_of(
        place, back[0], back[1], w_a, w_b, grad_middle, images, masked, [line(mask_token), line(attn_gain)]
    )
    grad_table = table_of(spots_down, spots_across, edge_rows, grad_biases[0], grad_biases[1])

    vectors = jnp.concatenate([sums_start[0:1], sums_middle[0:5], sums_end[0:3]], axis=0)
    qv_grad = by_place(jnp.stack([qv_sums[0][0:2], qv_sums[1][0:2]]))
    qv_grad = qv_grad.reshape(2, 2, groups // 2, heads * HEAD_DIM).transpose(0, 2, 1, 3)
    slots = jnp.concatenate(
        [
            grad_table.reshape(groups, heads, TABLE),
            jnp.pad(qv_grad.reshape(groups, 2, -1), ((0, 0), (0, 0), (0, D - heads * HEAD_DIM))),
        ],
        axis=1,
    )
    extra = slots.shape[1]

    if butterfly:
        sum_a = add_low(ffn_grads[0][0], net.swap(ffn_grads[0][1], net.core))
        sum_b = add_low(ffn_grads[1][0], net.swap(ffn_grads[1][1], net.core))
        tall = 2 * half_units
        sum_a = net.fold(net.fold(sum_a.reshape(2, 2, 4, tall, D), net.x), net.y)
        sum_b = net.fold(net.fold(sum_b.reshape(2, 2, 4, tall, D), net.y), net.x)
        both = jnp.stack([sum_a, sum_b], axis=1).reshape(2, 2, 2, tall, D)
        both = net.fold(net.fold(both, net.near), net.far)
        both = both.reshape(2, 2, half_units, D).transpose(1, 0, 2, 3).reshape(2, own_units, D)
        own_ffn = both.astype(F32)

        sum_b = add_low(attn_grads[1][0], net.swap(attn_grads[1][1], net.core))
        sum_b = net.fold(net.fold(sum_b.reshape((2, 2) + sum_b.shape[1:]), net.y), net.x)
        come = net.swap(sum_b, net.near)
        sum_a = add_low(attn_grads[0][0], net.swap(attn_grads[0][1], net.core))
        sum_a = net.fold(net.fold(sum_a.reshape((2, 2) + sum_a.shape[1:]), net.x), net.y)
        own = net.fold(add_low(sum_a, come), net.far)
        own = net.grow(net.grow(net.grow(own, net.y), net.x), net.core)
        gathered = own.reshape((2, 4) + own.shape[3:])

        units_a = unit_grads[0].reshape(2, 2, 2, 4, half_units)
        units_b = unit_grads[1].reshape(2, 2, 2, 4, half_units).transpose(0, 2, 1, 3, 4)
        units = jnp.concatenate([units_a, units_b], axis=-1)
        units = units.transpose(3, 0, 1, 2, 4).reshape(4, 2, 2, 2, own_units)
        rows = vectors.shape[0] * D
        vectors, slots = vectors.reshape(-1), slots.reshape(groups, -1)
        for mask in (net.near, net.far):
            slots, slots_out = jnp.split(slots, 2)
            units, units_out = jnp.split(units, 2)
            sent = jnp.concatenate([vectors, slots_out.reshape(-1), units_out.reshape(-1)])
            come = net.swap(sent, mask)
            vectors = vectors + come[:rows]
            slots = slots + come[rows : rows + slots.size].reshape(slots.shape)
            units = units + come[rows + slots.size :].reshape(units.shape)
        vectors = jnp.concatenate([vectors, slots.reshape(-1)])
        units = units[0]
        for axis, mask in ((2, net.y), (1, net.x), (0, net.core)):
            units, units_out = jnp.split(units, 2, axis=axis)
            come = net.swap(jnp.concatenate([vectors, units_out.reshape(-1)]), mask)
            vectors = vectors + come[: vectors.size]
            units = units + come[vectors.size :].reshape(units.shape)
        slots = vectors[rows:].reshape(extra, D)
        vectors = vectors[:rows].reshape(-1, D)
        up_bias_grad = units.reshape(own_units)
    else:
        parts = jnp.stack([jnp.stack(attn_grads[i]) for i in range(2)]).astype(F32)
        parts = parts.transpose(0, 3, 4, 2, 5, 1, 6).reshape(groups, blocks, HEAD_DIM, D)
        own = lax.psum_scatter(parts, "head", scatter_dimension=0, tiled=True)
        own = lax.psum(own, "dp").reshape(blocks, 4, part, 2, HALF)
        gathered = own.transpose(3, 1, 0, 2, 4)
        both = jnp.stack([jnp.stack(ffn_grads[i]) for i in range(2)]).astype(F32)
        both = both.reshape(2, 2, 16, 2, half_units, D).transpose(3, 0, 1, 2, 4, 5)
        own_ffn = lax.psum_scatter(
            both.reshape(2, -1, D), BOTH, scatter_dimension=1, tiled=True
        )
        units = jnp.stack(unit_grads).reshape(-1)
        up_bias_grad = lax.psum_scatter(units, BOTH, scatter_dimension=0, tiled=True)
        vectors = lax.psum(vectors, BOTH)
        slots = lax.psum_scatter(slots, "head", scatter_dimension=0, tiled=True)[0]
        slots = lax.psum(slots, "dp")

    qkv_weight_grad, out_weight_grad = order(place, gathered)
    (
        down_bias_grad,
        ffn_scale_grad,
        ffn_gain_grad,
        ffn_shift_grad,
        attn_scale_grad,
        out_bias_grad,
        attn_gain_grad,
        attn_shift_grad,
        mask_token_grad,
    ) = vectors
    return (
        output,
        images_grad,
        mask_token_grad,
        attn_gain_grad,
        attn_shift_grad,
        qkv_weight_grad,
        slots[heads : heads + 2, : heads * HEAD_DIM],
        slots[:heads, :table_rows].T,
        out_weight_grad,
        out_bias_grad,
        attn_scale_grad,
        ffn_gain_grad,
        ffn_shift_grad,
        own_ffn[0].T,
        up_bias_grad,
        own_ffn[1],
        down_bias_grad,
        ffn_scale_grad,
    )


def solution(mesh):
    in_specs = (
        P(("dp", "head"), None, None),
        P(("dp", "head"), None),
        P(),
        P(("dp", "head"), None, None),
        P(),
        P(),
        P(),
        P(None, None, "head"),
        P(None, "head"),
        P(None, "head"),
        P("head", None),
        P(),
        P(),
        P(),
        P(),
        P(None, ("dp", "head")),
        P(("dp", "head")),
        P(("dp", "head"), None),
        P(),
        P(),
    )
    out_specs = (
        P(("dp", "head"), None, None),
        P(("dp", "head"), None, None),
        P(),
        P(),
        P(),
        P(None, None, "head"),
        P(None, "head"),
        P(None, "head"),
        P("head", None),
        P(),
        P(),
        P(),
        P(),
        P(None, ("dp", "head")),
        P(("dp", "head")),
        P(("dp", "head"), None),
        P(),
        P(),
    )
    return jax.shard_map(
        partial(on_device, mesh), mesh=mesh, in_specs=in_specs, out_specs=out_specs, check_vma=False
    )
```

```python
from functools import partial

import jax
import jax.numpy as jnp
from jax import lax
from jax.experimental import pallas as pl
from jax.experimental.pallas import tpu as pltpu
from jax.sharding import PartitionSpec as P

HEAD_DIM = 64
SEQ = 200
VALID = 197
ROWS = 208
D = 768
HALF = 384
TABLE = 768
REACH = 384
CENTRE = 364
EPS = 1e-06
NEG = -1000000000.0
BOTH = ("dp", "head")
BF = jnp.bfloat16
F32 = jnp.float32
MIB = 1 << 20
GRANTS = dict(
    start=8, bias=10, project=16, attend=9, branch=12, feed=14,
    middle=16, attend_back=12, weights=16, end=16, table=14, order=10,
)


def nn(a, b):
    return lax.dot_general(a, b, (((1,), (0,)), ((), ())), preferred_element_type=F32)


def nt(a, b):
    return lax.dot_general(a, b, (((1,), (1,)), ((), ())), preferred_element_type=F32)


def tn(a, b):
    return lax.dot_general(a, b, (((0,), (0,)), ((), ())), preferred_element_type=F32)


def norm_stats(rows):
    row_mean = jnp.mean(rows, axis=-1, keepdims=True)
    centered = rows - row_mean
    inv_std = lax.rsqrt(jnp.mean(centered * centered, axis=-1, keepdims=True) + EPS)
    return centered * inv_std, inv_std


def norm_back(grad_normed, normal, inv_std, gain):
    scaled = grad_normed * gain
    return inv_std * (
        scaled
        - jnp.mean(scaled, axis=-1, keepdims=True)
        - normal * jnp.mean(scaled * normal, axis=-1, keepdims=True)
    )


def swap_halves(core, value):
    low, high = value[:, :HALF], value[:, HALF:]
    first = core == 0
    return jnp.where(first, low, high), jnp.where(first, high, low)


def turn(plane, value, part):
    width = value.shape[1]
    lane = lax.broadcasted_iota(jnp.int32, value.shape, 1)
    for bit in range(2):
        step = part << bit
        other = jnp.where((lane & step) != 0, pltpu.roll(value, step, 1), pltpu.roll(value, width - step, 1))
        value = jnp.where((plane >> bit) % 2 == 1, other, value)
    return value


def column_sum(value):
    return jnp.sum(value, axis=0, keepdims=True)


def split_two(value):
    high = value.astype(BF)
    return high, (value - high.astype(F32)).astype(BF)


def call(kernel, name, grid, in_specs, out_specs, out_shape, scratch=(), prefetch=0, vmem=None, time=5, aliases=None):
    vmem = GRANTS[name]
    return pl.pallas_call(
        kernel,
        name=name,
        grid_spec=pltpu.PrefetchScalarGridSpec(
            num_scalar_prefetch=prefetch,
            grid=grid,
            in_specs=in_specs,
            out_specs=out_specs,
            scratch_shapes=list(scratch),
        ),
        out_shape=out_shape,
        input_output_aliases=aliases or {},
        compiler_params=pltpu.CompilerParams(vmem_limit_bytes=vmem * MIB),
        cost_estimate=pl.CostEstimate(flops=int(time * 4e9), bytes_accessed=MIB, transcendentals=0),
    )


def whole(shape):
    count = len(shape)
    return pl.BlockSpec(shape, lambda *_: (0,) * count)


def once(shape):
    count = len(shape)
    return pl.BlockSpec(shape, lambda *_: (0,) * count, pipeline_mode=pl.Buffered(1))


def three_rows():
    return pl.BlockSpec((3, ROWS, HALF), lambda i, *_: (0, i, 0))


def hbm(*values):
    held = [pltpu.with_memory_space_constraint(value, pltpu.HBM) for value in values]
    return held if len(held) > 1 else held[0]


def in_hbm(shape, dtype):
    return pltpu.HBM(shape, dtype)


def rows_of(width):
    return pl.BlockSpec((ROWS, width), lambda i, *_: (i, 0))


def image_of(width):
    return pl.BlockSpec((1, SEQ, width), lambda i, *_: (i, 0, 0))


def like(shape, dtype):
    return jax.ShapeDtypeStruct(shape, dtype)


def start_kernel(place, images, masked, out_grad, token, gain, shift, ffn_scale, normed, grad_mlp, sums):
    step = pl.program_id(0)
    hidden = jnp.where(masked[0] > 0.0, token[...], images[0].astype(F32))
    normal, _ = norm_stats(hidden)
    rows = normal * gain[...] + shift[...]
    low, high = swap_halves(place[0], rows)
    normed[0:SEQ, 0:HALF] = low.astype(BF)
    normed[0:SEQ, HALF:D] = high.astype(BF)
    normed[SEQ:ROWS, :] = jnp.zeros((ROWS - SEQ, D), BF)
    scaled = (out_grad[0].astype(F32) * ffn_scale[...]).astype(BF)
    grad_mlp[0:SEQ, :] = scaled
    grad_mlp[SEQ:ROWS, :] = jnp.zeros((ROWS - SEQ, D), BF)

    @pl.when(step == 0)
    def _():
        sums[...] = jnp.zeros_like(sums)

    sums[0:1, :] += column_sum(scaled.astype(F32))


def start(place, images, masked, out_grad, token, gain, shift, ffn_scale):
    count = images.shape[0]
    return call(
        start_kernel,
        "start",
        (count,),
        [image_of(D), image_of(1), image_of(D)] + [whole((1, D))] * 4,
        [rows_of(D), rows_of(D), whole((8, D))],
        [like((count * ROWS, D), BF), like((count * ROWS, D), BF), like((8, D), F32)],
        prefetch=1,
        time=4,
    )(place, hbm(images), masked, hbm(out_grad), token, gain, shift, ffn_scale)


def bias_kernel(spots_down, spots_across, edge_rows, small, bias, ones_down, ones_across):
    few = bias.shape[0]

    @pl.when(pl.program_id(0) == 0)
    def _():
        where_down = lax.broadcasted_iota(jnp.int32, (ROWS, REACH), 1)
        where_across = lax.broadcasted_iota(jnp.int32, (REACH, ROWS), 0)
        ones_down[...] = (spots_down[...] == where_down).astype(BF)
        ones_across[...] = (spots_across[...] == where_across).astype(BF)

    table_high, table_low = split_two(small[0])
    reach = lax.broadcasted_iota(jnp.int32, (ROWS, TABLE), 1)
    picked = []
    for edge in range(SEQ - VALID):
        hot = (edge_rows[:, edge : edge + 1] == reach).astype(BF)
        picked.append(nt(hot, table_high) + nt(hot, table_low))
    key = lax.broadcasted_iota(jnp.int32, (ROWS, ROWS), 0)
    query = lax.broadcasted_iota(jnp.int32, (ROWS, ROWS), 1)
    for head in range(few):
        line = small[0, head : head + 1, :]
        spread = []
        for chunk in range(REACH // 128):
            turned = pltpu.roll(jnp.broadcast_to(line, (8, TABLE)), (TABLE - CENTRE + chunk * 128) % TABLE, 1)
            turned = jnp.broadcast_to(turned[0:1], (128, TABLE))
            spread.append(pltpu.roll(turned, 0, 1, stride=1, stride_axis=0)[:, :REACH])
        spread = jnp.concatenate(spread, axis=0)
        high, low = split_two(spread)
        middle = nn(nn(ones_down[...], high).astype(BF), ones_across[...])
        middle += nn(nn(ones_down[...], low).astype(BF), ones_across[...])
        value = jnp.where(key == 0, line[:, 730:731], middle)
        value = jnp.where(query == 0, jnp.where(key == 0, line[:, 731:732], line[:, 729:730]), value)
        for edge in range(SEQ - VALID):
            value = jnp.where(query == VALID + edge, picked[edge][:, head : head + 1], value)
        bias[head] = jnp.where(key >= VALID, NEG, value)


def bias_of(spots_down, spots_across, edge_rows, small, few):
    steps, tall, _ = small.shape
    return call(
        bias_kernel,
        "bias",
        (steps,),
        [
            whole(spots_down.shape),
            whole(spots_across.shape),
            whole(edge_rows.shape),
            pl.BlockSpec((1, tall, TABLE), lambda i: (i, 0, 0)),
        ],
        pl.BlockSpec((few, ROWS, ROWS), lambda i: (i, 0, 0)),
        like((steps * few, ROWS, ROWS), F32),
        scratch=[pltpu.VMEM((ROWS, REACH), BF), pltpu.VMEM((REACH, ROWS), BF)],
        time=6,
    )(spots_down, spots_across, edge_rows, small)


def table_kernel(spots_down, spots_across, edge_rows, grad_a, grad_b, out):
    each = grad_a.shape[0]
    down = spots_down[...]
    across = spots_across[...]
    ones_turned = ((REACH - 1) - across == lax.broadcasted_iota(jnp.int32, (REACH, ROWS), 0)).astype(BF)
    ones_turned = jnp.where(across >= 0, ones_turned, jnp.zeros_like(ones_turned))
    ones_down = (down == lax.broadcasted_iota(jnp.int32, (ROWS, REACH), 1)).astype(BF)
    reach = lax.broadcasted_iota(jnp.int32, (ROWS, TABLE), 1)
    line = lax.broadcasted_iota(jnp.int32, (1, TABLE), 1)
    key = lax.broadcasted_iota(jnp.int32, (ROWS, 1), 0)
    for head in range(2 * each):
        grads = grad_a if head < each else grad_b
        grad = grads[head % each]
        high, low = split_two(grad)
        both = nn(nn(ones_turned, high).astype(BF), ones_down)
        both += nn(nn(ones_turned, low).astype(BF), ones_down)
        total = jnp.zeros((1, TABLE), F32)
        for chunk in range(REACH // 128):
            rows = both[chunk * 128 : chunk * 128 + 128]
            wide = jnp.concatenate([rows, jnp.zeros((128, TABLE - REACH), F32)], axis=1)
            added = column_sum(pltpu.roll(wide, 0, 1, stride=1, stride_axis=0))
            shift = (TABLE - (REACH - 1 - CENTRE) + chunk * 128) % TABLE
            total += pltpu.roll(jnp.broadcast_to(added, (8, TABLE)), shift, 1)[0:1]
        first = grad[:, 0:1]
        total += jnp.where(line == 729, column_sum(jnp.where(key > 0, first, 0.0)), 0.0)
        total += jnp.where(line == 731, grad[0:1, 0:1], 0.0)
        top = lax.broadcasted_iota(jnp.int32, (1, ROWS), 1)
        row = jnp.where((top > 0) & (top < VALID), grad[0:1, :], 0.0)
        total += jnp.where(line == 730, jnp.sum(row, axis=1, keepdims=True), 0.0)
        for edge in range(SEQ - VALID):
            spot = edge_rows[:, edge : edge + 1] == reach
            total += column_sum(jnp.where(spot, grad[:, VALID + edge : VALID + edge + 1], 0.0))
        out[head : head + 1, :] = total


def table_of(spots_down, spots_across, edge_rows, grad_a, grad_b):
    heads = grad_a.shape[0] * 2
    return call(
        table_kernel,
        "table",
        (1,),
        [
            whole(spots_down.shape),
            whole(spots_across.shape),
            whole(edge_rows.shape),
            whole(grad_a.shape),
            whole(grad_b.shape),
        ],
        whole((heads, TABLE)),
        like((heads, TABLE), F32),
        time=9,
    )(spots_down, spots_across, edge_rows, grad_a, grad_b)


def project_kernel(half, has_own, late_x, place, *refs):
    own = refs[0] if has_own else None
    pieces = refs[1 if has_own else 0 :]
    normed, small, outs, weights = pieces[4:]
    kind = pl.program_id(0)
    part = pieces[0].shape[3]
    heads = pieces[0].shape[2] // 4
    skipped = 1 if has_own else 0
    if has_own:
        for head in range(heads):
            for plane in range(4):
                rows = own[kind * heads + head, plane * part : plane * part + part, :]
                low, high = swap_halves(place[0], rows)
                slot = jnp.bitwise_xor(place[1], plane)
                at = pl.ds(pl.multiple_of(head * HEAD_DIM + slot * part, part), part)
                weights[0, at, 0:HALF] = low
                weights[0, at, HALF:D] = high
    for core in range(2):
        for late in range(2):
            piece = pieces[2 * core + late]
            for early in range(2):
                plane = (late * 2 + early) if late_x else (early * 2 + late)
                for group in range(piece.shape[1]):
                    for head in range(heads):
                        at = ((group + skipped) * heads + head) * HEAD_DIM + plane * part
                        weights[0, at : at + part, core * HALF : core * HALF + HALF] = piece[
                            early, group, kind * heads + head
                        ]

    @pl.when(kind < 3)
    def _():
        scale = jnp.where(kind == 0, HEAD_DIM ** (-0.5), 1.0)
        row = pl.ds(heads + kind // 2, 1)
        low = jnp.broadcast_to(small[2 * half, row, 0:HALF], (8, HALF))
        high = jnp.broadcast_to(small[2 * half + 1, row, 0:HALF], (8, HALF))
        shift = turn(place[1], low + pltpu.roll(high, heads * HEAD_DIM, 1), part)[0:1]
        shift = shift * jnp.where(kind == 1, 0.0, 1.0)
        outs[0] = ((nt(normed[...], weights[0]) + shift) * scale).astype(BF)


def project(place, own, late_x, pieces, normed, small, half):
    total = normed.shape[0]
    operands = ([] if own is None else [own]) + list(pieces) + [normed, small]
    return call(
        partial(project_kernel, half, own is not None, late_x),
        "project",
        (4,),
        [once(value.shape) for value in operands],
        [
            pl.BlockSpec((1, total, HALF), lambda t, *_: (jnp.minimum(t, 2), 0, 0)),
            pl.BlockSpec((1, HALF, D), lambda t, *_: (t, 0, 0)),
        ],
        [like((3, total, HALF), BF), in_hbm((4, HALF, D), BF)],
        prefetch=1,
        time=6,
    )(place, *operands)


def attend_kernel(projected, bias, attended, probs):
    lane = lax.broadcasted_iota(jnp.int32, (ROWS, 128), 1)
    for pair in range(HALF // 128):
        cols = slice(pair * 128, pair * 128 + 128)
        query_pair, key_pair = projected[0, :, cols], projected[1, :, cols]
        turned = projected[2, :, cols].T
        parts = []
        for side in range(2):
            head = pair * 2 + side
            own = (lane >= 64) if side else (lane < 64)
            scores = nt(key_pair, jnp.where(own, query_pair, jnp.zeros_like(query_pair))) + bias[head]
            top = jnp.max(scores, axis=0, keepdims=True)
            expo = jnp.exp(scores - top)
            soft = (expo * (1.0 / jnp.sum(expo, axis=0, keepdims=True))).astype(BF)
            probs[0, head] = soft
            parts.append(nn(turned[side * 64 : side * 64 + 64, :], soft))
        attended[:, cols] = jnp.concatenate(parts, axis=0).T.astype(BF)


def attend(projected, bias, half):
    total = projected.shape[1]
    count, heads = total // ROWS, bias.shape[0] // 2
    return call(
        attend_kernel,
        "attend",
        (count,),
        [three_rows(), pl.BlockSpec((heads, ROWS, ROWS), lambda i: (half, 0, 0))],
        [rows_of(HALF), pl.BlockSpec((1, heads, ROWS, ROWS), lambda i: (i, 0, 0, 0))],
        [like((total, HALF), BF), in_hbm((count, heads, ROWS, ROWS), BF)],
        time=9,
    )(projected, bias)


def attend_back_kernel(projected, grad_att, probs, grads, grad_bias):
    step = pl.program_id(0)
    lane = lax.broadcasted_iota(jnp.int32, (ROWS, 128), 1)
    scale = HEAD_DIM ** (-0.5)

    @pl.when(step == 0)
    def _():
        grad_bias[...] = jnp.zeros_like(grad_bias)

    for pair in range(HALF // 128):
        cols = slice(pair * 128, pair * 128 + 128)
        query_pair, value_pair, grad_pair = projected[0, :, cols], projected[2, :, cols], grad_att[:, cols]
        turned = projected[1, :, cols].T
        parts_q, parts_k, parts_v = [], [], []
        for side in range(2):
            head = pair * 2 + side
            own = (lane >= 64) if side else (lane < 64)
            soft = probs[0, head]
            wide = soft.astype(F32)
            grad_probs = nt(value_pair, jnp.where(own, grad_pair, jnp.zeros_like(grad_pair)))
            centre = jnp.sum(wide * grad_probs, axis=0, keepdims=True)
            grad_scores = (wide * (grad_probs - centre)).astype(BF)
            grad_bias[head] += grad_scores.astype(F32)
            parts_v.append(nn(soft, grad_pair))
            parts_k.append(nn(grad_scores, query_pair))
            parts_q.append(nn(turned[side * 64 : side * 64 + 64, :], grad_scores))
        grads[2, :, cols] = jnp.where(lane < 64, parts_v[0], parts_v[1]).astype(BF)
        grads[1, :, cols] = jnp.where(lane < 64, parts_k[0], parts_k[1]).astype(BF)
        grads[0, :, cols] = (jnp.concatenate(parts_q, axis=0).T * scale).astype(BF)


def attend_back(projected, grad_att, probs):
    total = projected.shape[1]
    count, heads = probs.shape[:2]
    return call(
        attend_back_kernel,
        "attend_back",
        (count,),
        [three_rows(), rows_of(HALF), pl.BlockSpec((1, heads, ROWS, ROWS), lambda i: (i, 0, 0, 0))],
        [three_rows(), whole((heads, ROWS, ROWS))],
        [like((3, total, HALF), BF), like((heads, ROWS, ROWS), F32)],
        time=9,
    )(projected, grad_att, hbm(probs))


def branch_kernel(
    place, att_a, att_b, out_a, out_b, images, masked, token, out_bias, attn_scale, gain, shift, branch, normed
):
    mixed = nn(att_a[...], out_a[0]) + nn(att_b[...], out_b[0])
    low, high = swap_halves(place[0], mixed)
    rows = jnp.concatenate([low, high], axis=1) + out_bias[...]
    branch[...] = rows
    hidden = jnp.where(masked[0] > 0.0, token[...], images[0].astype(F32))
    middle = hidden + attn_scale[...] * rows[0:SEQ]
    normal, _ = norm_stats(middle)
    normed[0:SEQ, :] = (normal * gain[...] + shift[...]).astype(BF)
    normed[SEQ:ROWS, :] = jnp.zeros((ROWS - SEQ, D), BF)


def out_weight_spec():
    return pl.BlockSpec((1, HALF, D), lambda i, *_: (3, 0, 0), pipeline_mode=pl.Buffered(1))


def branch_of(place, att_a, att_b, w_a, w_b, images, masked, vectors):
    count = images.shape[0]
    return call(
        branch_kernel,
        "branch",
        (count,),
        [rows_of(HALF), rows_of(HALF), out_weight_spec(), out_weight_spec(), image_of(D), image_of(1)]
        + [whole((1, D))] * len(vectors),
        [rows_of(D), rows_of(D)],
        [in_hbm((count * ROWS, D), F32), like((count * ROWS, D), BF)],
        prefetch=1,
        time=6,
    )(place, att_a, att_b, *hbm(w_a, w_b, images), masked, *vectors)


def gelu_both(value):
    cdf = 0.5 * (1.0 + lax.erf(value * (0.5**0.5)))
    pdf = jnp.exp(value * value * -0.5) * 0.3989422804014327
    return value * cdf, cdf + value * pdf


def feed_kernel(first, half, up_0, up_1, down_0, down_1, bias, normed, grad_mlp, *rest):
    if not first:
        mlp_in, grad_in = rest[:2]
        rest = rest[2:]
    mlp, grad_normed, out, bias_grad, up, down, act, pre = rest
    step = pl.program_id(0)
    slots, part = up_0.shape[0], up_0.shape[1]
    some = slots // 2
    units = slots * part

    @pl.when(step == 0)
    def _():
        for slot in range(slots):
            up[slot * part : slot * part + part, :] = up_0[slot]
        if first:
            mlp[...] = jnp.zeros_like(mlp)
            grad_normed[...] = jnp.zeros_like(grad_normed)
        else:
            mlp[...] = mlp_in[...]
            grad_normed[...] = grad_in[...]

    @pl.when(step == 1)
    def _():
        for slot in range(slots):
            up[slot * part : slot * part + part, :] = up_1[slot]

    for slot in range(slots):
        source = down_0 if slot < some else down_1
        down[slot * part : slot * part + part, :] = source[step, slot % some]

    unit = lax.broadcasted_iota(jnp.int32, (slots, units), 1)
    owner = jnp.zeros_like(unit)
    for slot in range(1, slots):
        owner += (unit >= slot * part).astype(jnp.int32)
    is_own = owner == lax.broadcasted_iota(jnp.int32, (slots, units), 0)
    lane = (unit - owner * part + half * part)[0:1]
    hot = (lax.broadcasted_iota(jnp.int32, (128, units), 0) == lane).astype(BF)
    shift = column_sum(jnp.where(is_own, nn(bias[0].astype(BF), hot), 0.0))
    tiles = normed.shape[0] // ROWS

    def tile(index, total):
        at = pl.ds(pl.multiple_of(index * ROWS, ROWS), ROWS)
        value = nt(normed[at, :], up[...]) + shift
        active, slope = gelu_both(value)
        act[at, :] = active.astype(BF)
        grad = (nt(grad_mlp[at, :], down[...]) * slope).astype(BF)
        pre[at, :] = grad
        return total + column_sum(grad.astype(F32))

    unit_grad = lax.fori_loop(0, tiles, tile, jnp.zeros((1, units), F32))
    unit_high, unit_low = split_two(jnp.where(is_own, unit_grad, 0.0))
    bias_grad[0] = nt(unit_high, hot) + nt(unit_low, hot)
    mlp[...] += nn(act[...], down[...])
    grad_normed[...] += nn(pre[...], up[...])
    grad_up = tn(pre[...], normed[...]).astype(BF)
    grad_down = tn(act[...], grad_mlp[...]).astype(BF)
    for slot in range(slots):
        out[slot, 0:part, :] = grad_up[slot * part : slot * part + part, :]
        out[slot, part : 2 * part, :] = grad_down[slot * part : slot * part + part, :]


def feed(half, core, pieces, bias, normed, grad_mlp, carried):
    total = normed.shape[0]
    slots, part, _ = pieces[0].shape
    units = slots * part
    first = carried is None
    in_specs = [once(piece.shape) for piece in pieces]
    in_specs += [pl.BlockSpec((1, slots, 128), lambda i: (2 * core + i, 0, 0)), once((total, D)), once((total, D))]
    operands = list(pieces) + [bias, normed, grad_mlp]
    aliases = {}
    if not first:
        in_specs += [once((total, D))] * 2
        operands += list(carried)
        aliases = {7: 0, 8: 1}
    return call(
        partial(feed_kernel, first, half),
        "feed",
        (2,),
        in_specs,
        [
            once((total, D)),
            once((total, D)),
            pl.BlockSpec((slots, 2 * part, D), lambda i: (i, 0, 0)),
            pl.BlockSpec((1, slots, 128), lambda i: (i, 0, 0)),
        ],
        [
            like((total, D), F32),
            like((total, D), F32),
            like((2 * slots, 2 * part, D), BF),
            like((2, slots, 128), F32),
        ],
        scratch=[
            pltpu.VMEM((units, D), BF),
            pltpu.VMEM((units, D), BF),
            pltpu.VMEM((total, units), BF),
            pltpu.VMEM((total, units), BF),
        ],
        vmem=48,
        time=16,
        aliases=aliases,
    )(*operands)


def middle_kernel(
    place,
    mlp_ref,
    grad_normed,
    branch,
    images,
    masked,
    out_grad,
    out_a,
    out_b,
    token,
    attn_scale,
    gain,
    ffn_scale,
    down_bias,
    output,
    grad_middle,
    grad_branch,
    grad_a,
    grad_b,
    sums,
):
    step = pl.program_id(0)

    @pl.when(step == 0)
    def _():
        sums[...] = jnp.zeros_like(sums)

    hidden = jnp.where(masked[0] > 0.0, token[...], images[0].astype(F32))
    side = branch[0:SEQ, :]
    middle = hidden + attn_scale[...] * side
    mlp = mlp_ref[0:SEQ, :] + down_bias[...]
    output[0] = (middle + ffn_scale[...] * mlp).astype(BF)
    grad_out = out_grad[0].astype(F32)
    sums[0:1, :] += column_sum(grad_out * mlp)
    normal, inv_std = norm_stats(middle)
    grad_two = grad_normed[0:SEQ, :]
    sums[1:2, :] += column_sum(grad_two * normal)
    sums[2:3, :] += column_sum(grad_two)
    grad = grad_out + norm_back(grad_two, normal, inv_std, gain[...])
    grad_middle[0:SEQ, :] = grad
    grad_middle[SEQ:ROWS, :] = jnp.zeros((ROWS - SEQ, D), F32)
    sums[3:4, :] += column_sum(grad * side)
    low_branch = (grad * attn_scale[...]).astype(BF)
    sums[4:5, :] += column_sum(low_branch.astype(F32))
    low, high = swap_halves(place[0], low_branch)
    grad_branch[0:SEQ, 0:HALF] = low
    grad_branch[0:SEQ, HALF:D] = high
    grad_branch[SEQ:ROWS, :] = jnp.zeros((ROWS - SEQ, D), BF)
    grad_a[...] = nt(grad_branch[...], out_a[0]).astype(BF)
    grad_b[...] = nt(grad_branch[...], out_b[0]).astype(BF)


def middle_of(place, mlp, grad_normed, branch, images, masked, out_grad, w_a, w_b, vectors):
    count = images.shape[0]
    total = count * ROWS
    return call(
        middle_kernel,
        "middle",
        (count,),
        [rows_of(D)] * 3
        + [image_of(D), image_of(1), image_of(D), out_weight_spec(), out_weight_spec()]
        + [whole((1, D))] * len(vectors),
        [image_of(D), rows_of(D), rows_of(D), rows_of(HALF), rows_of(HALF), whole((8, D))],
        [
            like((count, SEQ, D), BF),
            in_hbm((total, D), F32),
            like((total, D), BF),
            like((total, HALF), BF),
            like((total, HALF), BF),
            like((8, D), F32),
        ],
        prefetch=1,
        time=11,
    )(place, mlp, grad_normed, *hbm(branch, images), masked, *hbm(out_grad, w_a, w_b), *vectors)


def weight_kernel(place, grads, attended, normed, grad_branch, mine, other, sums):
    kind = pl.program_id(0)
    planes, groups, heads, part, _ = mine.shape

    def put(left, right):
        grad = tn(left, right).astype(BF)
        for plane in range(planes):
            for group in range(groups):
                for head in range(heads):
                    at = (group * heads + head) * HEAD_DIM + plane * part
                    mine[plane, group, head] = grad[at : at + part, 0:HALF]
                    other[plane, group, head] = grad[at : at + part, HALF:D]

    @pl.when(kind < 3)
    def _():
        put(grads[0], normed[...])
        total = jnp.broadcast_to(column_sum(grads[0].astype(F32)), (8, HALF))
        sums[0] = turn(place[1], total, part)

    @pl.when(kind == 3)
    def _():
        put(attended[...], grad_branch[...])


def weights_of(place, grads, attended, normed, grad_branch, shape):
    total = normed.shape[0]
    planes, groups, blocks, part, _ = shape
    out = pl.BlockSpec((planes, groups, blocks // 4, part, HALF), lambda t, *_: (0, 0, t, 0, 0))
    return call(
        weight_kernel,
        "weights",
        (4,),
        [
            pl.BlockSpec((1, total, HALF), lambda t, *_: (jnp.minimum(t, 2), 0, 0)),
            once((total, HALF)),
            once((total, D)),
            once((total, D)),
        ],
        [out, out, pl.BlockSpec((1, 8, HALF), lambda t, *_: (jnp.minimum(t, 2), 0, 0))],
        [like(shape, BF), like(shape, BF), like((3, 8, HALF), F32)],
        prefetch=1,
        time=5,
    )(place, grads, attended, normed, grad_branch)


def end_kernel(
    place, back_a, back_b, w_a, w_b, grad_middle, images, masked, token, gain, images_grad, sums
):
    step = pl.program_id(0)

    @pl.when(step == 0)
    def _():
        sums[...] = jnp.zeros_like(sums)

    total = nn(back_a[0], w_a[0]) + nn(back_a[1], w_a[1]) + nn(back_a[2], w_a[2])
    total += nn(back_b[0], w_b[0]) + nn(back_b[1], w_b[1]) + nn(back_b[2], w_b[2])
    low, high = swap_halves(place[0], total)
    grad_one = jnp.concatenate([low, high], axis=1)[0:SEQ]
    is_masked = masked[0] > 0.0
    hidden = jnp.where(is_masked, token[...], images[0].astype(F32))
    normal, inv_std = norm_stats(hidden)
    sums[0:1, :] += column_sum(grad_one * normal)
    sums[1:2, :] += column_sum(grad_one)
    grad = grad_middle[0:SEQ, :] + norm_back(grad_one, normal, inv_std, gain[...])
    images_grad[0] = jnp.where(is_masked, 0.0, grad).astype(BF)
    sums[2:3, :] += column_sum(jnp.where(is_masked, grad, 0.0))


def end_of(place, grads_a, grads_b, w_a, w_b, grad_middle, images, masked, vectors):
    count = images.shape[0]
    return call(
        end_kernel,
        "end",
        (count,),
        [three_rows()] * 2
        + [pl.BlockSpec((3, HALF, D), lambda i, *_: (0, 0, 0), pipeline_mode=pl.Buffered(1))] * 2
        + [rows_of(D), image_of(D), image_of(1)]
        + [whole((1, D))] * len(vectors),
        [image_of(D), whole((8, D))],
        [like((count, SEQ, D), BF), like((8, D), F32)],
        prefetch=1,
        time=12,
    )(place, grads_a, grads_b, *hbm(w_a, w_b, grad_middle, images), masked, *vectors)


def order_kernel(place, own, other, qkv_grad, out_grad, wide):
    core, plane_here = place[0], place[1]
    planes, blocks, part, _ = own.shape
    heads = blocks // 4
    for plane in range(planes):
        slot = jnp.bitwise_xor(plane_here, plane)
        for block in range(blocks):
            at = block * HEAD_DIM + plane * part
            for source, side in ((own, core), (other, 1 - core)):
                columns = pl.ds(pl.multiple_of(side * HALF, HALF), HALF)
                wide[at : at + part, columns] = source[slot, block].astype(F32)
    size = heads * HEAD_DIM
    for kind in range(3):
        qkv_grad[kind] = wide[kind * size : kind * size + size, :].T
    out_grad[...] = wide[3 * size : 4 * size, :]


def order(place, gathered):
    planes, blocks, part, _ = gathered[0].shape
    size = blocks // 4 * HEAD_DIM
    return call(
        order_kernel,
        "order",
        (1,),
        [whole(gathered[0].shape)] * 2,
        [whole((3, D, size)), whole((size, D))],
        [like((3, D, size), F32), like((size, D), F32)],
        scratch=[pltpu.VMEM((4 * size, D), F32)],
        prefetch=1,
        time=2,
    )(place, *gathered)


class Butterfly:
    def __init__(self, mesh):
        self.dp, self.head = mesh.shape["dp"], mesh.shape["head"]
        self.far, self.near = 2, 1
        self.core, self.x, self.y = (self.head << bit for bit in range(3))

    def swap(self, value, mask):
        size = self.dp * self.head
        return lax.ppermute(value, BOTH, [(i, i ^ mask) for i in range(size)])


def after(done, *values):
    held = lax.optimization_barrier((done,) + values)[1:]
    return held if len(values) > 1 else held[0]


def tie(*values):
    return lax.optimization_barrier(values)


def add_low(own, come):
    return (own.astype(F32) + come.astype(F32)).astype(own.dtype)


def line(vector):
    return vector.reshape(1, -1)


class Layer:
    def __init__(self, place, args, masked, heads, groups):
        self.place, self.args, self.masked = place, args, masked
        self.heads, self.groups = heads, groups
        self.weights, self.streams, self.carried = [None, None], [None, None], None

    def lines(self, *names):
        return [line(self.args[name]) for name in names]

    def start(self):
        a = self.args
        self.normed_one, self.grad_mlp, self.sums_start = start(
            self.place,
            a["images"],
            self.masked,
            a["out_grad"],
            *self.lines("mask_token", "attn_gain", "attn_shift", "ffn_scale"),
        )
        return self.sums_start

    def spots(self):
        rel_index = self.args["rel_index"]
        positions = jnp.arange(SEQ, dtype=jnp.int32)
        column = rel_index[:, 1]
        patch = (positions >= 1) & (positions < VALID)
        corner = jnp.min(jnp.where(patch, column, TABLE))
        spots = jnp.where(patch, column - corner, -1)
        spots = jnp.pad(spots, (0, ROWS - SEQ), constant_values=-1)
        edges = jnp.pad(rel_index[VALID:, :].T, ((0, ROWS - SEQ), (0, 8 - (SEQ - VALID))))
        self.where = (spots[:, None], spots[None, :], edges)

    def bias(self, small):
        self.small = small
        self.rel_bias = bias_of(*self.where, small, self.heads)
        return self.rel_bias

    def project(self, half, own, late_x, pieces):
        projected, self.weights[half] = project(
            self.place, own, late_x, pieces, self.normed_one, self.small, half
        )
        self.streams[half] = [projected]
        return projected

    def attend(self, half):
        self.streams[half] += attend(self.streams[half][0], self.rel_bias, half)
        return self.streams[half][1]

    def branch(self):
        self.side, self.normed_two = branch_of(
            self.place,
            self.streams[0][1],
            self.streams[1][1],
            self.weights[0],
            self.weights[1],
            self.args["images"],
            self.masked,
            self.lines("mask_token", "out_bias", "attn_scale", "ffn_gain", "ffn_shift"),
        )
        return self.normed_two

    def feed(self, half, core, pieces, bias):
        *self.carried, grads, unit_grads = feed(
            half, core, pieces, bias, self.normed_two, self.grad_mlp, self.carried
        )
        return grads, unit_grads

    def middle(self):
        self.output, self.grad_middle, self.grad_branch, *self.grad_att, self.sums_middle = middle_of(
            self.place,
            *self.carried,
            self.side,
            self.args["images"],
            self.masked,
            self.args["out_grad"],
            self.weights[0],
            self.weights[1],
            self.lines("mask_token", "attn_scale", "ffn_gain", "ffn_scale", "down_bias"),
        )
        self.back, self.grad_bias, self.shift_sums = [None, None], [None, None], [None, None]
        return self.grad_att[0]

    def attend_back(self, half):
        projected, _, probs = self.streams[half]
        self.back[half], self.grad_bias[half] = attend_back(projected, self.grad_att[half], probs)
        return self.grad_bias[half]

    def weight_grads(self, half):
        mine, other, self.shift_sums[half] = weights_of(
            self.place,
            self.back[half],
            self.streams[half][1],
            self.normed_one,
            self.grad_branch,
            (4, self.groups // 2, 4 * self.heads, HEAD_DIM // 4, HALF),
        )
        return mine, other

    def table(self):
        self.grad_table = table_of(*self.where, *self.grad_bias)
        return self.grad_table

    def end(self):
        self.images_grad, self.sums_end = end_of(
            self.place,
            self.back[0],
            self.back[1],
            self.weights[0],
            self.weights[1],
            self.grad_middle,
            self.args["images"],
            self.masked,
            self.lines("mask_token", "attn_gain"),
        )
        return self.sums_end

    def vectors(self):
        heads, groups = self.heads, self.groups
        rows = jnp.concatenate([self.sums_start[0:1], self.sums_middle[0:5], self.sums_end[0:3]], axis=0)
        width = heads * HEAD_DIM
        slots = []
        for group in range(groups):
            half, at = divmod(group, groups // 2)
            slots.append(self.grad_table[group * heads : group * heads + heads])
            sums = self.shift_sums[half][:, 0, at * width : at * width + width]
            slots += [jnp.pad(sums[kind : kind + 1], ((0, 0), (0, D - width))) for kind in (0, 2)]
        return rows, slots


def run_butterfly(net, layer, own_stack, small, shares):
    heads, groups = layer.heads, layer.groups
    dp_here = lax.axis_index("dp")
    core = dp_here % 2
    x_here, y_here = dp_here // 2 % 2, dp_here // 4
    plane = x_here * 2 + y_here
    layer.place = jnp.stack([core, plane]).astype(jnp.int32)
    part = HEAD_DIM // 4
    cut = 2 * heads
    swap = net.swap
    own_units = shares.shape[1]
    half_units = own_units // 2

    mine = lax.dynamic_slice(own_stack, (0, plane * part, core * HALF), (4 * heads, part, HALF))
    far, near = swap(mine, net.far), swap(mine, net.near)
    small_far = swap(small, net.far)
    layer.spots()
    layer.masked, layer.place, *layer.where = tie(layer.masked, layer.place, *layer.where)
    done = layer.start()
    far, near, small_far = after(done, far, near, small_far)
    both = swap(far, net.near)
    small = jnp.stack([small, small_far])
    small_near = swap(small, net.near)

    early_a = jnp.stack([far[None], swap(far[None], net.y)])
    small = jnp.concatenate([small, small_near]).reshape(groups, 8, D)
    late_a = swap(early_a, net.x)
    rest = jnp.stack([near, both])
    early_b = jnp.stack([rest, swap(rest, net.x)])
    ffn = shares.reshape(2, 2, half_units, D).transpose(1, 0, 2, 3).reshape(2, 2 * half_units, D)
    ffn = after(both, ffn)
    ffn_far, ffn_near = swap(ffn, net.far), swap(ffn, net.near)
    unit_bias = small[:, heads + 2, :128]
    unit_y = swap(unit_bias, net.y)
    small, unit_y = tie(small, unit_y)
    layer.bias(small)
    unit_bias = jnp.concatenate([unit_bias, unit_y])
    unit_x = swap(unit_bias, net.x)
    early_a, late_a, early_b = after(layer.rel_bias, early_a, late_a, early_b)
    pieces_a = [early_a, late_a, swap(early_a, net.core), swap(late_a, net.core)]
    late_b = swap(early_b, net.y)
    done = layer.project(0, own_stack, True, pieces_a)
    early_b, late_b, ffn_far, ffn_near, unit_x = after(done, early_b, late_b, ffn_far, ffn_near, unit_x)
    pieces_b = [early_b, late_b, swap(early_b, net.core), swap(late_b, net.core)]
    ffn_both = swap(ffn_far, net.near)
    unit_bias = jnp.stack([unit_bias, unit_x])
    unit_core = swap(unit_bias, net.core)
    done = layer.attend(0)
    pieces_b = list(after(done, *pieces_b))
    done = layer.project(1, None, False, pieces_b)
    ffn_both, unit_core = after(done, ffn_both, unit_core)
    ffn = jnp.stack([ffn, ffn_far, ffn_near, ffn_both], axis=1)
    biases = jnp.concatenate([unit_bias, unit_core])

    def second(pair):
        return [pair[0], swap(pair[0], net.x), pair[1], swap(pair[1], net.y)]

    def crossed(pieces):
        return pieces + [swap(piece, net.core) for piece in pieces]

    def first_ffn(value):
        up, down = value[:, :half_units], value[:, half_units:]
        return [jnp.stack([up, swap(up, net.y)]), jnp.stack([down, swap(down, net.x)])]

    def as_feed(four):
        return [v.reshape(-1, half_units, D) for v in four[:2]] + four[2:]

    ffn_a = first_ffn(ffn[0])
    done = layer.attend(1)
    ffn_a = list(after(done, *ffn_a))
    four_a = second(ffn_a)
    done = layer.branch()
    four_a = list(after(done, *four_a))
    cross_a = crossed(four_a)[4:]
    ffn_b = first_ffn(after(four_a[1], ffn[1]))
    grads_am, unit_am = layer.feed(0, 0, as_feed(four_a), biases)
    ffn_b = list(after(grads_am, *ffn_b))
    cross_a = list(after(grads_am, *cross_a))
    four_b = second(ffn_b)
    grads_ao, unit_ao = layer.feed(0, 1, as_feed(cross_a), biases)

    come_a = swap(grads_ao, net.core)
    four_b = list(after(grads_ao, *four_b))
    cross_b = crossed(four_b)[4:]
    grads_bm, unit_bm = layer.feed(1, 0, as_feed(four_b), biases)
    layer.carried[0], come_a, *cross_b = tie(layer.carried[0], come_a, *cross_b)
    tall = 2 * half_units
    sum_a = add_low(grads_am, come_a).reshape(2, 2, 2, 2, tall, D)
    come_a = swap(sum_a[1], net.x)
    grads_bo, unit_bo = layer.feed(1, 1, as_feed(cross_b), biases)
    come_b = swap(grads_bo, net.core)
    done = layer.middle()
    layer.grad_att[1], come_a, come_b = tie(layer.grad_att[1], come_a, come_b)
    sum_a = add_low(sum_a[0], come_a)
    come_a = swap(sum_a[1], net.y)
    sum_b = grads_bm.reshape(2, 2, 2, 2, tall, D), come_b.reshape(2, 2, 2, 2, tall, D)
    up_b = add_low(sum_b[0][..., :half_units, :], sum_b[1][..., :half_units, :])
    down_b = add_low(sum_b[0][..., half_units:, :], sum_b[1][..., half_units:, :])
    come_up, come_down = swap(up_b[1], net.x), swap(down_b[:, 1], net.y)
    layer.attend_back(1)
    attn_b = layer.weight_grads(1)
    layer.grad_att[0], come_a, come_up, come_down, *attn_b = tie(
        layer.grad_att[0], come_a, come_up, come_down, *attn_b
    )
    come_attn_b = swap(attn_b[1], net.core)
    sum_a = add_low(sum_a[0], come_a)
    come_a = swap(sum_a[1], net.near)
    up_b, down_b = add_low(up_b[0], come_up), add_low(down_b[:, 0], come_down)
    come_up, come_down = swap(up_b[1], net.y), swap(down_b[1], net.x)
    layer.attend_back(0)
    layer.back[0], come_a, come_up, come_down, come_attn_b = tie(
        layer.back[0], come_a, come_up, come_down, come_attn_b
    )
    sum_a = add_low(sum_a[0], come_a)
    come_a = swap(sum_a[1], net.far)
    sum_b = jnp.concatenate([add_low(up_b[0], come_up), add_low(down_b[0], come_down)], axis=-2)
    come_b = swap(sum_b[1], net.near)
    attn_b = add_low(attn_b[0], come_attn_b).reshape(2, 2, 2, 4 * heads, part, HALF)
    come_attn_b = swap(attn_b[1], net.x)
    attn_a = layer.weight_grads(0)
    layer.grad_middle, *attn_a = tie(layer.grad_middle, *attn_a)
    come_attn_a = swap(attn_a[1], net.core)
    layer.end()
    layer.sums_end, layer.grad_bias[0], come_a, come_b, come_attn_a, come_attn_b = tie(
        layer.sums_end, layer.grad_bias[0], come_a, come_b, come_attn_a, come_attn_b
    )
    sum_a, sum_b = add_low(sum_a[0], come_a), add_low(sum_b[0], come_b)
    come_b = swap(sum_b[1], net.far)
    attn_b = add_low(attn_b[0], come_attn_b)
    come_attn_b = swap(attn_b[1], net.y)
    attn_a = [v.reshape(2, 2, 2, 4 * heads, part, HALF) for v in (attn_a[0], come_attn_a)]
    head_a = add_low(attn_a[0][..., :cut, :, :], attn_a[1][..., :cut, :, :])
    tail_a = add_low(attn_a[0][..., cut:, :, :], attn_a[1][..., cut:, :, :])
    come_head, come_tail = swap(head_a[1], net.x), swap(tail_a[:, 1], net.y)
    layer.table()
    layer.grad_table, come_head, come_tail, come_attn_b, come_b = tie(
        layer.grad_table, come_head, come_tail, come_attn_b, come_b
    )
    sum_b = add_low(sum_b[0], come_b)
    attn_b = add_low(attn_b[0], come_attn_b)
    head_a, tail_a = add_low(head_a[0], come_head), add_low(tail_a[:, 0], come_tail)
    come_head, come_tail = swap(head_a[1], net.y), swap(tail_a[1], net.x)
    come_attn_b = swap(attn_b, net.near)

    unit_am, unit_ao, unit_bm, unit_bo = after(layer.sums_end, unit_am, unit_ao, unit_bm, unit_bo)
    rows, slots = layer.vectors()
    extra = heads + 2
    units = [jnp.pad(v.reshape(-1, 128), ((0, 0), (0, D - 128))) for v in (unit_am + unit_bm, unit_ao + unit_bo)]
    fixed = rows.shape[0]

    state = jnp.concatenate([rows] + slots + [units[0]])
    wide = state.shape[0] - units[0].shape[0]
    come = swap(jnp.concatenate([rows] + slots + [units[1]]), net.core)
    come, come_head, come_tail, come_attn_b = tie(come, come_head, come_tail, come_attn_b)
    state = state + come
    head_a, tail_a = add_low(head_a[0], come_head), add_low(tail_a[0], come_tail)
    attn = add_low(jnp.concatenate([head_a, tail_a], axis=1), come_attn_b)

    def halve(state):
        middle = wide + (state.shape[0] - wide) // 2
        return state[:middle], jnp.concatenate([state[:wide], state[middle:]])

    state, sent = halve(state)
    come, last = tie(swap(sent, net.x), swap(attn[1], net.far))
    state = state + come
    own = add_low(attn[0], last)
    low, high = own[:cut], own[cut:]
    state, sent = halve(state)
    come, come_low, come_high = tie(swap(sent, net.y), swap(low, net.y), swap(high, net.x))
    state = state + come
    low, high = jnp.stack([low, come_low]), jnp.stack([high, come_high])
    both = fixed + 2 * extra
    sent = jnp.concatenate([state[:fixed], state[both:wide], state[wide + 2 :]])
    state = jnp.concatenate([state[:both], state[wide : wide + 2]])
    come, come_low, come_high = tie(swap(sent, net.near), swap(low, net.x), swap(high, net.y))
    state = state + come
    low, high = jnp.stack([low, come_low]), jnp.stack([high, come_high], axis=1)
    own = jnp.concatenate([low, high], axis=2).reshape(4, 4 * heads, part, HALF)
    one = fixed + extra
    sent = jnp.concatenate([state[:fixed], state[one:both], state[both + 1 :]])
    state = jnp.concatenate([state[:one], state[both : both + 1]])
    come, other = tie(swap(sent, net.far), swap(own, net.core))
    state = state + come
    rows, slots, units = state[:fixed], state[fixed:one], state[one, :own_units]
    gathered = [own, other]

    own_ffn = jnp.stack([sum_a, sum_b]).reshape(2, 2, half_units, D).transpose(1, 0, 2, 3)
    own_ffn = own_ffn.reshape(2, own_units, D).astype(F32)
    return gathered, own_ffn, units, rows, slots


def run_plain(layer, own_stack, small, shares, up_bias):
    heads, groups = layer.heads, layer.groups
    layer.place = jnp.zeros((2,), jnp.int32)
    part = HEAD_DIM // 4
    blocks = 4 * heads
    attn = lax.all_gather(own_stack, "head", axis=0, tiled=False)
    attn = attn.reshape(2, groups // 2, blocks, 2, 2, part, 2, HALF).transpose(0, 6, 3, 4, 1, 2, 5, 7)
    ffn = lax.all_gather(shares, BOTH, axis=1, tiled=True)
    half_units = ffn.shape[1] // 64
    ffn = ffn.reshape(2, 2, 2, 2, 2, 4, half_units, D)
    small = lax.all_gather(small, "head", axis=0, tiled=False)
    biases = lax.all_gather(up_bias, BOTH, axis=0, tiled=True).reshape(2, 4, 8, half_units)
    biases = jnp.concatenate([biases[0], biases[1]], axis=-1)
    biases = jnp.pad(biases, ((0, 0), (0, 0), (0, 128 - 2 * half_units)))
    layer.start()
    layer.spots()
    layer.bias(small)
    for half in range(2):
        pieces = []
        for core in range(2):
            here = attn[half, core]
            pieces += [here[x] for x in range(2)]
        layer.project(half, None, True, pieces)
        layer.attend(half)
    layer.branch()
    ffn_grads, unit_grads = [], []
    for half in range(2):
        for core in range(2):
            up, down = ffn[0, half, core], ffn[1, half, core]
            pieces = [up[x].reshape(8, half_units, D) for x in range(2)] + [down[:, y] for y in range(2)]
            grads, units = layer.feed(half, core, pieces, biases)
            ffn_grads.append(grads)
            unit_grads.append(units[..., half * half_units : half * half_units + half_units])
    layer.middle()
    attn_grads = []
    for half in range(2):
        layer.attend_back(half)
        attn_grads.append(jnp.stack(layer.weight_grads(half)))
    layer.table()
    layer.end()
    parts = jnp.stack(attn_grads).astype(F32)
    parts = parts.transpose(0, 3, 4, 2, 5, 1, 6).reshape(groups, blocks, HEAD_DIM, D)
    own = lax.psum_scatter(parts, "head", scatter_dimension=0, tiled=True)
    own = lax.psum(own, "dp").reshape(blocks, 4, part, 2, HALF)
    both = jnp.stack(ffn_grads).astype(F32).reshape(2, 2, 16, 2, half_units, D).transpose(3, 0, 1, 2, 4, 5)
    own_ffn = lax.psum_scatter(both.reshape(2, -1, D), BOTH, scatter_dimension=1, tiled=True)
    units = lax.psum_scatter(jnp.stack(unit_grads).reshape(-1), BOTH, scatter_dimension=0, tiled=True)
    rows, slots = layer.vectors()
    slots = jnp.concatenate(slots).reshape(groups, -1, D)
    slots = lax.psum_scatter(slots, "head", scatter_dimension=0, tiled=True)[0]
    return own.transpose(3, 1, 0, 2, 4), own_ffn, units, lax.psum(rows, BOTH), lax.psum(slots, "dp")


NAMES = (
    "images mask_ids rel_index out_grad mask_token attn_gain attn_shift qkv_weight qv_bias rel_table "
    "out_weight out_bias attn_scale ffn_gain ffn_shift up_weight up_bias down_weight down_bias ffn_scale"
).split()


def on_device(mesh, *arrays):
    args = dict(zip(NAMES, arrays))
    rel_table, up_weight = args["rel_table"], args["up_weight"]
    table_rows, heads = rel_table.shape
    own_units = up_weight.shape[1]
    positions = jnp.arange(SEQ, dtype=jnp.int32)
    masked = jnp.any(args["mask_ids"][:, :, None] == positions, axis=1).astype(F32)[:, :, None]
    net = Butterfly(mesh)
    layer = Layer(None, args, masked, heads, net.head)

    own_stack = jnp.concatenate([jnp.swapaxes(args["qkv_weight"], 1, 2), args["out_weight"][None]], axis=0)
    own_stack = own_stack.reshape(4 * heads, HEAD_DIM, D)
    up_bias = args["up_bias"].astype(F32)
    small = jnp.concatenate(
        [
            jnp.pad(rel_table.T, ((0, 0), (0, TABLE - table_rows))),
            jnp.pad(args["qv_bias"], ((0, 0), (0, D - heads * HEAD_DIM))),
            jnp.pad(up_bias[None], ((0, 8 - heads - 3), (0, D - own_units))),
        ]
    )
    small = jnp.pad(small, ((0, 8 - small.shape[0]), (0, 0)))
    shares = jnp.stack([up_weight.T, args["down_weight"]])
    if net.dp == 8 and net.head == 4:
        gathered, own_ffn, units, rows, slots = run_butterfly(net, layer, own_stack, small, shares)
    else:
        gathered, own_ffn, units, rows, slots = run_plain(layer, own_stack, small, shares, up_bias)
    qkv_weight_grad, out_weight_grad = order(layer.place, gathered)
    (
        down_bias_grad,
        ffn_scale_grad,
        ffn_gain_grad,
        ffn_shift_grad,
        attn_scale_grad,
        out_bias_grad,
        attn_gain_grad,
        attn_shift_grad,
        mask_token_grad,
    ) = rows
    return (
        layer.output,
        layer.images_grad,
        mask_token_grad,
        attn_gain_grad,
        attn_shift_grad,
        qkv_weight_grad,
        slots[heads : heads + 2, : heads * HEAD_DIM],
        slots[:heads, :table_rows].T,
        out_weight_grad,
        out_bias_grad,
        attn_scale_grad,
        ffn_gain_grad,
        ffn_shift_grad,
        own_ffn[0].T,
        units,
        own_ffn[1],
        down_bias_grad,
        ffn_scale_grad,
    )


def solution(mesh):
    in_specs = (
        P(("dp", "head"), None, None),
        P(("dp", "head"), None),
        P(),
        P(("dp", "head"), None, None),
        P(),
        P(),
        P(),
        P(None, None, "head"),
        P(None, "head"),
        P(None, "head"),
        P("head", None),
        P(),
        P(),
        P(),
        P(),
        P(None, ("dp", "head")),
        P(("dp", "head")),
        P(("dp", "head"), None),
        P(),
        P(),
    )
    out_specs = (
        P(("dp", "head"), None, None),
        P(("dp", "head"), None, None),
        P(),
        P(),
        P(),
        P(None, None, "head"),
        P(None, "head"),
        P(None, "head"),
        P("head", None),
        P(),
        P(),
        P(),
        P(),
        P(None, ("dp", "head")),
        P(("dp", "head")),
        P(("dp", "head"), None),
        P(),
        P(),
    )
    return jax.shard_map(
        partial(on_device, mesh), mesh=mesh, in_specs=in_specs, out_specs=out_specs, check_vma=False
    )
```

```python
from functools import partial

import jax
import jax.numpy as jnp
from jax import lax
from jax.experimental import pallas as pl
from jax.experimental.pallas import tpu as pltpu
from jax.sharding import PartitionSpec as P

HEAD_DIM = 64
SEQ = 200
VALID = 197
ROWS = 208
D = 768
HALF = 384
TABLE = 768
REACH = 384
CENTRE = 364
EPS = 1e-06
NEG = -1000000000.0
BOTH = ("dp", "head")
BF = jnp.bfloat16
F32 = jnp.float32
MIB = 1 << 20
UNROLL = 5
WEIGHT = dict(
    start=16, bias0=1, bias1=1, project0=1, project1=1, attend0=36, attend1=1, units=1, branch=24,
    feed00=64, feed01=1, feed10=64, feed11=64, middle=44, attend_back1=36, weights1=20, attend_back0=36,
    weights0=20, end=48, table=36, order=8, rows=1,
)
GRANTS = dict(
    start=8, bias=10, project=16, attend=9, branch=12, feed=14,
    middle=16, attend_back=12, weights=16, end=16, table=14, order=10, units=6, rows=6,
)


def nn(a, b):
    return lax.dot_general(a, b, (((1,), (0,)), ((), ())), preferred_element_type=F32)


def nt(a, b):
    return lax.dot_general(a, b, (((1,), (1,)), ((), ())), preferred_element_type=F32)


def tn(a, b):
    return lax.dot_general(a, b, (((0,), (0,)), ((), ())), preferred_element_type=F32)


def norm_stats(rows):
    row_mean = jnp.mean(rows, axis=-1, keepdims=True)
    centered = rows - row_mean
    inv_std = lax.rsqrt(jnp.mean(centered * centered, axis=-1, keepdims=True) + EPS)
    return centered * inv_std, inv_std


def norm_back(grad_normed, normal, inv_std, gain):
    scaled = grad_normed * gain
    return inv_std * (
        scaled
        - jnp.mean(scaled, axis=-1, keepdims=True)
        - normal * jnp.mean(scaled * normal, axis=-1, keepdims=True)
    )


def swap_halves(core, value):
    low, high = value[:, :HALF], value[:, HALF:]
    first = core == 0
    return jnp.where(first, low, high), jnp.where(first, high, low)


def turn(plane, value, part):
    width = value.shape[1]
    lane = lax.broadcasted_iota(jnp.int32, value.shape, 1)
    for bit in range(2):
        step = part << bit
        other = jnp.where((lane & step) != 0, pltpu.roll(value, step, 1), pltpu.roll(value, width - step, 1))
        value = jnp.where((plane >> bit) % 2 == 1, other, value)
    return value


def column_sum(value):
    return jnp.sum(value, axis=0, keepdims=True)


def split_two(value):
    high = value.astype(BF)
    return high, (value - high.astype(F32)).astype(BF)


def call(kernel, name, grid, in_specs, out_specs, out_shape, scratch=(), prefetch=0, aliases=None, turn=""):
    vmem, time = GRANTS[name], WEIGHT[name + turn]
    return pl.pallas_call(
        kernel,
        name=name,
        grid_spec=pltpu.PrefetchScalarGridSpec(
            num_scalar_prefetch=prefetch,
            grid=grid,
            in_specs=in_specs,
            out_specs=out_specs,
            scratch_shapes=list(scratch),
        ),
        out_shape=out_shape,
        input_output_aliases=aliases or {},
        compiler_params=pltpu.CompilerParams(vmem_limit_bytes=vmem * MIB),
        cost_estimate=pl.CostEstimate(flops=int(time * 1e9), bytes_accessed=MIB, transcendentals=0),
    )


def whole(shape):
    count = len(shape)
    return pl.BlockSpec(shape, lambda *_: (0,) * count)


def once(shape):
    count = len(shape)
    return pl.BlockSpec(shape, lambda *_: (0,) * count, pipeline_mode=pl.Buffered(1))


def three_rows():
    return pl.BlockSpec((3, ROWS, HALF), lambda i, *_: (0, i, 0))


def hbm(*values):
    held = [pltpu.with_memory_space_constraint(value, pltpu.HBM) for value in values]
    return held if len(held) > 1 else held[0]


def in_hbm(shape, dtype):
    return pltpu.HBM(shape, dtype)


def rows_of(width):
    return pl.BlockSpec((ROWS, width), lambda i, *_: (i, 0))


def image_of(width):
    return pl.BlockSpec((1, SEQ, width), lambda i, *_: (i, 0, 0))


def like(shape, dtype):
    return jax.ShapeDtypeStruct(shape, dtype)


def start_kernel(place, images, masked, out_grad, token, gain, shift, ffn_scale, normed, grad_mlp, sums):
    step = pl.program_id(0)
    hidden = jnp.where(masked[0] > 0.0, token[...], images[0].astype(F32))
    normal, _ = norm_stats(hidden)
    rows = normal * gain[...] + shift[...]
    low, high = swap_halves(place[0], rows)
    normed[0:SEQ, 0:HALF] = low.astype(BF)
    normed[0:SEQ, HALF:D] = high.astype(BF)
    normed[SEQ:ROWS, :] = jnp.zeros((ROWS - SEQ, D), BF)
    scaled = (out_grad[0].astype(F32) * ffn_scale[...]).astype(BF)
    grad_mlp[0:SEQ, :] = scaled
    grad_mlp[SEQ:ROWS, :] = jnp.zeros((ROWS - SEQ, D), BF)

    @pl.when(step == 0)
    def _():
        sums[...] = jnp.zeros_like(sums)

    sums[0:1, :] += column_sum(scaled.astype(F32))


def start(place, images, masked, out_grad, token, gain, shift, ffn_scale):
    count = images.shape[0]
    return call(
        start_kernel,
        "start",
        (count,),
        [image_of(D), image_of(1), image_of(D)] + [whole((1, D))] * 4,
        [rows_of(D), rows_of(D), whole((8, D))],
        [like((count * ROWS, D), BF), like((count * ROWS, D), BF), like((8, D), F32)],
        prefetch=1,
    )(place, hbm(images), masked, hbm(out_grad), token, gain, shift, ffn_scale)


def table_lines(block, few):
    both = block.astype(F32)
    both = both[0 : 2 * few] + both[2 * few : 4 * few]
    lines = [jnp.concatenate([both[2 * i : 2 * i + 1], both[2 * i + 1 : 2 * i + 2]], axis=1) for i in range(few)]
    return lines


def bias_kernel(spots_across, edge_rows, first, second, bias, ones_down, ones_across):
    few = bias.shape[0]
    lines = table_lines(jnp.where(pl.program_id(0) == 0, first[0], second[0]), few)

    @pl.when(pl.program_id(0) == 0)
    def _():
        where_across = lax.broadcasted_iota(jnp.int32, (REACH, ROWS), 0)
        hot = (spots_across[...] == where_across).astype(F32)
        ones_across[...] = hot.astype(BF)
        ones_down[...] = hot.T.astype(BF)

    table_high, table_low = split_two(jnp.concatenate(lines + [jnp.zeros((8 - few, TABLE), F32)], axis=0))
    reach = lax.broadcasted_iota(jnp.int32, (ROWS, TABLE), 1)
    picked = []
    for edge in range(SEQ - VALID):
        hot = (edge_rows[:, edge : edge + 1] == reach).astype(BF)
        picked.append(nt(hot, table_high) + nt(hot, table_low))
    key = lax.broadcasted_iota(jnp.int32, (ROWS, ROWS), 0)
    query = lax.broadcasted_iota(jnp.int32, (ROWS, ROWS), 1)
    for head in range(few):
        line = lines[head]
        spread = []
        for chunk in range(REACH // 128):
            turned = pltpu.roll(jnp.broadcast_to(line, (8, TABLE)), (TABLE - CENTRE + chunk * 128) % TABLE, 1)
            turned = jnp.broadcast_to(turned[0:1], (128, TABLE))
            spread.append(pltpu.roll(turned, 0, 1, stride=1, stride_axis=0)[:, :REACH])
        spread = jnp.concatenate(spread, axis=0)
        high, low = split_two(spread)
        middle = nn(nn(ones_down[...], high).astype(BF), ones_across[...])
        middle += nn(nn(ones_down[...], low).astype(BF), ones_across[...])
        value = jnp.where(key == 0, line[:, 730:731], middle)
        value = jnp.where(query == 0, jnp.where(key == 0, line[:, 731:732], line[:, 729:730]), value)
        for edge in range(SEQ - VALID):
            value = jnp.where(query == VALID + edge, picked[edge][:, head : head + 1], value)
        bias[head] = jnp.where(key >= VALID, NEG, value)


def small_spec(block):
    return pl.BlockSpec((1, 16, HALF), lambda *_: (block, 0, 0))


def bias_of(spots_across, edge_rows, sources, block, few, half):
    return call(
        bias_kernel,
        "bias",
        (2,),
        [whole(spots_across.shape), whole(edge_rows.shape)] + [small_spec(block)] * 2,
        pl.BlockSpec((few, ROWS, ROWS), lambda i: (i, 0, 0)),
        like((2 * few, ROWS, ROWS), F32),
        scratch=[pltpu.VMEM((ROWS, REACH), BF), pltpu.VMEM((REACH, ROWS), BF)],
        turn=str(half),
    )(spots_across, edge_rows, *sources)


def table_kernel(spots_across, edge_rows, grad_a, grad_b, out):
    each = grad_a.shape[0]
    across = spots_across[...]
    ones_turned = ((REACH - 1) - across == lax.broadcasted_iota(jnp.int32, (REACH, ROWS), 0)).astype(BF)
    ones_turned = jnp.where(across >= 0, ones_turned, jnp.zeros_like(ones_turned))
    where_across = lax.broadcasted_iota(jnp.int32, (REACH, ROWS), 0)
    ones_down = (across == where_across).astype(F32).T.astype(BF)
    reach = lax.broadcasted_iota(jnp.int32, (ROWS, TABLE), 1)
    line = lax.broadcasted_iota(jnp.int32, (1, TABLE), 1)
    key = lax.broadcasted_iota(jnp.int32, (ROWS, 1), 0)
    for head in range(2 * each):
        grads = grad_a if head < each else grad_b
        grad = grads[head % each]
        high, low = split_two(grad)
        both = nn(nn(ones_turned, high).astype(BF), ones_down)
        both += nn(nn(ones_turned, low).astype(BF), ones_down)
        total = jnp.zeros((1, TABLE), F32)
        for chunk in range(REACH // 128):
            rows = both[chunk * 128 : chunk * 128 + 128]
            wide = jnp.concatenate([rows, jnp.zeros((128, TABLE - REACH), F32)], axis=1)
            added = column_sum(pltpu.roll(wide, 0, 1, stride=1, stride_axis=0))
            shift = (TABLE - (REACH - 1 - CENTRE) + chunk * 128) % TABLE
            total += pltpu.roll(jnp.broadcast_to(added, (8, TABLE)), shift, 1)[0:1]
        first = grad[:, 0:1]
        total += jnp.where(line == 729, column_sum(jnp.where(key > 0, first, 0.0)), 0.0)
        total += jnp.where(line == 731, grad[0:1, 0:1], 0.0)
        top = lax.broadcasted_iota(jnp.int32, (1, ROWS), 1)
        row = jnp.where((top > 0) & (top < VALID), grad[0:1, :], 0.0)
        total += jnp.where(line == 730, jnp.sum(row, axis=1, keepdims=True), 0.0)
        for edge in range(SEQ - VALID):
            spot = edge_rows[:, edge : edge + 1] == reach
            total += column_sum(jnp.where(spot, grad[:, VALID + edge : VALID + edge + 1], 0.0))
        out[head : head + 1, :] = total


def table_of(spots_across, edge_rows, grad_a, grad_b):
    heads = grad_a.shape[0] * 2
    return call(
        table_kernel,
        "table",
        (1,),
        [
            whole(spots_across.shape),
            whole(edge_rows.shape),
            whole(grad_a.shape),
            whole(grad_b.shape),
        ],
        whole((heads, TABLE)),
        like((heads, TABLE), F32),
    )(spots_across, edge_rows, grad_a, grad_b)


def project_kernel(has_own, heads, place, *refs):
    own = refs[0] if has_own else None
    pieces = refs[1 if has_own else 0 :]
    normed, small_low, small_high, outs, weights = pieces[2:]
    kind = pl.program_id(0)
    part = pieces[0].shape[3]
    skipped = 1 if has_own else 0
    if has_own:
        for head in range(heads):
            for plane in range(4):
                rows = own[kind * heads + head, plane * part : plane * part + part, :]
                low, high = swap_halves(place[0], rows)
                slot = jnp.bitwise_xor(place[1], plane)
                at = pl.ds(pl.multiple_of(head * HEAD_DIM + slot * part, part), part)
                weights[0, at, 0:HALF] = low
                weights[0, at, HALF:D] = high
    for core in range(2):
        for plane in range(4):
            piece = pieces[core]
            for group in range(piece.shape[1]):
                for head in range(heads):
                    at = ((group + skipped) * heads + head) * HEAD_DIM + plane * part
                    weights[0, at : at + part, core * HALF : core * HALF + HALF] = piece[
                        plane, group, kind * heads + head
                    ]

    @pl.when(kind < 3)
    def _():
        lane = lax.broadcasted_iota(jnp.int32, (8, HALF), 1)

        def shift_of(ref):
            block = ref[0].astype(F32)
            queries = block[4 * heads : 4 * heads + 1] + block[4 * heads + 2 : 4 * heads + 3]
            values = block[4 * heads + 1 : 4 * heads + 2] + block[4 * heads + 3 : 4 * heads + 4]
            row = jnp.broadcast_to(jnp.where(kind == 0, queries, values), (8, HALF))
            return jnp.where(lane < heads * HEAD_DIM, row, 0.0)

        scale = jnp.where(kind == 0, HEAD_DIM ** (-0.5), 1.0)
        shift = shift_of(small_low) + pltpu.roll(shift_of(small_high), heads * HEAD_DIM, 1)
        shift = turn(place[1], shift, part)[0:1] * jnp.where(kind == 1, 0.0, 1.0)
        outs[0] = ((nt(normed[...], weights[0]) + shift) * scale).astype(BF)


def project(place, own, pieces, normed, sources, block, heads, half):
    total = normed.shape[0]
    operands = ([] if own is None else [own]) + list(pieces) + [normed]
    return call(
        partial(project_kernel, own is not None, heads),
        "project",
        (4,),
        [once(value.shape) for value in operands] + [small_spec(block)] * 2,
        [
            pl.BlockSpec((1, total, HALF), lambda t, *_: (jnp.minimum(t, 2), 0, 0)),
            pl.BlockSpec((1, HALF, D), lambda t, *_: (t, 0, 0)),
        ],
        [like((3, total, HALF), BF), in_hbm((4, HALF, D), BF)],
        prefetch=1,
        turn=str(half),
    )(place, *operands, *sources)


def unit_kernel(own_at, far_at, row, *refs):
    pieces, out = refs[:-1], refs[-1]
    for core in range(2):
        for plane in range(4):
            far, near = pieces[core], pieces[2 + core]
            four = [far[plane, 0, own_at], far[plane, 0, far_at], near[plane, 0, 0], near[plane, 1, 0]]
            x, y = divmod(plane, 2)
            for z in range(4):
                rows = four[z].astype(F32)[row : row + 1, HALF - 128 : HALF]
                out[2 * core + x, 4 * y + z : 4 * y + z + 1, :] = rows


def units_of(far, near, heads):
    last = 4 * heads
    return call(
        partial(unit_kernel, 1, 0, last),
        "units",
        (1,),
        [pl.BlockSpec((4, 1, 2, 16, HALF), lambda i: (0, 0, last // 2, 0, 0))] * 2
        + [pl.BlockSpec((4, 2, 1, 16, HALF), lambda i: (0, 0, last, 0, 0))] * 2,
        whole((4, 8, 128)),
        like((4, 8, 128), F32),
    )(*far, *near)


def attend_kernel(projected, bias, attended, probs):
    lane = lax.broadcasted_iota(jnp.int32, (ROWS, 128), 1)
    for pair in range(HALF // 128):
        cols = slice(pair * 128, pair * 128 + 128)
        query_pair, key_pair = projected[0, :, cols], projected[1, :, cols]
        turned = projected[2, :, cols].T
        parts = []
        for side in range(2):
            head = pair * 2 + side
            own = (lane >= 64) if side else (lane < 64)
            scores = nt(key_pair, jnp.where(own, query_pair, jnp.zeros_like(query_pair))) + bias[head]
            top = jnp.max(scores, axis=0, keepdims=True)
            expo = jnp.exp(scores - top)
            soft = (expo * (1.0 / jnp.sum(expo, axis=0, keepdims=True))).astype(BF)
            probs[0, head] = soft
            parts.append(nn(turned[side * 64 : side * 64 + 64, :], soft))
        attended[:, cols] = jnp.concatenate(parts, axis=0).T.astype(BF)


def attend(projected, bias, half):
    total = projected.shape[1]
    count, heads = total // ROWS, bias.shape[0]
    return call(
        attend_kernel,
        "attend",
        (count,),
        [three_rows(), once(bias.shape)],
        [rows_of(HALF), pl.BlockSpec((1, heads, ROWS, ROWS), lambda i: (i, 0, 0, 0))],
        [like((total, HALF), BF), in_hbm((count, heads, ROWS, ROWS), BF)],
        turn=str(half),
    )(projected, bias)


def attend_back_kernel(projected, grad_att, probs, grads, grad_bias):
    step = pl.program_id(0)
    lane = lax.broadcasted_iota(jnp.int32, (ROWS, 128), 1)
    scale = HEAD_DIM ** (-0.5)

    @pl.when(step == 0)
    def _():
        grad_bias[...] = jnp.zeros_like(grad_bias)

    for pair in range(HALF // 128):
        cols = slice(pair * 128, pair * 128 + 128)
        query_pair, value_pair, grad_pair = projected[0, :, cols], projected[2, :, cols], grad_att[:, cols]
        turned = projected[1, :, cols].T
        parts_q, parts_k, parts_v = [], [], []
        for side in range(2):
            head = pair * 2 + side
            own = (lane >= 64) if side else (lane < 64)
            soft = probs[0, head]
            wide = soft.astype(F32)
            grad_probs = nt(value_pair, jnp.where(own, grad_pair, jnp.zeros_like(grad_pair)))
            centre = jnp.sum(wide * grad_probs, axis=0, keepdims=True)
            grad_scores = (wide * (grad_probs - centre)).astype(BF)
            grad_bias[head] += grad_scores.astype(F32)
            parts_v.append(nn(soft, grad_pair))
            parts_k.append(nn(grad_scores, query_pair))
            parts_q.append(nn(turned[side * 64 : side * 64 + 64, :], grad_scores))
        grads[2, :, cols] = jnp.where(lane < 64, parts_v[0], parts_v[1]).astype(BF)
        grads[1, :, cols] = jnp.where(lane < 64, parts_k[0], parts_k[1]).astype(BF)
        grads[0, :, cols] = (jnp.concatenate(parts_q, axis=0).T * scale).astype(BF)


def attend_back(projected, grad_att, probs, half):
    total = projected.shape[1]
    count, heads = probs.shape[:2]
    return call(
        attend_back_kernel,
        "attend_back",
        (count,),
        [three_rows(), rows_of(HALF), pl.BlockSpec((1, heads, ROWS, ROWS), lambda i: (i, 0, 0, 0))],
        [three_rows(), whole((heads, ROWS, ROWS))],
        [like((3, total, HALF), BF), like((heads, ROWS, ROWS), F32)],
        turn=str(half),
    )(projected, grad_att, hbm(probs))


def branch_kernel(
    place, att_a, att_b, out_a, out_b, images, masked, token, out_bias, attn_scale, gain, shift, branch, normed
):
    mixed = nn(att_a[...], out_a[0]) + nn(att_b[...], out_b[0])
    low, high = swap_halves(place[0], mixed)
    rows = jnp.concatenate([low, high], axis=1) + out_bias[...]
    branch[...] = rows
    hidden = jnp.where(masked[0] > 0.0, token[...], images[0].astype(F32))
    middle = hidden + attn_scale[...] * rows[0:SEQ]
    normal, _ = norm_stats(middle)
    normed[0:SEQ, :] = (normal * gain[...] + shift[...]).astype(BF)
    normed[SEQ:ROWS, :] = jnp.zeros((ROWS - SEQ, D), BF)


def out_weight_spec():
    return pl.BlockSpec((1, HALF, D), lambda i, *_: (3, 0, 0), pipeline_mode=pl.Buffered(1))


def branch_of(place, att_a, att_b, w_a, w_b, images, masked, vectors):
    count = images.shape[0]
    return call(
        branch_kernel,
        "branch",
        (count,),
        [rows_of(HALF), rows_of(HALF), out_weight_spec(), out_weight_spec(), image_of(D), image_of(1)]
        + [whole((1, D))] * len(vectors),
        [rows_of(D), rows_of(D)],
        [in_hbm((count * ROWS, D), F32), like((count * ROWS, D), BF)],
        prefetch=1,
    )(place, att_a, att_b, *hbm(w_a, w_b, images), masked, *vectors)


def gelu_both(value):
    cdf = 0.5 * (1.0 + lax.erf(value * (0.5**0.5)))
    pdf = jnp.exp(value * value * -0.5) * 0.3989422804014327
    return value * cdf, cdf + value * pdf


def feed_kernel(first, half, pieces, bias, normed, grad_mlp, *rest):
    if not first:
        mlp_in, grad_in = rest[:2]
        rest = rest[2:]
    mlp, grad_normed, out, bias_grad, up, down, act, pre = rest
    step = pl.program_id(0)
    some, part = pieces.shape[1], pieces.shape[2] // 2
    slots = 2 * some
    units = slots * part
    for slot in range(slots):
        at = slice(slot * part, slot * part + part)
        up[at, :] = pieces[slot // some, slot % some, 0:part]
        down[at, :] = pieces[slot // some, slot % some, part : 2 * part]

    @pl.when(step == 0)
    def _():
        if first:
            mlp[...] = jnp.zeros_like(mlp)
            grad_normed[...] = jnp.zeros_like(grad_normed)
        else:
            mlp[...] = mlp_in[...]
            grad_normed[...] = grad_in[...]

    unit = lax.broadcasted_iota(jnp.int32, (slots, units), 1)
    owner = jnp.zeros_like(unit)
    for slot in range(1, slots):
        owner += (unit >= slot * part).astype(jnp.int32)
    is_own = owner == lax.broadcasted_iota(jnp.int32, (slots, units), 0)
    lane = (unit - owner * part + half * part)[0:1]
    hot = (lax.broadcasted_iota(jnp.int32, (128, units), 0) == lane).astype(BF)
    shift = column_sum(jnp.where(is_own, nn(bias[0].astype(BF), hot), 0.0))
    tiles = normed.shape[0] // ROWS

    def tile(index, total):
        at = pl.ds(pl.multiple_of(index * ROWS, ROWS), ROWS)
        value = nt(normed[at, :], up[...]) + shift
        active, slope = gelu_both(value)
        act[at, :] = active.astype(BF)
        grad = (nt(grad_mlp[at, :], down[...]) * slope).astype(BF)
        pre[at, :] = grad
        return total + column_sum(grad.astype(F32))

    unit_grad = lax.fori_loop(0, tiles, tile, jnp.zeros((1, units), F32), unroll=UNROLL)
    unit_high, unit_low = split_two(jnp.where(is_own, unit_grad, 0.0))
    bias_grad[0] = nt(unit_high, hot) + nt(unit_low, hot)
    mlp[...] += nn(act[...], down[...])
    grad_normed[...] += nn(pre[...], up[...])
    grad_up = tn(pre[...], normed[...]).astype(BF)
    grad_down = tn(act[...], grad_mlp[...]).astype(BF)
    for slot in range(slots):
        out[slot, 0:part, :] = grad_up[slot * part : slot * part + part, :]
        out[slot, part : 2 * part, :] = grad_down[slot * part : slot * part + part, :]


def feed(half, core, pieces, bias, normed, grad_mlp, carried):
    total = normed.shape[0]
    _, some, twice, _ = pieces.shape
    slots, part = 2 * some, twice // 2
    units = slots * part
    first = carried is None
    in_specs = [pl.BlockSpec((2, some, twice, D), lambda i: (i, 0, 0, 0))]
    in_specs += [pl.BlockSpec((1, slots, 128), lambda i: (2 * core + i, 0, 0)), once((total, D)), once((total, D))]
    operands = [pieces, bias, normed, grad_mlp]
    aliases = {}
    if not first:
        in_specs += [once((total, D))] * 2
        operands += list(carried)
        aliases = {4: 0, 5: 1}
    return call(
        partial(feed_kernel, first, half),
        "feed",
        (2,),
        in_specs,
        [
            once((total, D)),
            once((total, D)),
            pl.BlockSpec((slots, 2 * part, D), lambda i: (i, 0, 0)),
            pl.BlockSpec((1, slots, 128), lambda i: (i, 0, 0)),
        ],
        [
            like((total, D), F32),
            like((total, D), F32),
            like((2 * slots, 2 * part, D), BF),
            like((2, slots, 128), F32),
        ],
        scratch=[
            pltpu.VMEM((units, D), BF),
            pltpu.VMEM((units, D), BF),
            pltpu.VMEM((total, units), BF),
            pltpu.VMEM((total, units), BF),
        ],
        aliases=aliases,
        turn=f"{half}{core}",
    )(*operands)


def middle_kernel(
    place,
    mlp_ref,
    grad_normed,
    branch,
    images,
    masked,
    out_grad,
    out_a,
    out_b,
    token,
    attn_scale,
    gain,
    ffn_scale,
    down_bias,
    output,
    grad_middle,
    grad_branch,
    grad_a,
    grad_b,
    sums,
):
    step = pl.program_id(0)

    @pl.when(step == 0)
    def _():
        sums[...] = jnp.zeros_like(sums)

    hidden = jnp.where(masked[0] > 0.0, token[...], images[0].astype(F32))
    side = branch[0:SEQ, :]
    middle = hidden + attn_scale[...] * side
    mlp = mlp_ref[0:SEQ, :] + down_bias[...]
    output[0] = (middle + ffn_scale[...] * mlp).astype(BF)
    grad_out = out_grad[0].astype(F32)
    sums[0:1, :] += column_sum(grad_out * mlp)
    normal, inv_std = norm_stats(middle)
    grad_two = grad_normed[0:SEQ, :]
    sums[1:2, :] += column_sum(grad_two * normal)
    sums[2:3, :] += column_sum(grad_two)
    grad = grad_out + norm_back(grad_two, normal, inv_std, gain[...])
    grad_middle[0:SEQ, :] = grad
    grad_middle[SEQ:ROWS, :] = jnp.zeros((ROWS - SEQ, D), F32)
    sums[3:4, :] += column_sum(grad * side)
    low_branch = (grad * attn_scale[...]).astype(BF)
    sums[4:5, :] += column_sum(low_branch.astype(F32))
    low, high = swap_halves(place[0], low_branch)
    grad_branch[0:SEQ, 0:HALF] = low
    grad_branch[0:SEQ, HALF:D] = high
    grad_branch[SEQ:ROWS, :] = jnp.zeros((ROWS - SEQ, D), BF)
    grad_a[...] = nt(grad_branch[...], out_a[0]).astype(BF)
    grad_b[...] = nt(grad_branch[...], out_b[0]).astype(BF)


def middle_of(place, mlp, grad_normed, branch, images, masked, out_grad, w_a, w_b, vectors):
    count = images.shape[0]
    total = count * ROWS
    return call(
        middle_kernel,
        "middle",
        (count,),
        [rows_of(D)] * 3
        + [image_of(D), image_of(1), image_of(D), out_weight_spec(), out_weight_spec()]
        + [whole((1, D))] * len(vectors),
        [image_of(D), rows_of(D), rows_of(D), rows_of(HALF), rows_of(HALF), whole((8, D))],
        [
            like((count, SEQ, D), BF),
            in_hbm((total, D), F32),
            like((total, D), BF),
            like((total, HALF), BF),
            like((total, HALF), BF),
            like((8, D), F32),
        ],
        prefetch=1,
    )(place, mlp, grad_normed, *hbm(branch, images), masked, *hbm(out_grad, w_a, w_b), *vectors)


def weight_kernel(place, grads, attended, normed, grad_branch, mine, other, sums):
    kind = pl.program_id(0)
    planes, groups, heads, part, _ = mine.shape

    def put(left, right):
        grad = tn(left, right).astype(BF)
        for plane in range(planes):
            for group in range(groups):
                for head in range(heads):
                    at = (group * heads + head) * HEAD_DIM + plane * part
                    mine[plane, group, head] = grad[at : at + part, 0:HALF]
                    other[plane, group, head] = grad[at : at + part, HALF:D]

    @pl.when(kind < 3)
    def _():
        put(grads[0], normed[...])
        total = jnp.broadcast_to(column_sum(grads[0].astype(F32)), (8, HALF))
        sums[0] = turn(place[1], total, part)

    @pl.when(kind == 3)
    def _():
        put(attended[...], grad_branch[...])


def weights_of(place, grads, attended, normed, grad_branch, shape, half):
    total = normed.shape[0]
    planes, groups, blocks, part, _ = shape
    out = pl.BlockSpec((planes, groups, blocks // 4, part, HALF), lambda t, *_: (0, 0, t, 0, 0))
    return call(
        weight_kernel,
        "weights",
        (4,),
        [
            pl.BlockSpec((1, total, HALF), lambda t, *_: (jnp.minimum(t, 2), 0, 0)),
            once((total, HALF)),
            once((total, D)),
            once((total, D)),
        ],
        [out, out, pl.BlockSpec((1, 8, HALF), lambda t, *_: (jnp.minimum(t, 2), 0, 0))],
        [like(shape, BF), like(shape, BF), like((3, 8, HALF), F32)],
        prefetch=1,
        turn=str(half),
    )(place, grads, attended, normed, grad_branch)


def end_kernel(
    place, back_a, back_b, w_a, w_b, grad_middle, images, masked, token, gain, images_grad, sums
):
    step = pl.program_id(0)

    @pl.when(step == 0)
    def _():
        sums[...] = jnp.zeros_like(sums)

    total = nn(back_a[0], w_a[0]) + nn(back_a[1], w_a[1]) + nn(back_a[2], w_a[2])
    total += nn(back_b[0], w_b[0]) + nn(back_b[1], w_b[1]) + nn(back_b[2], w_b[2])
    low, high = swap_halves(place[0], total)
    grad_one = jnp.concatenate([low, high], axis=1)[0:SEQ]
    is_masked = masked[0] > 0.0
    hidden = jnp.where(is_masked, token[...], images[0].astype(F32))
    normal, inv_std = norm_stats(hidden)
    sums[0:1, :] += column_sum(grad_one * normal)
    sums[1:2, :] += column_sum(grad_one)
    grad = grad_middle[0:SEQ, :] + norm_back(grad_one, normal, inv_std, gain[...])
    images_grad[0] = jnp.where(is_masked, 0.0, grad).astype(BF)
    sums[2:3, :] += column_sum(jnp.where(is_masked, grad, 0.0))


def end_of(place, grads_a, grads_b, w_a, w_b, grad_middle, images, masked, vectors):
    count = images.shape[0]
    return call(
        end_kernel,
        "end",
        (count,),
        [three_rows()] * 2
        + [pl.BlockSpec((3, HALF, D), lambda i, *_: (0, 0, 0), pipeline_mode=pl.Buffered(1))] * 2
        + [rows_of(D), image_of(D), image_of(1)]
        + [whole((1, D))] * len(vectors),
        [image_of(D), whole((8, D))],
        [like((count, SEQ, D), BF), like((8, D), F32)],
        prefetch=1,
    )(place, grads_a, grads_b, *hbm(w_a, w_b, grad_middle, images), masked, *vectors)


def rows_kernel(heads, first, middle, last, table, shift_a, shift_b, unit_am, unit_ao, unit_bm, unit_bo, keep, send):
    lane = lax.broadcasted_iota(jnp.int32, (8, HALF), 1)
    for out, unit_a, unit_b in ((keep, unit_am, unit_bm), (send, unit_ao, unit_bo)):
        out[...] = jnp.zeros_like(out)
        out[0:1, :] = first[0:1, :]
        out[1:6, :] = middle[0:5, :]
        out[6:9, :] = last[0:3, :]
        at = 9
        for group in range(4):
            out[at : at + heads, :] = table[group * heads : group * heads + heads, :]
            at += heads
            for kind in (0, 2):
                row = (shift_a if group < 2 else shift_b)[kind]
                row = row if group % 2 == 0 else pltpu.roll(row, HALF - heads * HEAD_DIM, 1)
                out[at : at + 1, 0:HALF] = jnp.where(lane < heads * HEAD_DIM, row, 0.0)[0:1]
                at += 1
        for x in range(2):
            out[at + 8 * x : at + 8 * x + 8, 0:128] = unit_a[x] + unit_b[x]


def rows_of_sums(heads, operands):
    tall = 9 + 4 * (heads + 2) + 16
    return call(
        partial(rows_kernel, heads),
        "rows",
        (1,),
        [whole(value.shape) for value in operands],
        [whole((tall, D))] * 2,
        [like((tall, D), F32)] * 2,
    )(*operands)


def order_kernel(place, own, other, qkv_grad, out_grad, wide):
    core, plane_here = place[0], place[1]
    planes, blocks, part, _ = own.shape
    heads = blocks // 4
    for plane in range(planes):
        slot = jnp.bitwise_xor(plane_here, plane)
        for block in range(blocks):
            at = block * HEAD_DIM + plane * part
            for source, side in ((own, core), (other, 1 - core)):
                columns = pl.ds(pl.multiple_of(side * HALF, HALF), HALF)
                wide[at : at + part, columns] = source[slot, block].astype(F32)
    size = heads * HEAD_DIM
    for kind in range(3):
        qkv_grad[kind] = wide[kind * size : kind * size + size, :]
    out_grad[...] = wide[3 * size : 4 * size, :]


def order(place, gathered):
    planes, blocks, part, _ = gathered[0].shape
    size = blocks // 4 * HEAD_DIM
    return call(
        order_kernel,
        "order",
        (1,),
        [whole(gathered[0].shape)] * 2,
        [whole((3, size, D)), whole((size, D))],
        [like((3, size, D), F32), like((size, D), F32)],
        scratch=[pltpu.VMEM((4 * size, D), F32)],
        prefetch=1,
    )(place, *gathered)


class Butterfly:
    def __init__(self, mesh):
        self.dp, self.head = mesh.shape["dp"], mesh.shape["head"]
        self.far, self.near = 2, 1
        self.core, self.x, self.y = (self.head << bit for bit in range(3))

    def swap(self, value, mask):
        size = self.dp * self.head
        return lax.ppermute(value, BOTH, [(i, i ^ mask) for i in range(size)])


def after(done, *values):
    held = lax.optimization_barrier((done,) + values)[1:]
    return held if len(values) > 1 else held[0]


def tie(*values):
    return lax.optimization_barrier(values)


def add_low(own, come):
    return (own.astype(F32) + come.astype(F32)).astype(own.dtype)


def line(vector):
    return vector.reshape(1, -1)


class Layer:
    def __init__(self, place, args, masked, heads, groups):
        self.place, self.args, self.masked = place, args, masked
        self.heads, self.groups = heads, groups
        self.weights, self.streams, self.carried = [None, None], [None, None], None
        self.rel_bias, self.sources, self.block = [None, None], [None, None], 0

    def lines(self, *names):
        return [line(self.args[name]) for name in names]

    def start(self):
        a = self.args
        self.normed_one, self.grad_mlp, self.sums_start = start(
            self.place,
            a["images"],
            self.masked,
            a["out_grad"],
            *self.lines("mask_token", "attn_gain", "attn_shift", "ffn_scale"),
        )
        return self.sums_start

    def spots(self):
        rel_index = self.args["rel_index"]
        positions = jnp.arange(SEQ, dtype=jnp.int32)
        column = rel_index[:, 1]
        patch = (positions >= 1) & (positions < VALID)
        corner = jnp.min(jnp.where(patch, column, TABLE))
        spots = jnp.where(patch, column - corner, -1)
        spots = jnp.pad(spots, (0, ROWS - SEQ), constant_values=-1)
        edges = jnp.pad(rel_index[VALID:, :].T, ((0, ROWS - SEQ), (0, 8 - (SEQ - VALID))))
        self.where = (spots[None, :], edges)

    def bias(self, half):
        self.rel_bias[half] = bias_of(*self.where, self.sources[half], self.block, self.heads, half)

    def project(self, half, own, pieces):
        projected, self.weights[half] = project(
            self.place, own, pieces, self.normed_one, self.sources[half], self.block, self.heads, half
        )
        self.streams[half] = [projected]
        return projected

    def attend(self, half):
        self.streams[half] += attend(self.streams[half][0], self.rel_bias[half], half)
        return self.streams[half][1]

    def branch(self):
        self.side, self.normed_two = branch_of(
            self.place,
            self.streams[0][1],
            self.streams[1][1],
            self.weights[0],
            self.weights[1],
            self.args["images"],
            self.masked,
            self.lines("mask_token", "out_bias", "attn_scale", "ffn_gain", "ffn_shift"),
        )
        return self.normed_two

    def feed(self, half, core, pieces, bias):
        *self.carried, grads, unit_grads = feed(
            half, core, pieces, bias, self.normed_two, self.grad_mlp, self.carried
        )
        return grads, unit_grads

    def middle(self):
        self.output, self.grad_middle, self.grad_branch, *self.grad_att, self.sums_middle = middle_of(
            self.place,
            *self.carried,
            self.side,
            self.args["images"],
            self.masked,
            self.args["out_grad"],
            self.weights[0],
            self.weights[1],
            self.lines("mask_token", "attn_scale", "ffn_gain", "ffn_scale", "down_bias"),
        )
        self.back, self.grad_bias, self.shift_sums = [None, None], [None, None], [None, None]
        return self.grad_att[0]

    def attend_back(self, half):
        projected, _, probs = self.streams[half]
        self.back[half], self.grad_bias[half] = attend_back(projected, self.grad_att[half], probs, half)
        return self.grad_bias[half]

    def weight_grads(self, half):
        mine, other, self.shift_sums[half] = weights_of(
            self.place,
            self.back[half],
            self.streams[half][1],
            self.normed_one,
            self.grad_branch,
            (4, self.groups // 2, 4 * self.heads, HEAD_DIM // 4, HALF),
            half,
        )
        return mine, other

    def table(self):
        self.grad_table = table_of(*self.where, *self.grad_bias)
        return self.grad_table

    def end(self):
        self.images_grad, self.sums_end = end_of(
            self.place,
            self.back[0],
            self.back[1],
            self.weights[0],
            self.weights[1],
            self.grad_middle,
            self.args["images"],
            self.masked,
            self.lines("mask_token", "attn_gain"),
        )
        return self.sums_end

    def vectors(self):
        heads, groups = self.heads, self.groups
        rows = jnp.concatenate([self.sums_start[0:1], self.sums_middle[0:5], self.sums_end[0:3]], axis=0)
        width = heads * HEAD_DIM
        slots = []
        for group in range(groups):
            half, at = divmod(group, groups // 2)
            slots.append(self.grad_table[group * heads : group * heads + heads])
            sums = self.shift_sums[half][:, 0, at * width : at * width + width]
            slots += [jnp.pad(sums[kind : kind + 1], ((0, 0), (0, D - width))) for kind in (0, 2)]
        return rows, slots


def run_butterfly(net, layer, own_stack, small, shares):
    heads, groups = layer.heads, layer.groups
    dp_here = lax.axis_index("dp")
    core = dp_here % 2
    x_here, y_here = dp_here // 2 % 2, dp_here // 4
    plane = x_here * 2 + y_here
    layer.place = jnp.stack([core, plane]).astype(jnp.int32)
    part = HEAD_DIM // 4
    swap = net.swap
    own_units = shares.shape[1]
    half_units = own_units // 2
    blocks = 4 * heads
    thirds = (net.far, net.near, net.far + net.near)
    planes = (net.y, net.x, net.x + net.y)

    def around(value, masks):
        return [swap(value, mask) for mask in masks]

    def total(*values):
        return sum(value.astype(F32) for value in values).astype(values[0].dtype)

    mine = lax.dynamic_slice(own_stack, (0, plane * part, core * HALF), (blocks, part, HALF))
    mine = jnp.concatenate([mine, small], axis=0)
    far, near, third = around(mine, thirds)
    layer.spots()
    layer.masked, layer.place, *layer.where = tie(layer.masked, layer.place, *layer.where)
    done = layer.start()
    far, near, third = after(done, far, near, third)
    layer.sources, layer.block = [(mine, far), (near, third)], blocks

    far_own = jnp.concatenate([far, small], axis=0)[None]
    come_a = around(far_own, planes)
    ffn = shares.reshape(2, 2, half_units, D).transpose(1, 0, 2, 3).reshape(2, 2 * half_units, D)
    ffn = after(far, ffn)
    ffn_a, ffn_b = ffn[0], ffn[1]
    far_fa = swap(ffn_a, net.far)
    layer.bias(0)
    layer.rel_bias[0], near, third, far_fa, *come_a = tie(layer.rel_bias[0], near, third, far_fa, *come_a)
    pieces_a = jnp.stack([far_own] + come_a)
    cross_a = swap(pieces_a, net.core)
    rest = jnp.stack([near, third])
    come_b = around(rest, planes)
    ffn_a = jnp.stack([ffn_a, far_fa])
    near_fa = swap(ffn_a, net.near)
    layer.bias(1)
    layer.rel_bias[1], cross_a, near_fa = tie(layer.rel_bias[1], cross_a, near_fa)
    ffn_a = jnp.concatenate([ffn_a, near_fa])
    come_fa = around(ffn_a, planes[:2])
    layer.project(0, own_stack, (pieces_a, cross_a))
    layer.streams[0][0], ffn_b, ffn_a, *come_b = tie(layer.streams[0][0], ffn_b, ffn_a, *come_b)
    come_fa += around(ffn_a, planes[2:])
    pieces_b = jnp.stack([rest] + come_b)
    cross_b = swap(pieces_b, net.core)
    far_fb = swap(ffn_b, net.far)
    layer.attend(0)
    layer.streams[0][1], cross_b, far_fb = tie(layer.streams[0][1], cross_b, far_fb)
    ffn_b = jnp.stack([ffn_b, far_fb])
    near_fb = swap(ffn_b, net.near)
    layer.project(1, None, (pieces_b, cross_b))
    biases = units_of((pieces_a, cross_a), (pieces_b, cross_b), heads)
    layer.attend(1)
    layer.streams[1][1], biases, near_fb = tie(layer.streams[1][1], biases, near_fb)
    layer.branch()
    layer.normed_two, ffn_b, near_fb, *come_fa = tie(layer.normed_two, ffn_b, near_fb, *come_fa)
    pieces_fa = jnp.stack([ffn_a] + come_fa)
    cross_fa = swap(pieces_fa, net.core)
    ffn_b = jnp.concatenate([ffn_b, near_fb])
    come_fb = around(ffn_b, planes)
    grads_am, unit_am = layer.feed(0, 0, pieces_fa, biases)
    layer.carried[0], cross_fa = tie(layer.carried[0], cross_fa)
    grads_ao, unit_ao = layer.feed(0, 1, cross_fa, biases)
    layer.carried[0], *come_fb = tie(layer.carried[0], *come_fb)
    ffn_b = jnp.stack([ffn_b] + come_fb)

    def parts_of(own, come):
        own, come = [v.reshape(2, 2, 2, 2, 2 * half_units, D) for v in (own, come)]
        return (
            add_low(own[..., :half_units, :], come[..., :half_units, :]),
            add_low(own[..., half_units:, :], come[..., half_units:, :]),
        )

    come_a = swap(grads_ao, net.core)
    cross_fb = swap(ffn_b, net.core)
    grads_bm, unit_bm = layer.feed(1, 0, ffn_b, biases)
    layer.carried[0], come_a, cross_fb = tie(layer.carried[0], come_a, cross_fb)
    up_a, down_a = parts_of(grads_am, come_a)
    come_up_a, come_down_a = swap(up_a[1], net.x), swap(down_a[:, 1], net.y)
    grads_bo, unit_bo = layer.feed(1, 1, cross_fb, biases)
    come_b = swap(grads_bo, net.core)
    layer.middle()
    layer.grad_att[1], come_up_a, come_down_a, come_b = tie(layer.grad_att[1], come_up_a, come_down_a, come_b)
    up_a, down_a = add_low(up_a[0], come_up_a), add_low(down_a[:, 0], come_down_a)
    come_up_a, come_down_a = swap(up_a[1], net.y), swap(down_a[1], net.x)
    up_b, down_b = parts_of(grads_bm, come_b)
    come_up, come_down = swap(up_b[1], net.x), swap(down_b[:, 1], net.y)
    layer.attend_back(1)
    attn_b = layer.weight_grads(1)
    layer.grad_att[0], come_up_a, come_down_a, come_up, come_down, *attn_b = tie(
        layer.grad_att[0], come_up_a, come_down_a, come_up, come_down, *attn_b
    )
    come_attn_b = swap(attn_b[1], net.core)
    sum_a = jnp.concatenate([add_low(up_a[0], come_up_a), add_low(down_a[0], come_down_a)], axis=-2)
    come_a = swap(sum_a[1], net.near)
    up_b, down_b = add_low(up_b[0], come_up), add_low(down_b[:, 0], come_down)
    come_up, come_down = swap(up_b[1], net.y), swap(down_b[1], net.x)
    layer.attend_back(0)
    layer.back[0], come_a, come_up, come_down, come_attn_b = tie(
        layer.back[0], come_a, come_up, come_down, come_attn_b
    )
    sum_a = add_low(sum_a[0], come_a)
    come_a = swap(sum_a[1], net.far)
    sum_b = jnp.concatenate([add_low(up_b[0], come_up), add_low(down_b[0], come_down)], axis=-2)
    come_b = swap(sum_b[1], net.near)
    attn_b = add_low(attn_b[0], come_attn_b).reshape(2, 2, 2, 4 * heads, part, HALF)
    come_attn_b = swap(attn_b[1], net.x)
    attn_a = layer.weight_grads(0)
    layer.grad_middle, *attn_a = tie(layer.grad_middle, *attn_a)
    come_attn_a = swap(attn_a[1], net.core)
    layer.end()
    layer.sums_end, layer.grad_bias[0], come_a, come_b, come_attn_a, come_attn_b = tie(
        layer.sums_end, layer.grad_bias[0], come_a, come_b, come_attn_a, come_attn_b
    )
    sum_a, sum_b = add_low(sum_a[0], come_a), add_low(sum_b[0], come_b)
    come_b = swap(sum_b[1], net.far)
    attn_b = add_low(attn_b[0], come_attn_b)
    come_attn_b = swap(attn_b[1], net.y)
    attn_a = add_low(*attn_a[:1], come_attn_a).reshape(2, 2, 2, 4 * heads, part, HALF)
    come_plane = [swap(attn_a[0, 1], net.y), swap(attn_a[1, 0], net.x), swap(attn_a[1, 1], net.x + net.y)]
    layer.table()
    layer.grad_table, come_attn_b, come_b = tie(layer.grad_table, come_attn_b, come_b)
    sum_b = add_low(sum_b[0], come_b)
    attn_b = add_low(attn_b[0], come_attn_b)
    come_attn_b = swap(attn_b, net.near)

    unit_am, unit_ao, unit_bm, unit_bo = after(layer.sums_end, unit_am, unit_ao, unit_bm, unit_bo)
    extra = heads + 2
    fixed = 9
    wide = fixed + 4 * extra
    state, sent = rows_of_sums(
        heads,
        [layer.sums_start, layer.sums_middle, layer.sums_end, layer.grad_table]
        + layer.shift_sums
        + [unit_am, unit_ao, unit_bm, unit_bo],
    )
    come = swap(sent, net.core)
    come, come_attn_b, *come_plane = tie(come, come_attn_b, *come_plane)
    state = state + come
    attn = total(attn_a[0, 0], come_attn_b, *come_plane)

    fixed_wide, each = state[:wide], groups
    sent = [jnp.concatenate([fixed_wide, state[wide + at * each : wide + at * each + each]]) for at in (1, 2, 3)]
    last, *come = tie(swap(attn[1], net.far), *[swap(v, mask) for v, mask in zip(sent, planes)])
    state = state[: wide + each] + come[0] + come[1] + come[2]
    own = add_low(attn[0], last)
    last = [swap(own, mask) for mask in planes]
    sent = []
    for at in (1, 2, 3):
        group = state[fixed + at * extra : fixed + at * extra + extra]
        sent.append(jnp.concatenate([state[:fixed], group, state[wide + at : wide + at + 1]]))
    state = jnp.concatenate([state[: fixed + extra], state[wide : wide + 1]])
    *last, come_far, come_near, come_third = tie(*last, *[swap(v, mask) for v, mask in zip(sent, thirds)])
    own = jnp.stack([own] + last)
    other = swap(own, net.core)
    state = state + come_far + come_near + come_third
    rows, slots, units = state[:fixed], state[fixed : fixed + extra], state[fixed + extra, :own_units]
    gathered = [own, other]

    own_ffn = jnp.stack([sum_a, sum_b]).reshape(2, 2, half_units, D).transpose(1, 0, 2, 3)
    own_ffn = own_ffn.reshape(2, own_units, D).astype(F32)
    return gathered, own_ffn, units, rows, slots


def run_plain(layer, own_stack, small, shares, up_bias):
    heads, groups = layer.heads, layer.groups
    layer.place = jnp.zeros((2,), jnp.int32)
    part = HEAD_DIM // 4
    blocks = 4 * heads
    attn = lax.all_gather(own_stack, "head", axis=0, tiled=False)
    attn = attn.reshape(2, groups // 2, blocks, 4, part, 2, HALF).transpose(0, 5, 3, 1, 2, 4, 6)
    ffn = lax.all_gather(shares, BOTH, axis=1, tiled=True)
    half_units = ffn.shape[1] // 64
    ffn = ffn.reshape(2, 2, 2, 4, 4, half_units, D).transpose(1, 2, 3, 4, 0, 5, 6)
    ffn = ffn.reshape(2, 2, 4, 4, 2 * half_units, D)
    small = lax.all_gather(small, "head", axis=0, tiled=False)
    layer.sources = [(small[0], small[1]), (small[2], small[3])]
    biases = lax.all_gather(up_bias, BOTH, axis=0, tiled=True).reshape(2, 4, 8, half_units)
    biases = jnp.concatenate([biases[0], biases[1]], axis=-1)
    biases = jnp.pad(biases, ((0, 0), (0, 0), (0, 128 - 2 * half_units)))
    layer.start()
    layer.spots()
    for half in range(2):
        layer.bias(half)
        layer.project(half, None, (attn[half, 0], attn[half, 1]))
        layer.attend(half)
    layer.branch()
    ffn_grads, unit_grads = [], []
    for half in range(2):
        for core in range(2):
            grads, units = layer.feed(half, core, ffn[half, core], biases)
            ffn_grads.append(grads)
            unit_grads.append(units[..., half * half_units : half * half_units + half_units])
    layer.middle()
    attn_grads = []
    for half in range(2):
        layer.attend_back(half)
        attn_grads.append(jnp.stack(layer.weight_grads(half)))
    layer.table()
    layer.end()
    parts = jnp.stack(attn_grads).astype(F32)
    parts = parts.transpose(0, 3, 4, 2, 5, 1, 6).reshape(groups, blocks, HEAD_DIM, D)
    own = lax.psum_scatter(parts, "head", scatter_dimension=0, tiled=True)
    own = lax.psum(own, "dp").reshape(blocks, 4, part, 2, HALF)
    both = jnp.stack(ffn_grads).astype(F32).reshape(2, 2, 16, 2, half_units, D).transpose(3, 0, 1, 2, 4, 5)
    own_ffn = lax.psum_scatter(both.reshape(2, -1, D), BOTH, scatter_dimension=1, tiled=True)
    units = lax.psum_scatter(jnp.stack(unit_grads).reshape(-1), BOTH, scatter_dimension=0, tiled=True)
    rows, slots = layer.vectors()
    slots = jnp.concatenate(slots).reshape(groups, -1, D)
    slots = lax.psum_scatter(slots, "head", scatter_dimension=0, tiled=True)[0]
    return own.transpose(3, 1, 0, 2, 4), own_ffn, units, lax.psum(rows, BOTH), lax.psum(slots, "dp")


NAMES = (
    "images",
    "mask_ids",
    "rel_index",
    "out_grad",
    "mask_token",
    "attn_gain",
    "attn_shift",
    "qkv_weight",
    "qv_bias",
    "rel_table",
    "out_weight",
    "out_bias",
    "attn_scale",
    "ffn_gain",
    "ffn_shift",
    "up_weight",
    "up_bias",
    "down_weight",
    "down_bias",
    "ffn_scale",
)


def on_device(mesh, *arrays):
    args = dict(zip(NAMES, arrays))
    rel_table, up_weight = args["rel_table"], args["up_weight"]
    table_rows, heads = rel_table.shape
    own_units = up_weight.shape[1]
    positions = jnp.arange(SEQ, dtype=jnp.int32)
    masked = jnp.any(args["mask_ids"][:, :, None] == positions, axis=1).astype(F32)[:, :, None]
    net = Butterfly(mesh)
    layer = Layer(None, args, masked, heads, net.head)

    own_stack = jnp.concatenate([jnp.swapaxes(args["qkv_weight"], 1, 2), args["out_weight"][None]], axis=0)
    own_stack = own_stack.reshape(4 * heads, HEAD_DIM, D)
    up_bias = args["up_bias"].astype(F32)
    lines = jnp.pad(rel_table.T, ((0, 0), (0, TABLE - table_rows))).reshape(2 * heads, HALF)
    shifts = jnp.pad(args["qv_bias"], ((0, 0), (0, HALF - heads * HEAD_DIM)))
    high_lines, high_shifts = lax.reduce_precision(lines, 8, 7), lax.reduce_precision(shifts, 8, 7)
    beside = jnp.pad(up_bias[None], ((0, 1), (HALF - 128, 128 - own_units)))
    small = jnp.concatenate(
        [high_lines, lines - high_lines, high_shifts + beside, shifts - high_shifts], axis=0
    ).astype(BF)[None]
    shares = jnp.stack([up_weight.T, args["down_weight"]])
    if net.dp == 8 and net.head == 4:
        gathered, own_ffn, units, rows, slots = run_butterfly(net, layer, own_stack, small, shares)
    else:
        gathered, own_ffn, units, rows, slots = run_plain(layer, own_stack, small, shares, up_bias)
    qkv_weight_grad, out_weight_grad = order(layer.place, gathered)
    (
        down_bias_grad,
        ffn_scale_grad,
        ffn_gain_grad,
        ffn_shift_grad,
        attn_scale_grad,
        out_bias_grad,
        attn_gain_grad,
        attn_shift_grad,
        mask_token_grad,
    ) = rows
    return (
        layer.output,
        layer.images_grad,
        mask_token_grad,
        attn_gain_grad,
        attn_shift_grad,
        jnp.swapaxes(qkv_weight_grad, 1, 2),
        slots[heads : heads + 2, : heads * HEAD_DIM],
        slots[:heads, :table_rows].T,
        out_weight_grad,
        out_bias_grad,
        attn_scale_grad,
        ffn_gain_grad,
        ffn_shift_grad,
        own_ffn[0].T,
        units,
        own_ffn[1],
        down_bias_grad,
        ffn_scale_grad,
    )


def solution(mesh):
    in_specs = (
        P(("dp", "head"), None, None),
        P(("dp", "head"), None),
        P(),
        P(("dp", "head"), None, None),
        P(),
        P(),
        P(),
        P(None, None, "head"),
        P(None, "head"),
        P(None, "head"),
        P("head", None),
        P(),
        P(),
        P(),
        P(),
        P(None, ("dp", "head")),
        P(("dp", "head")),
        P(("dp", "head"), None),
        P(),
        P(),
    )
    out_specs = (
        P(("dp", "head"), None, None),
        P(("dp", "head"), None, None),
        P(),
        P(),
        P(),
        P(None, None, "head"),
        P(None, "head"),
        P(None, "head"),
        P("head", None),
        P(),
        P(),
        P(),
        P(),
        P(None, ("dp", "head")),
        P(("dp", "head")),
        P(("dp", "head"), None),
        P(),
        P(),
    )
    return jax.shard_map(
        partial(on_device, mesh), mesh=mesh, in_specs=in_specs, out_specs=out_specs, check_vma=False
    )
```

```python
from functools import partial

import jax
import jax.numpy as jnp
from jax import lax
from jax.experimental import pallas as pl
from jax.experimental.pallas import tpu as pltpu
from jax.sharding import PartitionSpec as P

HEAD_DIM = 64
SEQ = 200
VALID = 197
ROWS = 208
D = 768
HALF = 384
TABLE = 768
REACH = 384
CENTRE = 364
EPS = 1e-06
NEG = -1000000000.0
BOTH = ("dp", "head")
BF = jnp.bfloat16
F32 = jnp.float32
MIB = 1 << 20
UNROLL = 5
WEIGHT = dict(
    start=16, bias0=1, bias1=1, project0=1, project1=1, attend0=1, attend1=1, units=1, branch=1,
    feed00=64, feed01=1, feed10=64, feed11=64, middle=44, attend_back1=36, weights1=20, attend_back0=36,
    weights0=20, end=1, table=36, order=8, rows=1,
)
GRANTS = dict(
    start=8, bias=10, project=16, attend=20, branch=14, feed=26,
    middle=20, attend_back=18, weights=16, end=20, table=14, order=10, units=6, rows=6,
)


def nn(a, b):
    return lax.dot_general(a, b, (((1,), (0,)), ((), ())), preferred_element_type=F32)


def nt(a, b):
    return lax.dot_general(a, b, (((1,), (1,)), ((), ())), preferred_element_type=F32)


def tn(a, b):
    return lax.dot_general(a, b, (((0,), (0,)), ((), ())), preferred_element_type=F32)


def norm_stats(rows):
    row_mean = jnp.mean(rows, axis=-1, keepdims=True)
    centered = rows - row_mean
    inv_std = lax.rsqrt(jnp.mean(centered * centered, axis=-1, keepdims=True) + EPS)
    return centered * inv_std, inv_std


def norm_back(grad_normed, normal, inv_std, gain):
    scaled = grad_normed * gain
    return inv_std * (
        scaled
        - jnp.mean(scaled, axis=-1, keepdims=True)
        - normal * jnp.mean(scaled * normal, axis=-1, keepdims=True)
    )


def swap_halves(core, value):
    low, high = value[:, :HALF], value[:, HALF:]
    first = core == 0
    return jnp.where(first, low, high), jnp.where(first, high, low)


def turn(plane, value, part):
    width = value.shape[1]
    lane = lax.broadcasted_iota(jnp.int32, value.shape, 1)
    for bit in range(2):
        step = part << bit
        other = jnp.where((lane & step) != 0, pltpu.roll(value, step, 1), pltpu.roll(value, width - step, 1))
        value = jnp.where((plane >> bit) % 2 == 1, other, value)
    return value


def column_sum(value):
    return jnp.sum(value, axis=0, keepdims=True)


def split_two(value):
    high = value.astype(BF)
    return high, (value - high.astype(F32)).astype(BF)


def call(kernel, name, grid, in_specs, out_specs, out_shape, scratch=(), prefetch=0, aliases=None, turn=""):
    vmem, time = GRANTS[name], WEIGHT[name + turn]
    return pl.pallas_call(
        kernel,
        name=name,
        grid_spec=pltpu.PrefetchScalarGridSpec(
            num_scalar_prefetch=prefetch,
            grid=grid,
            in_specs=in_specs,
            out_specs=out_specs,
            scratch_shapes=list(scratch),
        ),
        out_shape=out_shape,
        input_output_aliases=aliases or {},
        compiler_params=pltpu.CompilerParams(vmem_limit_bytes=vmem * MIB),
        cost_estimate=pl.CostEstimate(flops=int(time * 1e9), bytes_accessed=MIB, transcendentals=0),
    )


def whole(shape):
    count = len(shape)
    return pl.BlockSpec(shape, lambda *_: (0,) * count)


def once(shape):
    count = len(shape)
    return pl.BlockSpec(shape, lambda *_: (0,) * count, pipeline_mode=pl.Buffered(1))


def three_rows():
    return pl.BlockSpec((3, ROWS, HALF), lambda i, *_: (0, i, 0))


def hbm(*values):
    held = [pltpu.with_memory_space_constraint(value, pltpu.HBM) for value in values]
    return held if len(held) > 1 else held[0]


def in_hbm(shape, dtype):
    return pltpu.HBM(shape, dtype)


def rows_of(width):
    return pl.BlockSpec((ROWS, width), lambda i, *_: (i, 0))


def image_of(width):
    return pl.BlockSpec((1, SEQ, width), lambda i, *_: (i, 0, 0))


def like(shape, dtype):
    return jax.ShapeDtypeStruct(shape, dtype)


def start_kernel(place, images, masked, out_grad, token, gain, shift, ffn_scale, normed, grad_mlp, sums):
    step = pl.program_id(0)
    hidden = jnp.where(masked[0] > 0.0, token[...], images[0].astype(F32))
    normal, _ = norm_stats(hidden)
    rows = normal * gain[...] + shift[...]
    low, high = swap_halves(place[0], rows)
    normed[0:SEQ, 0:HALF] = low.astype(BF)
    normed[0:SEQ, HALF:D] = high.astype(BF)
    normed[SEQ:ROWS, :] = jnp.zeros((ROWS - SEQ, D), BF)
    scaled = (out_grad[0].astype(F32) * ffn_scale[...]).astype(BF)
    grad_mlp[0:SEQ, :] = scaled
    grad_mlp[SEQ:ROWS, :] = jnp.zeros((ROWS - SEQ, D), BF)

    @pl.when(step == 0)
    def _():
        sums[...] = jnp.zeros_like(sums)

    sums[0:1, :] += column_sum(scaled.astype(F32))


def start(place, images, masked, out_grad, token, gain, shift, ffn_scale):
    count = images.shape[0]
    return call(
        start_kernel,
        "start",
        (count,),
        [image_of(D), image_of(1), image_of(D)] + [whole((1, D))] * 4,
        [rows_of(D), rows_of(D), whole((8, D))],
        [like((count * ROWS, D), BF), like((count * ROWS, D), BF), like((8, D), F32)],
        prefetch=1,
    )(place, hbm(images), masked, hbm(out_grad), token, gain, shift, ffn_scale)


def table_lines(block, few):
    both = block.astype(F32)
    both = both[0 : 2 * few] + both[2 * few : 4 * few]
    lines = [jnp.concatenate([both[2 * i : 2 * i + 1], both[2 * i + 1 : 2 * i + 2]], axis=1) for i in range(few)]
    return lines


def bias_kernel(spots_across, edge_rows, first, second, bias, ones_down, ones_across):
    few = bias.shape[0]
    lines = table_lines(jnp.where(pl.program_id(0) == 0, first[0], second[0]), few)

    @pl.when(pl.program_id(0) == 0)
    def _():
        where_across = lax.broadcasted_iota(jnp.int32, (REACH, ROWS), 0)
        hot = (spots_across[...] == where_across).astype(F32)
        ones_across[...] = hot.astype(BF)
        ones_down[...] = hot.T.astype(BF)

    table_high, table_low = split_two(jnp.concatenate(lines + [jnp.zeros((8 - few, TABLE), F32)], axis=0))
    reach = lax.broadcasted_iota(jnp.int32, (ROWS, TABLE), 1)
    picked = []
    for edge in range(SEQ - VALID):
        hot = (edge_rows[:, edge : edge + 1] == reach).astype(BF)
        picked.append(nt(hot, table_high) + nt(hot, table_low))
    key = lax.broadcasted_iota(jnp.int32, (ROWS, ROWS), 0)
    query = lax.broadcasted_iota(jnp.int32, (ROWS, ROWS), 1)
    for head in range(few):
        line = lines[head]
        spread = []
        for chunk in range(REACH // 128):
            turned = pltpu.roll(jnp.broadcast_to(line, (8, TABLE)), (TABLE - CENTRE + chunk * 128) % TABLE, 1)
            turned = jnp.broadcast_to(turned[0:1], (128, TABLE))
            spread.append(pltpu.roll(turned, 0, 1, stride=1, stride_axis=0)[:, :REACH])
        spread = jnp.concatenate(spread, axis=0)
        high, low = split_two(spread)
        middle = nn(nn(ones_down[...], high).astype(BF), ones_across[...])
        middle += nn(nn(ones_down[...], low).astype(BF), ones_across[...])
        value = jnp.where(key == 0, line[:, 730:731], middle)
        value = jnp.where(query == 0, jnp.where(key == 0, line[:, 731:732], line[:, 729:730]), value)
        for edge in range(SEQ - VALID):
            value = jnp.where(query == VALID + edge, picked[edge][:, head : head + 1], value)
        bias[head] = jnp.where(key >= VALID, NEG, value)


def small_spec(block):
    return pl.BlockSpec((1, 16, HALF), lambda *_: (block, 0, 0))


def bias_of(spots_across, edge_rows, sources, block, few, half):
    return call(
        bias_kernel,
        "bias",
        (2,),
        [whole(spots_across.shape), whole(edge_rows.shape)] + [small_spec(block)] * 2,
        pl.BlockSpec((few, ROWS, ROWS), lambda i: (i, 0, 0)),
        like((2 * few, ROWS, ROWS), F32),
        scratch=[pltpu.VMEM((ROWS, REACH), BF), pltpu.VMEM((REACH, ROWS), BF)],
        turn=str(half),
    )(spots_across, edge_rows, *sources)


def table_kernel(spots_across, edge_rows, grad_a, grad_b, out):
    each = grad_a.shape[0]
    across = spots_across[...]
    ones_turned = ((REACH - 1) - across == lax.broadcasted_iota(jnp.int32, (REACH, ROWS), 0)).astype(BF)
    ones_turned = jnp.where(across >= 0, ones_turned, jnp.zeros_like(ones_turned))
    where_across = lax.broadcasted_iota(jnp.int32, (REACH, ROWS), 0)
    ones_down = (across == where_across).astype(F32).T.astype(BF)
    reach = lax.broadcasted_iota(jnp.int32, (ROWS, TABLE), 1)
    line = lax.broadcasted_iota(jnp.int32, (1, TABLE), 1)
    key = lax.broadcasted_iota(jnp.int32, (ROWS, 1), 0)
    for head in range(2 * each):
        grads = grad_a if head < each else grad_b
        grad = grads[head % each]
        high, low = split_two(grad)
        both = nn(nn(ones_turned, high).astype(BF), ones_down)
        both += nn(nn(ones_turned, low).astype(BF), ones_down)
        total = jnp.zeros((1, TABLE), F32)
        for chunk in range(REACH // 128):
            rows = both[chunk * 128 : chunk * 128 + 128]
            wide = jnp.concatenate([rows, jnp.zeros((128, TABLE - REACH), F32)], axis=1)
            added = column_sum(pltpu.roll(wide, 0, 1, stride=1, stride_axis=0))
            shift = (TABLE - (REACH - 1 - CENTRE) + chunk * 128) % TABLE
            total += pltpu.roll(jnp.broadcast_to(added, (8, TABLE)), shift, 1)[0:1]
        first = grad[:, 0:1]
        total += jnp.where(line == 729, column_sum(jnp.where(key > 0, first, 0.0)), 0.0)
        total += jnp.where(line == 731, grad[0:1, 0:1], 0.0)
        top = lax.broadcasted_iota(jnp.int32, (1, ROWS), 1)
        row = jnp.where((top > 0) & (top < VALID), grad[0:1, :], 0.0)
        total += jnp.where(line == 730, jnp.sum(row, axis=1, keepdims=True), 0.0)
        for edge in range(SEQ - VALID):
            spot = edge_rows[:, edge : edge + 1] == reach
            total += column_sum(jnp.where(spot, grad[:, VALID + edge : VALID + edge + 1], 0.0))
        out[head : head + 1, :] = total


def table_of(spots_across, edge_rows, grad_a, grad_b):
    heads = grad_a.shape[0] * 2
    return call(
        table_kernel,
        "table",
        (1,),
        [
            whole(spots_across.shape),
            whole(edge_rows.shape),
            whole(grad_a.shape),
            whole(grad_b.shape),
        ],
        whole((heads, TABLE)),
        like((heads, TABLE), F32),
    )(spots_across, edge_rows, grad_a, grad_b)


def project_kernel(has_own, heads, place, *refs):
    own = refs[0] if has_own else None
    pieces = refs[1 if has_own else 0 :]
    normed, small_low, small_high, outs, weights = pieces[2:]
    kind = pl.program_id(0)
    part = pieces[0].shape[3]
    skipped = 1 if has_own else 0
    if has_own:
        for head in range(heads):
            for plane in range(4):
                rows = own[kind * heads + head, plane * part : plane * part + part, :]
                low, high = swap_halves(place[0], rows)
                slot = jnp.bitwise_xor(place[1], plane)
                at = pl.ds(pl.multiple_of(head * HEAD_DIM + slot * part, part), part)
                weights[0, at, 0:HALF] = low
                weights[0, at, HALF:D] = high
    for core in range(2):
        for plane in range(4):
            piece = pieces[core]
            for group in range(piece.shape[1]):
                for head in range(heads):
                    at = ((group + skipped) * heads + head) * HEAD_DIM + plane * part
                    weights[0, at : at + part, core * HALF : core * HALF + HALF] = piece[
                        plane, group, kind * heads + head
                    ]

    @pl.when(kind < 3)
    def _():
        lane = lax.broadcasted_iota(jnp.int32, (8, HALF), 1)

        def shift_of(ref):
            block = ref[0].astype(F32)
            queries = block[4 * heads : 4 * heads + 1] + block[4 * heads + 2 : 4 * heads + 3]
            values = block[4 * heads + 1 : 4 * heads + 2] + block[4 * heads + 3 : 4 * heads + 4]
            row = jnp.broadcast_to(jnp.where(kind == 0, queries, values), (8, HALF))
            return jnp.where(lane < heads * HEAD_DIM, row, 0.0)

        scale = jnp.where(kind == 0, HEAD_DIM ** (-0.5), 1.0)
        shift = shift_of(small_low) + pltpu.roll(shift_of(small_high), heads * HEAD_DIM, 1)
        shift = turn(place[1], shift, part)[0:1] * jnp.where(kind == 1, 0.0, 1.0)
        outs[0] = ((nt(normed[...], weights[0]) + shift) * scale).astype(BF)


def project(place, own, pieces, normed, sources, block, heads, half):
    total = normed.shape[0]
    operands = ([] if own is None else [own]) + list(pieces) + [normed]
    return call(
        partial(project_kernel, own is not None, heads),
        "project",
        (4,),
        [once(value.shape) for value in operands] + [small_spec(block)] * 2,
        [
            pl.BlockSpec((1, total, HALF), lambda t, *_: (jnp.minimum(t, 2), 0, 0)),
            pl.BlockSpec((1, HALF, D), lambda t, *_: (t, 0, 0)),
        ],
        [like((3, total, HALF), BF), in_hbm((4, HALF, D), BF)],
        prefetch=1,
        turn=str(half),
    )(place, *operands, *sources)


def unit_kernel(own_at, far_at, row, *refs):
    pieces, out = refs[:-1], refs[-1]
    for core in range(2):
        for plane in range(4):
            far, near = pieces[core], pieces[2 + core]
            four = [far[plane, 0, own_at], far[plane, 0, far_at], near[plane, 0, 0], near[plane, 1, 0]]
            x, y = divmod(plane, 2)
            for z in range(4):
                rows = four[z].astype(F32)[row : row + 1, HALF - 128 : HALF]
                out[2 * core + x, 4 * y + z : 4 * y + z + 1, :] = rows


def units_of(far, near, heads):
    last = 4 * heads
    return call(
        partial(unit_kernel, 1, 0, last),
        "units",
        (1,),
        [pl.BlockSpec((4, 1, 2, 16, HALF), lambda i: (0, 0, last // 2, 0, 0))] * 2
        + [pl.BlockSpec((4, 2, 1, 16, HALF), lambda i: (0, 0, last, 0, 0))] * 2,
        whole((4, 8, 128)),
        like((4, 8, 128), F32),
    )(*far, *near)


PAIRS = [slice(pair * 128, pair * 128 + 128) for pair in range(HALF // 128)]


def one_side(pair, side):
    lane = lax.broadcasted_iota(jnp.int32, pair.shape, 1)
    return jnp.where((lane >= 64) if side else (lane < 64), pair, jnp.zeros_like(pair))


def attend_kernel(projected, bias, attended, probs):
    scores = []
    for index, cols in enumerate(PAIRS):
        for side in range(2):
            queries = one_side(projected[0, :, cols], side)
            scores.append(nt(projected[1, :, cols], queries) + bias[index * 2 + side])
    soft = []
    for head, score in enumerate(scores):
        expo = jnp.exp(score - jnp.max(score, axis=0, keepdims=True))
        soft.append((expo * (1.0 / jnp.sum(expo, axis=0, keepdims=True))).astype(BF))
        probs[0, head] = soft[head]
    for index, cols in enumerate(PAIRS):
        turned = projected[2, :, cols].T
        parts = [nn(turned[side * 64 : side * 64 + 64, :], soft[index * 2 + side]) for side in range(2)]
        attended[:, cols] = jnp.concatenate(parts, axis=0).T.astype(BF)


def attend(projected, bias, half):
    total = projected.shape[1]
    count, heads = total // ROWS, bias.shape[0]
    return call(
        attend_kernel,
        "attend",
        (count,),
        [three_rows(), once(bias.shape)],
        [rows_of(HALF), pl.BlockSpec((1, heads, ROWS, ROWS), lambda i: (i, 0, 0, 0))],
        [like((total, HALF), BF), in_hbm((count, heads, ROWS, ROWS), BF)],
        turn=str(half),
    )(projected, bias)


def attend_back_kernel(projected, grad_att, probs, grads, grad_bias):
    scale = HEAD_DIM ** (-0.5)

    @pl.when(pl.program_id(0) == 0)
    def _():
        grad_bias[...] = jnp.zeros_like(grad_bias)

    grad_probs = []
    for cols in PAIRS:
        for side in range(2):
            grad_probs.append(nt(projected[2, :, cols], one_side(grad_att[:, cols], side)))
    grad_scores = []
    for head, grad in enumerate(grad_probs):
        wide = probs[0, head].astype(F32)
        centre = jnp.sum(wide * grad, axis=0, keepdims=True)
        grad_scores.append((wide * (grad - centre)).astype(BF))
        grad_bias[head] += grad_scores[head].astype(F32)
    first = lax.broadcasted_iota(jnp.int32, (ROWS, 128), 1) < 64
    for index, cols in enumerate(PAIRS):
        heads = (2 * index, 2 * index + 1)
        turned = projected[1, :, cols].T
        by_value = [nn(probs[0, head], grad_att[:, cols]) for head in heads]
        by_key = [nn(grad_scores[head], projected[0, :, cols]) for head in heads]
        by_query = [nn(turned[64 * (head % 2) : 64 * (head % 2) + 64, :], grad_scores[head]) for head in heads]
        grads[2, :, cols] = jnp.where(first, by_value[0], by_value[1]).astype(BF)
        grads[1, :, cols] = jnp.where(first, by_key[0], by_key[1]).astype(BF)
        grads[0, :, cols] = (jnp.concatenate(by_query, axis=0).T * scale).astype(BF)


def attend_back(projected, grad_att, probs, half):
    total = projected.shape[1]
    count, heads = probs.shape[:2]
    return call(
        attend_back_kernel,
        "attend_back",
        (count,),
        [three_rows(), rows_of(HALF), pl.BlockSpec((1, heads, ROWS, ROWS), lambda i: (i, 0, 0, 0))],
        [three_rows(), whole((heads, ROWS, ROWS))],
        [like((3, total, HALF), BF), like((heads, ROWS, ROWS), F32)],
        turn=str(half),
    )(projected, grad_att, hbm(probs))


def branch_kernel(
    place, att_a, att_b, out_a, out_b, images, masked, token, out_bias, attn_scale, gain, shift, branch, normed, every
):
    @pl.when(pl.program_id(0) == 0)
    def _():
        every[0:HALF, :] = out_a[0]
        every[HALF:D, :] = out_b[0]

    mixed = nn(jnp.concatenate([att_a[...], att_b[...]], axis=1), every[...])
    low, high = swap_halves(place[0], mixed)
    rows = jnp.concatenate([low, high], axis=1) + out_bias[...]
    branch[...] = rows
    hidden = jnp.where(masked[0] > 0.0, token[...], images[0].astype(F32))
    middle = hidden + attn_scale[...] * rows[0:SEQ]
    normal, _ = norm_stats(middle)
    normed[0:SEQ, :] = (normal * gain[...] + shift[...]).astype(BF)
    normed[SEQ:ROWS, :] = jnp.zeros((ROWS - SEQ, D), BF)


def out_weight_spec():
    return pl.BlockSpec((1, HALF, D), lambda i, *_: (3, 0, 0), pipeline_mode=pl.Buffered(1))


def branch_of(place, att_a, att_b, w_a, w_b, images, masked, vectors):
    count = images.shape[0]
    return call(
        branch_kernel,
        "branch",
        (count,),
        [rows_of(HALF), rows_of(HALF), out_weight_spec(), out_weight_spec(), image_of(D), image_of(1)]
        + [whole((1, D))] * len(vectors),
        [rows_of(D), rows_of(D)],
        [in_hbm((count * ROWS, D), F32), like((count * ROWS, D), BF)],
        scratch=[pltpu.VMEM((D, D), BF)],
        prefetch=1,
    )(place, att_a, att_b, *hbm(w_a, w_b, images), masked, *vectors)


def gelu_both(value):
    cdf = 0.5 * (1.0 + lax.erf(value * (0.5**0.5)))
    pdf = jnp.exp(value * value * -0.5) * 0.3989422804014327
    return value * cdf, cdf + value * pdf


def feed_kernel(first, half, pieces, bias, normed, grad_mlp, *rest):
    if not first:
        mlp_in, grad_in = rest[:2]
        rest = rest[2:]
    mlp, grad_normed, out, bias_grad, up, down, act, pre = rest
    planes, some, twice, _ = pieces.shape
    part = twice // 2
    slots = planes * some
    units = slots * part
    for slot in range(slots):
        at = slice(slot * part, slot * part + part)
        up[at, :] = pieces[slot // some, slot % some, 0:part]
        down[at, :] = pieces[slot // some, slot % some, part:twice]
    unit = lax.broadcasted_iota(jnp.int32, (slots, units), 1)
    owner = jnp.zeros_like(unit)
    for slot in range(1, slots):
        owner += (unit >= slot * part).astype(jnp.int32)
    is_own = owner == lax.broadcasted_iota(jnp.int32, (slots, units), 0)
    lane = (unit - owner * part + half * part)[0:1]
    hot = (lax.broadcasted_iota(jnp.int32, (128, units), 0) == lane).astype(BF)
    rows = jnp.concatenate([bias[0], bias[1]], axis=0).astype(BF)
    shift = column_sum(jnp.where(is_own, nn(rows, hot), 0.0))
    tiles = normed.shape[0] // ROWS

    def tile(index, total):
        at = pl.ds(pl.multiple_of(index * ROWS, ROWS), ROWS)
        value = nt(normed[at, :], up[...]) + shift
        active, slope = gelu_both(value)
        act[at, :] = active.astype(BF)
        grad = (nt(grad_mlp[at, :], down[...]) * slope).astype(BF)
        pre[at, :] = grad
        return total + column_sum(grad.astype(F32))

    unit_grad = lax.fori_loop(0, tiles, tile, jnp.zeros((1, units), F32), unroll=UNROLL)
    unit_high, unit_low = split_two(jnp.where(is_own, unit_grad, 0.0))
    grads = nt(unit_high, hot) + nt(unit_low, hot)
    bias_grad[0] = grads[0 : slots // 2]
    bias_grad[1] = grads[slots // 2 : slots]
    if first:
        mlp[...] = nn(act[...], down[...])
        grad_normed[...] = nn(pre[...], up[...])
    else:
        mlp[...] = mlp_in[...] + nn(act[...], down[...])
        grad_normed[...] = grad_in[...] + nn(pre[...], up[...])
    grad_up = tn(pre[...], normed[...]).astype(BF)
    grad_down = tn(act[...], grad_mlp[...]).astype(BF)
    for slot in range(slots):
        out[slot, 0:part, :] = grad_up[slot * part : slot * part + part, :]
        out[slot, part : 2 * part, :] = grad_down[slot * part : slot * part + part, :]


def feed(half, core, pieces, bias, normed, grad_mlp, carried):
    total = normed.shape[0]
    planes, some, twice, _ = pieces.shape
    slots, part = planes * some, twice // 2
    units = slots * part
    first = carried is None
    in_specs = [once(pieces.shape), pl.BlockSpec((2, slots // 2, 128), lambda i: (core, 0, 0))]
    in_specs += [once((total, D))] * 2
    operands = [pieces, bias, normed, grad_mlp]
    aliases = {}
    if not first:
        in_specs += [once((total, D))] * 2
        operands += list(carried)
        aliases = {4: 0, 5: 1}
    return call(
        partial(feed_kernel, first, half),
        "feed",
        (1,),
        in_specs,
        [once((total, D))] * 2 + [once((slots, twice, D)), whole((2, slots // 2, 128))],
        [
            like((total, D), F32),
            like((total, D), F32),
            like((slots, twice, D), BF),
            like((2, slots // 2, 128), F32),
        ],
        scratch=[
            pltpu.VMEM((units, D), BF),
            pltpu.VMEM((units, D), BF),
            pltpu.VMEM((total, units), BF),
            pltpu.VMEM((total, units), BF),
        ],
        aliases=aliases,
        turn=f"{half}{core}",
    )(*operands)


def middle_kernel(
    place,
    mlp_ref,
    grad_normed,
    branch,
    images,
    masked,
    out_grad,
    out_a,
    out_b,
    token,
    attn_scale,
    gain,
    ffn_scale,
    down_bias,
    output,
    grad_middle,
    grad_branch,
    grad_a,
    grad_b,
    sums,
    every,
):
    step = pl.program_id(0)

    @pl.when(step == 0)
    def _():
        sums[...] = jnp.zeros_like(sums)
        every[0:HALF, :] = out_a[0]
        every[HALF:D, :] = out_b[0]

    hidden = jnp.where(masked[0] > 0.0, token[...], images[0].astype(F32))
    side = branch[0:SEQ, :]
    middle = hidden + attn_scale[...] * side
    mlp = mlp_ref[0:SEQ, :] + down_bias[...]
    output[0] = (middle + ffn_scale[...] * mlp).astype(BF)
    grad_out = out_grad[0].astype(F32)
    sums[0:1, :] += column_sum(grad_out * mlp)
    normal, inv_std = norm_stats(middle)
    grad_two = grad_normed[0:SEQ, :]
    sums[1:2, :] += column_sum(grad_two * normal)
    sums[2:3, :] += column_sum(grad_two)
    grad = grad_out + norm_back(grad_two, normal, inv_std, gain[...])
    grad_middle[0:SEQ, :] = grad
    grad_middle[SEQ:ROWS, :] = jnp.zeros((ROWS - SEQ, D), F32)
    sums[3:4, :] += column_sum(grad * side)
    low_branch = (grad * attn_scale[...]).astype(BF)
    sums[4:5, :] += column_sum(low_branch.astype(F32))
    low, high = swap_halves(place[0], low_branch)
    grad_branch[0:SEQ, 0:HALF] = low
    grad_branch[0:SEQ, HALF:D] = high
    grad_branch[SEQ:ROWS, :] = jnp.zeros((ROWS - SEQ, D), BF)
    both = nt(grad_branch[...], every[...])
    grad_a[...] = both[:, 0:HALF].astype(BF)
    grad_b[...] = both[:, HALF:D].astype(BF)


def middle_of(place, mlp, grad_normed, branch, images, masked, out_grad, w_a, w_b, vectors):
    count = images.shape[0]
    total = count * ROWS
    return call(
        middle_kernel,
        "middle",
        (count,),
        [rows_of(D)] * 3
        + [image_of(D), image_of(1), image_of(D), out_weight_spec(), out_weight_spec()]
        + [whole((1, D))] * len(vectors),
        [image_of(D), rows_of(D), rows_of(D), rows_of(HALF), rows_of(HALF), whole((8, D))],
        [
            like((count, SEQ, D), BF),
            in_hbm((total, D), F32),
            like((total, D), BF),
            like((total, HALF), BF),
            like((total, HALF), BF),
            like((8, D), F32),
        ],
        scratch=[pltpu.VMEM((D, D), BF)],
        prefetch=1,
    )(place, mlp, grad_normed, *hbm(branch, images), masked, *hbm(out_grad, w_a, w_b), *vectors)


def weight_kernel(place, grads, attended, normed, grad_branch, mine, other, sums):
    kind = pl.program_id(0)
    planes, groups, heads, part, _ = mine.shape

    def put(left, right):
        grad = tn(left, right).astype(BF)
        for plane in range(planes):
            for group in range(groups):
                for head in range(heads):
                    at = (group * heads + head) * HEAD_DIM + plane * part
                    mine[plane, group, head] = grad[at : at + part, 0:HALF]
                    other[plane, group, head] = grad[at : at + part, HALF:D]

    @pl.when(kind < 3)
    def _():
        put(grads[0], normed[...])
        total = jnp.broadcast_to(column_sum(grads[0].astype(F32)), (8, HALF))
        sums[0] = turn(place[1], total, part)

    @pl.when(kind == 3)
    def _():
        put(attended[...], grad_branch[...])


def weights_of(place, grads, attended, normed, grad_branch, shape, half):
    total = normed.shape[0]
    planes, groups, blocks, part, _ = shape
    out = pl.BlockSpec((planes, groups, blocks // 4, part, HALF), lambda t, *_: (0, 0, t, 0, 0))
    return call(
        weight_kernel,
        "weights",
        (4,),
        [
            pl.BlockSpec((1, total, HALF), lambda t, *_: (jnp.minimum(t, 2), 0, 0)),
            once((total, HALF)),
            once((total, D)),
            once((total, D)),
        ],
        [out, out, pl.BlockSpec((1, 8, HALF), lambda t, *_: (jnp.minimum(t, 2), 0, 0))],
        [like(shape, BF), like(shape, BF), like((3, 8, HALF), F32)],
        prefetch=1,
        turn=str(half),
    )(place, grads, attended, normed, grad_branch)


def end_kernel(
    place, back_a, back_b, w_a, w_b, grad_middle, images, masked, token, gain, images_grad, sums, every
):
    step = pl.program_id(0)

    @pl.when(step == 0)
    def _():
        sums[...] = jnp.zeros_like(sums)
        for index, ref in enumerate((w_a, w_b)):
            for kind in range(3):
                at = (3 * index + kind) * HALF
                every[at : at + HALF, :] = ref[kind]

    total = nn(jnp.concatenate([ref[kind] for ref in (back_a, back_b) for kind in range(3)], axis=1), every[...])
    low, high = swap_halves(place[0], total)
    grad_one = jnp.concatenate([low, high], axis=1)[0:SEQ]
    is_masked = masked[0] > 0.0
    hidden = jnp.where(is_masked, token[...], images[0].astype(F32))
    normal, inv_std = norm_stats(hidden)
    sums[0:1, :] += column_sum(grad_one * normal)
    sums[1:2, :] += column_sum(grad_one)
    grad = grad_middle[0:SEQ, :] + norm_back(grad_one, normal, inv_std, gain[...])
    images_grad[0] = jnp.where(is_masked, 0.0, grad).astype(BF)
    sums[2:3, :] += column_sum(jnp.where(is_masked, grad, 0.0))


def end_of(place, grads_a, grads_b, w_a, w_b, grad_middle, images, masked, vectors):
    count = images.shape[0]
    return call(
        end_kernel,
        "end",
        (count,),
        [three_rows()] * 2
        + [pl.BlockSpec((3, HALF, D), lambda i, *_: (0, 0, 0), pipeline_mode=pl.Buffered(1))] * 2
        + [rows_of(D), image_of(D), image_of(1)]
        + [whole((1, D))] * len(vectors),
        [image_of(D), whole((8, D))],
        [like((count, SEQ, D), BF), like((8, D), F32)],
        scratch=[pltpu.VMEM((6 * HALF, D), BF)],
        prefetch=1,
    )(place, grads_a, grads_b, *hbm(w_a, w_b, grad_middle, images), masked, *vectors)


def rows_kernel(heads, first, middle, last, table, shift_a, shift_b, unit_am, unit_ao, unit_bm, unit_bo, keep, send):
    lane = lax.broadcasted_iota(jnp.int32, (8, HALF), 1)
    for out, unit_a, unit_b in ((keep, unit_am, unit_bm), (send, unit_ao, unit_bo)):
        out[...] = jnp.zeros_like(out)
        out[0:1, :] = first[0:1, :]
        out[1:6, :] = middle[0:5, :]
        out[6:9, :] = last[0:3, :]
        at = 9
        for group in range(4):
            out[at : at + heads, :] = table[group * heads : group * heads + heads, :]
            at += heads
            for kind in (0, 2):
                row = (shift_a if group < 2 else shift_b)[kind]
                row = row if group % 2 == 0 else pltpu.roll(row, HALF - heads * HEAD_DIM, 1)
                out[at : at + 1, 0:HALF] = jnp.where(lane < heads * HEAD_DIM, row, 0.0)[0:1]
                at += 1
        for x in range(2):
            out[at + 8 * x : at + 8 * x + 8, 0:128] = unit_a[x] + unit_b[x]


def rows_of_sums(heads, operands):
    tall = 9 + 4 * (heads + 2) + 16
    return call(
        partial(rows_kernel, heads),
        "rows",
        (1,),
        [whole(value.shape) for value in operands],
        [whole((tall, D))] * 2,
        [like((tall, D), F32)] * 2,
    )(*operands)


def order_kernel(place, own, other, qkv_grad, out_grad, wide):
    core, plane_here = place[0], place[1]
    planes, blocks, part, _ = own.shape
    heads = blocks // 4
    for plane in range(planes):
        slot = jnp.bitwise_xor(plane_here, plane)
        for block in range(blocks):
            at = block * HEAD_DIM + plane * part
            for source, side in ((own, core), (other, 1 - core)):
                columns = pl.ds(pl.multiple_of(side * HALF, HALF), HALF)
                wide[at : at + part, columns] = source[slot, block].astype(F32)
    size = heads * HEAD_DIM
    for kind in range(3):
        qkv_grad[kind] = wide[kind * size : kind * size + size, :]
    out_grad[...] = wide[3 * size : 4 * size, :]


def order(place, gathered):
    planes, blocks, part, _ = gathered[0].shape
    size = blocks // 4 * HEAD_DIM
    return call(
        order_kernel,
        "order",
        (1,),
        [whole(gathered[0].shape)] * 2,
        [whole((3, size, D)), whole((size, D))],
        [like((3, size, D), F32), like((size, D), F32)],
        scratch=[pltpu.VMEM((4 * size, D), F32)],
        prefetch=1,
    )(place, *gathered)


class Butterfly:
    def __init__(self, mesh):
        self.dp, self.head = mesh.shape["dp"], mesh.shape["head"]
        self.far, self.near = 2, 1
        self.core, self.x, self.y = (self.head << bit for bit in range(3))

    def swap(self, value, mask):
        size = self.dp * self.head
        return lax.ppermute(value, BOTH, [(i, i ^ mask) for i in range(size)])


def after(done, *values):
    held = lax.optimization_barrier((done,) + values)[1:]
    return held if len(values) > 1 else held[0]


def tie(*values):
    return lax.optimization_barrier(values)


def add_low(own, come):
    return (own.astype(F32) + come.astype(F32)).astype(own.dtype)


def line(vector):
    return vector.reshape(1, -1)


class Layer:
    def __init__(self, place, args, masked, heads, groups):
        self.place, self.args, self.masked = place, args, masked
        self.heads, self.groups = heads, groups
        self.weights, self.streams, self.carried = [None, None], [None, None], None
        self.rel_bias, self.sources, self.block = [None, None], [None, None], 0

    def lines(self, *names):
        return [line(self.args[name]) for name in names]

    def start(self):
        a = self.args
        self.normed_one, self.grad_mlp, self.sums_start = start(
            self.place,
            a["images"],
            self.masked,
            a["out_grad"],
            *self.lines("mask_token", "attn_gain", "attn_shift", "ffn_scale"),
        )
        return self.sums_start

    def spots(self):
        rel_index = self.args["rel_index"]
        positions = jnp.arange(SEQ, dtype=jnp.int32)
        column = rel_index[:, 1]
        patch = (positions >= 1) & (positions < VALID)
        corner = jnp.min(jnp.where(patch, column, TABLE))
        spots = jnp.where(patch, column - corner, -1)
        spots = jnp.pad(spots, (0, ROWS - SEQ), constant_values=-1)
        edges = jnp.pad(rel_index[VALID:, :].T, ((0, ROWS - SEQ), (0, 8 - (SEQ - VALID))))
        self.where = (spots[None, :], edges)

    def bias(self, half):
        self.rel_bias[half] = bias_of(*self.where, self.sources[half], self.block, self.heads, half)

    def project(self, half, own, pieces):
        projected, self.weights[half] = project(
            self.place, own, pieces, self.normed_one, self.sources[half], self.block, self.heads, half
        )
        self.streams[half] = [projected]
        return projected

    def attend(self, half):
        self.streams[half] += attend(self.streams[half][0], self.rel_bias[half], half)
        return self.streams[half][1]

    def branch(self):
        self.side, self.normed_two = branch_of(
            self.place,
            self.streams[0][1],
            self.streams[1][1],
            self.weights[0],
            self.weights[1],
            self.args["images"],
            self.masked,
            self.lines("mask_token", "out_bias", "attn_scale", "ffn_gain", "ffn_shift"),
        )
        return self.normed_two

    def feed(self, half, core, pieces, bias):
        *self.carried, grads, unit_grads = feed(
            half, core, pieces, bias, self.normed_two, self.grad_mlp, self.carried
        )
        return grads, unit_grads

    def middle(self):
        self.output, self.grad_middle, self.grad_branch, *self.grad_att, self.sums_middle = middle_of(
            self.place,
            *self.carried,
            self.side,
            self.args["images"],
            self.masked,
            self.args["out_grad"],
            self.weights[0],
            self.weights[1],
            self.lines("mask_token", "attn_scale", "ffn_gain", "ffn_scale", "down_bias"),
        )
        self.back, self.grad_bias, self.shift_sums = [None, None], [None, None], [None, None]
        return self.grad_att[0]

    def attend_back(self, half):
        projected, _, probs = self.streams[half]
        self.back[half], self.grad_bias[half] = attend_back(projected, self.grad_att[half], probs, half)
        return self.grad_bias[half]

    def weight_grads(self, half):
        mine, other, self.shift_sums[half] = weights_of(
            self.place,
            self.back[half],
            self.streams[half][1],
            self.normed_one,
            self.grad_branch,
            (4, self.groups // 2, 4 * self.heads, HEAD_DIM // 4, HALF),
            half,
        )
        return mine, other

    def table(self):
        self.grad_table = table_of(*self.where, *self.grad_bias)
        return self.grad_table

    def end(self):
        self.images_grad, self.sums_end = end_of(
            self.place,
            self.back[0],
            self.back[1],
            self.weights[0],
            self.weights[1],
            self.grad_middle,
            self.args["images"],
            self.masked,
            self.lines("mask_token", "attn_gain"),
        )
        return self.sums_end

    def vectors(self):
        heads, groups = self.heads, self.groups
        rows = jnp.concatenate([self.sums_start[0:1], self.sums_middle[0:5], self.sums_end[0:3]], axis=0)
        width = heads * HEAD_DIM
        slots = []
        for group in range(groups):
            half, at = divmod(group, groups // 2)
            slots.append(self.grad_table[group * heads : group * heads + heads])
            sums = self.shift_sums[half][:, 0, at * width : at * width + width]
            slots += [jnp.pad(sums[kind : kind + 1], ((0, 0), (0, D - width))) for kind in (0, 2)]
        return rows, slots


def run_butterfly(net, layer, own_stack, small, shares):
    heads, groups = layer.heads, layer.groups
    dp_here = lax.axis_index("dp")
    core = dp_here % 2
    x_here, y_here = dp_here // 2 % 2, dp_here // 4
    plane = x_here * 2 + y_here
    layer.place = jnp.stack([core, plane]).astype(jnp.int32)
    part = HEAD_DIM // 4
    swap = net.swap
    own_units = shares.shape[1]
    half_units = own_units // 2
    blocks = 4 * heads
    thirds = (net.far, net.near, net.far + net.near)
    planes = (net.y, net.x, net.x + net.y)

    def around(value, masks):
        return [swap(value, mask) for mask in masks]

    def total(*values):
        return sum(value.astype(F32) for value in values).astype(values[0].dtype)

    mine = lax.dynamic_slice(own_stack, (0, plane * part, core * HALF), (blocks, part, HALF))
    mine = jnp.concatenate([mine, small], axis=0)
    far, near, third = around(mine, thirds)
    layer.spots()
    layer.masked, layer.place, *layer.where = tie(layer.masked, layer.place, *layer.where)
    done = layer.start()
    far, near, third = after(done, far, near, third)
    layer.sources, layer.block = [(mine, far), (near, third)], blocks

    far_own = jnp.concatenate([far, small], axis=0)[None]
    come_a = around(far_own, planes)
    ffn = shares.reshape(2, 2, half_units, D).transpose(1, 0, 2, 3).reshape(2, 2 * half_units, D)
    ffn = after(far, ffn)
    ffn_a, ffn_b = ffn[0], ffn[1]
    far_fa = swap(ffn_a, net.far)
    layer.bias(0)
    layer.rel_bias[0], near, third, far_fa, *come_a = tie(layer.rel_bias[0], near, third, far_fa, *come_a)
    pieces_a = jnp.stack([far_own] + come_a)
    cross_a = swap(pieces_a, net.core)
    rest = jnp.stack([near, third])
    come_b = around(rest, planes)
    ffn_a = jnp.stack([ffn_a, far_fa])
    near_fa = swap(ffn_a, net.near)
    layer.bias(1)
    layer.rel_bias[1], cross_a, near_fa = tie(layer.rel_bias[1], cross_a, near_fa)
    ffn_a = jnp.concatenate([ffn_a, near_fa])
    come_fa = around(ffn_a, planes[:2])
    layer.project(0, own_stack, (pieces_a, cross_a))
    layer.streams[0][0], ffn_b, ffn_a, *come_b = tie(layer.streams[0][0], ffn_b, ffn_a, *come_b)
    come_fa += around(ffn_a, planes[2:])
    pieces_b = jnp.stack([rest] + come_b)
    cross_b = swap(pieces_b, net.core)
    far_fb = swap(ffn_b, net.far)
    layer.attend(0)
    layer.streams[0][1], cross_b, far_fb = tie(layer.streams[0][1], cross_b, far_fb)
    ffn_b = jnp.stack([ffn_b, far_fb])
    near_fb = swap(ffn_b, net.near)
    layer.project(1, None, (pieces_b, cross_b))
    biases = units_of((pieces_a, cross_a), (pieces_b, cross_b), heads)
    layer.attend(1)
    layer.streams[1][1], biases, near_fb = tie(layer.streams[1][1], biases, near_fb)
    ffn_b = jnp.concatenate([ffn_b, near_fb])
    come_fb = around(ffn_b, planes[:2])
    layer.branch()
    layer.normed_two, ffn_b, *come_fa = tie(layer.normed_two, ffn_b, *come_fa)
    pieces_fa = jnp.stack([ffn_a] + come_fa)
    cross_fa = swap(pieces_fa, net.core)
    come_fb += around(ffn_b, planes[2:])
    grads_am, unit_am = layer.feed(0, 0, pieces_fa, biases)
    layer.carried[0], cross_fa = tie(layer.carried[0], cross_fa)
    grads_ao, unit_ao = layer.feed(0, 1, cross_fa, biases)
    layer.carried[0], *come_fb = tie(layer.carried[0], *come_fb)
    ffn_b = jnp.stack([ffn_b] + come_fb)

    def parts_of(own, come):
        own, come = [v.reshape(2, 2, 2, 2, 2 * half_units, D) for v in (own, come)]
        return (
            add_low(own[..., :half_units, :], come[..., :half_units, :]),
            add_low(own[..., half_units:, :], come[..., half_units:, :]),
        )

    come_a = swap(grads_ao, net.core)
    cross_fb = swap(ffn_b, net.core)
    grads_bm, unit_bm = layer.feed(1, 0, ffn_b, biases)
    layer.carried[0], come_a, cross_fb = tie(layer.carried[0], come_a, cross_fb)
    up_a, down_a = parts_of(grads_am, come_a)
    come_up_a, come_down_a = swap(up_a[1], net.x), swap(down_a[:, 1], net.y)
    grads_bo, unit_bo = layer.feed(1, 1, cross_fb, biases)
    come_b = swap(grads_bo, net.core)
    layer.middle()
    layer.grad_att[1], come_up_a, come_down_a, come_b = tie(layer.grad_att[1], come_up_a, come_down_a, come_b)
    up_a, down_a = add_low(up_a[0], come_up_a), add_low(down_a[:, 0], come_down_a)
    come_up_a, come_down_a = swap(up_a[1], net.y), swap(down_a[1], net.x)
    up_b, down_b = parts_of(grads_bm, come_b)
    come_up, come_down = swap(up_b[1], net.x), swap(down_b[:, 1], net.y)
    layer.attend_back(1)
    attn_b = layer.weight_grads(1)
    layer.grad_att[0], come_up_a, come_down_a, come_up, come_down, *attn_b = tie(
        layer.grad_att[0], come_up_a, come_down_a, come_up, come_down, *attn_b
    )
    come_attn_b = swap(attn_b[1], net.core)
    sum_a = jnp.concatenate([add_low(up_a[0], come_up_a), add_low(down_a[0], come_down_a)], axis=-2)
    come_a = swap(sum_a[1], net.near)
    up_b, down_b = add_low(up_b[0], come_up), add_low(down_b[:, 0], come_down)
    come_up, come_down = swap(up_b[1], net.y), swap(down_b[1], net.x)
    layer.attend_back(0)
    layer.back[0], come_a, come_up, come_down, come_attn_b = tie(
        layer.back[0], come_a, come_up, come_down, come_attn_b
    )
    sum_a = add_low(sum_a[0], come_a)
    sum_b = jnp.concatenate([add_low(up_b[0], come_up), add_low(down_b[0], come_down)], axis=-2)
    come_b = swap(sum_b[1], net.near)
    attn_b = [total(attn_b[0][slot], come_attn_b[slot]) for slot in range(4)]
    come_attn_b = [swap(value, mask) for value, mask in zip(attn_b[1:], planes)]
    attn_a = layer.weight_grads(0)
    layer.grad_bias[0], *attn_a = tie(layer.grad_bias[0], *attn_a)
    come_attn_a = swap(attn_a[1], net.core)
    layer.table()
    layer.grad_table, layer.grad_middle, come_b, come_attn_a, *come_attn_b = tie(
        layer.grad_table, layer.grad_middle, come_b, come_attn_a, *come_attn_b
    )
    attn_a = add_low(*attn_a[:1], come_attn_a).reshape(2, 2, 2, 4 * heads, part, HALF)
    come_plane = [swap(attn_a[0, 1], net.y), swap(attn_a[1, 0], net.x), swap(attn_a[1, 1], net.x + net.y)]
    attn_b = total(attn_b[0], *come_attn_b)
    come_attn_b = swap(attn_b, net.near)
    sum_b = add_low(sum_b[0], come_b)
    come_both = swap(jnp.stack([sum_a[1], sum_b[1]]), net.far)
    layer.end()
    layer.sums_end, come_attn_b, come_both = tie(layer.sums_end, come_attn_b, come_both)
    sum_a, sum_b = add_low(sum_a[0], come_both[0]), add_low(sum_b[0], come_both[1])

    unit_am, unit_ao, unit_bm, unit_bo = after(layer.sums_end, unit_am, unit_ao, unit_bm, unit_bo)
    extra = heads + 2
    fixed = 9
    wide = fixed + 4 * extra
    state, sent = rows_of_sums(
        heads,
        [layer.sums_start, layer.sums_middle, layer.sums_end, layer.grad_table]
        + layer.shift_sums
        + [unit_am, unit_ao, unit_bm, unit_bo],
    )
    come = swap(sent, net.core)
    come, come_attn_b, *come_plane = tie(come, come_attn_b, *come_plane)
    state = state + come
    attn = total(attn_a[0, 0], come_attn_b, *come_plane)

    fixed_wide, each = state[:wide], groups
    sent = [jnp.concatenate([fixed_wide, state[wide + at * each : wide + at * each + each]]) for at in (1, 2, 3)]
    last, *come = tie(swap(attn[1], net.far), *[swap(v, mask) for v, mask in zip(sent, planes)])
    state = state[: wide + each] + come[0] + come[1] + come[2]
    own = add_low(attn[0], last)
    last = [swap(own, mask) for mask in planes]
    sent = []
    for at in (1, 2, 3):
        group = state[fixed + at * extra : fixed + at * extra + extra]
        sent.append(jnp.concatenate([state[:fixed], group, state[wide + at : wide + at + 1]]))
    state = jnp.concatenate([state[: fixed + extra], state[wide : wide + 1]])
    *last, come_far, come_near, come_third = tie(*last, *[swap(v, mask) for v, mask in zip(sent, thirds)])
    own = jnp.stack([own] + last)
    other = swap(own, net.core)
    state = state + come_far + come_near + come_third
    rows, slots, units = state[:fixed], state[fixed : fixed + extra], state[fixed + extra, :own_units]
    gathered = [own, other]

    own_ffn = jnp.stack([sum_a, sum_b]).reshape(2, 2, half_units, D).transpose(1, 0, 2, 3)
    own_ffn = own_ffn.reshape(2, own_units, D).astype(F32)
    return gathered, own_ffn, units, rows, slots


def run_plain(layer, own_stack, small, shares, up_bias):
    heads, groups = layer.heads, layer.groups
    layer.place = jnp.zeros((2,), jnp.int32)
    part = HEAD_DIM // 4
    blocks = 4 * heads
    attn = lax.all_gather(own_stack, "head", axis=0, tiled=False)
    attn = attn.reshape(2, groups // 2, blocks, 4, part, 2, HALF).transpose(0, 5, 3, 1, 2, 4, 6)
    ffn = lax.all_gather(shares, BOTH, axis=1, tiled=True)
    half_units = ffn.shape[1] // 64
    ffn = ffn.reshape(2, 2, 2, 4, 4, half_units, D).transpose(1, 2, 3, 4, 0, 5, 6)
    ffn = ffn.reshape(2, 2, 4, 4, 2 * half_units, D)
    small = lax.all_gather(small, "head", axis=0, tiled=False)
    layer.sources = [(small[0], small[1]), (small[2], small[3])]
    biases = lax.all_gather(up_bias, BOTH, axis=0, tiled=True).reshape(2, 4, 8, half_units)
    biases = jnp.concatenate([biases[0], biases[1]], axis=-1)
    biases = jnp.pad(biases, ((0, 0), (0, 0), (0, 128 - 2 * half_units)))
    layer.start()
    layer.spots()
    for half in range(2):
        layer.bias(half)
        layer.project(half, None, (attn[half, 0], attn[half, 1]))
        layer.attend(half)
    layer.branch()
    ffn_grads, unit_grads = [], []
    for half in range(2):
        for core in range(2):
            grads, units = layer.feed(half, core, ffn[half, core], biases)
            ffn_grads.append(grads)
            unit_grads.append(units[..., half * half_units : half * half_units + half_units])
    layer.middle()
    attn_grads = []
    for half in range(2):
        layer.attend_back(half)
        attn_grads.append(jnp.stack(layer.weight_grads(half)))
    layer.table()
    layer.end()
    parts = jnp.stack(attn_grads).astype(F32)
    parts = parts.transpose(0, 3, 4, 2, 5, 1, 6).reshape(groups, blocks, HEAD_DIM, D)
    own = lax.psum_scatter(parts, "head", scatter_dimension=0, tiled=True)
    own = lax.psum(own, "dp").reshape(blocks, 4, part, 2, HALF)
    both = jnp.stack(ffn_grads).astype(F32).reshape(2, 2, 16, 2, half_units, D).transpose(3, 0, 1, 2, 4, 5)
    own_ffn = lax.psum_scatter(both.reshape(2, -1, D), BOTH, scatter_dimension=1, tiled=True)
    units = lax.psum_scatter(jnp.stack(unit_grads).reshape(-1), BOTH, scatter_dimension=0, tiled=True)
    rows, slots = layer.vectors()
    slots = jnp.concatenate(slots).reshape(groups, -1, D)
    slots = lax.psum_scatter(slots, "head", scatter_dimension=0, tiled=True)[0]
    return own.transpose(3, 1, 0, 2, 4), own_ffn, units, lax.psum(rows, BOTH), lax.psum(slots, "dp")


NAMES = (
    "images",
    "mask_ids",
    "rel_index",
    "out_grad",
    "mask_token",
    "attn_gain",
    "attn_shift",
    "qkv_weight",
    "qv_bias",
    "rel_table",
    "out_weight",
    "out_bias",
    "attn_scale",
    "ffn_gain",
    "ffn_shift",
    "up_weight",
    "up_bias",
    "down_weight",
    "down_bias",
    "ffn_scale",
)


def on_device(mesh, *arrays):
    args = dict(zip(NAMES, arrays))
    rel_table, up_weight = args["rel_table"], args["up_weight"]
    table_rows, heads = rel_table.shape
    own_units = up_weight.shape[1]
    positions = jnp.arange(SEQ, dtype=jnp.int32)
    masked = jnp.any(args["mask_ids"][:, :, None] == positions, axis=1).astype(F32)[:, :, None]
    net = Butterfly(mesh)
    layer = Layer(None, args, masked, heads, net.head)

    own_stack = jnp.concatenate([jnp.swapaxes(args["qkv_weight"], 1, 2), args["out_weight"][None]], axis=0)
    own_stack = own_stack.reshape(4 * heads, HEAD_DIM, D)
    up_bias = args["up_bias"].astype(F32)
    lines = jnp.pad(rel_table.T, ((0, 0), (0, TABLE - table_rows))).reshape(2 * heads, HALF)
    shifts = jnp.pad(args["qv_bias"], ((0, 0), (0, HALF - heads * HEAD_DIM)))
    high_lines, high_shifts = lax.reduce_precision(lines, 8, 7), lax.reduce_precision(shifts, 8, 7)
    beside = jnp.pad(up_bias[None], ((0, 1), (HALF - 128, 128 - own_units)))
    small = jnp.concatenate(
        [high_lines, lines - high_lines, high_shifts + beside, shifts - high_shifts], axis=0
    ).astype(BF)[None]
    shares = jnp.stack([up_weight.T, args["down_weight"]])
    if net.dp == 8 and net.head == 4:
        gathered, own_ffn, units, rows, slots = run_butterfly(net, layer, own_stack, small, shares)
    else:
        gathered, own_ffn, units, rows, slots = run_plain(layer, own_stack, small, shares, up_bias)
    qkv_weight_grad, out_weight_grad = order(layer.place, gathered)
    (
        down_bias_grad,
        ffn_scale_grad,
        ffn_gain_grad,
        ffn_shift_grad,
        attn_scale_grad,
        out_bias_grad,
        attn_gain_grad,
        attn_shift_grad,
        mask_token_grad,
    ) = rows
    return (
        layer.output,
        layer.images_grad,
        mask_token_grad,
        attn_gain_grad,
        attn_shift_grad,
        jnp.swapaxes(qkv_weight_grad, 1, 2),
        slots[heads : heads + 2, : heads * HEAD_DIM],
        slots[:heads, :table_rows].T,
        out_weight_grad,
        out_bias_grad,
        attn_scale_grad,
        ffn_gain_grad,
        ffn_shift_grad,
        own_ffn[0].T,
        units,
        own_ffn[1],
        down_bias_grad,
        ffn_scale_grad,
    )


def solution(mesh):
    in_specs = (
        P(("dp", "head"), None, None),
        P(("dp", "head"), None),
        P(),
        P(("dp", "head"), None, None),
        P(),
        P(),
        P(),
        P(None, None, "head"),
        P(None, "head"),
        P(None, "head"),
        P("head", None),
        P(),
        P(),
        P(),
        P(),
        P(None, ("dp", "head")),
        P(("dp", "head")),
        P(("dp", "head"), None),
        P(),
        P(),
    )
    out_specs = (
        P(("dp", "head"), None, None),
        P(("dp", "head"), None, None),
        P(),
        P(),
        P(),
        P(None, None, "head"),
        P(None, "head"),
        P(None, "head"),
        P("head", None),
        P(),
        P(),
        P(),
        P(),
        P(None, ("dp", "head")),
        P(("dp", "head")),
        P(("dp", "head"), None),
        P(),
        P(),
    )
    return jax.shard_map(
        partial(on_device, mesh), mesh=mesh, in_specs=in_specs, out_specs=out_specs, check_vma=False
    )
```

```python
from functools import partial

import jax
import jax.numpy as jnp
from jax import lax
from jax.experimental import pallas as pl
from jax.experimental.pallas import tpu as pltpu
from jax.sharding import PartitionSpec as P

HEAD_DIM = 64
SEQ = 200
VALID = 197
ROWS = 208
D = 768
HALF = 384
TABLE = 768
REACH = 384
CENTRE = 364
EPS = 1e-06
NEG = -1000000000.0
BOTH = ("dp", "head")
BF = jnp.bfloat16
F32 = jnp.float32
MIB = 1 << 20
UNROLL = 5
WEIGHT = dict(
    start=16, bias0=1, bias1=1, project0=1, project1=1, attend0=1, attend1=1, units=1, branch=1,
    feed00=64, feed01=1, feed10=64, feed11=64, middle=44, attend_back1=36, weights1=20, attend_back0=36,
    weights0=20, end=1, table=36, order=8, rows=1,
)
GRANTS = dict(
    start=8, bias=10, project=16, attend=20, branch=14, feed=26,
    middle=20, attend_back=18, weights=16, end=20, table=14, order=10, units=6, rows=6,
)


def nn(a, b):
    return lax.dot_general(a, b, (((1,), (0,)), ((), ())), preferred_element_type=F32)


def nt(a, b):
    return lax.dot_general(a, b, (((1,), (1,)), ((), ())), preferred_element_type=F32)


def tn(a, b):
    return lax.dot_general(a, b, (((0,), (0,)), ((), ())), preferred_element_type=F32)


def norm_stats(rows):
    row_mean = jnp.mean(rows, axis=-1, keepdims=True)
    centered = rows - row_mean
    inv_std = lax.rsqrt(jnp.mean(centered * centered, axis=-1, keepdims=True) + EPS)
    return centered * inv_std, inv_std


def norm_back(grad_normed, normal, inv_std, gain):
    scaled = grad_normed * gain
    return inv_std * (
        scaled
        - jnp.mean(scaled, axis=-1, keepdims=True)
        - normal * jnp.mean(scaled * normal, axis=-1, keepdims=True)
    )


def swap_halves(core, value):
    low, high = value[:, :HALF], value[:, HALF:]
    first = core == 0
    return jnp.where(first, low, high), jnp.where(first, high, low)


def turn(plane, value, part):
    width = value.shape[1]
    lane = lax.broadcasted_iota(jnp.int32, value.shape, 1)
    for bit in range(2):
        step = part << bit
        other = jnp.where((lane & step) != 0, pltpu.roll(value, step, 1), pltpu.roll(value, width - step, 1))
        value = jnp.where((plane >> bit) % 2 == 1, other, value)
    return value


def column_sum(value):
    return jnp.sum(value, axis=0, keepdims=True)


def split_two(value):
    high = value.astype(BF)
    return high, (value - high.astype(F32)).astype(BF)


def call(kernel, name, grid, in_specs, out_specs, out_shape, scratch=(), prefetch=0, aliases=None, turn=""):
    vmem, time = GRANTS[name], WEIGHT[name + turn]
    return pl.pallas_call(
        kernel,
        name=name,
        grid_spec=pltpu.PrefetchScalarGridSpec(
            num_scalar_prefetch=prefetch,
            grid=grid,
            in_specs=in_specs,
            out_specs=out_specs,
            scratch_shapes=list(scratch),
        ),
        out_shape=out_shape,
        input_output_aliases=aliases or {},
        compiler_params=pltpu.CompilerParams(vmem_limit_bytes=vmem * MIB),
        cost_estimate=pl.CostEstimate(flops=int(time * 1e9), bytes_accessed=MIB, transcendentals=0),
    )


def whole(shape):
    count = len(shape)
    return pl.BlockSpec(shape, lambda *_: (0,) * count)


def once(shape):
    count = len(shape)
    return pl.BlockSpec(shape, lambda *_: (0,) * count, pipeline_mode=pl.Buffered(1))


def three_rows():
    return pl.BlockSpec((3, ROWS, HALF), lambda i, *_: (0, i, 0))


def hbm(*values):
    held = [pltpu.with_memory_space_constraint(value, pltpu.HBM) for value in values]
    return held if len(held) > 1 else held[0]


def in_hbm(shape, dtype):
    return pltpu.HBM(shape, dtype)


def rows_of(width):
    return pl.BlockSpec((ROWS, width), lambda i, *_: (i, 0))


def image_of(width):
    return pl.BlockSpec((1, SEQ, width), lambda i, *_: (i, 0, 0))


def like(shape, dtype):
    return jax.ShapeDtypeStruct(shape, dtype)


def start_kernel(place, images, masked, out_grad, token, gain, shift, ffn_scale, normed, grad_mlp, sums):
    step = pl.program_id(0)
    hidden = jnp.where(masked[0] > 0.0, token[...], images[0].astype(F32))
    normal, _ = norm_stats(hidden)
    rows = normal * gain[...] + shift[...]
    low, high = swap_halves(place[0], rows)
    normed[0:SEQ, 0:HALF] = low.astype(BF)
    normed[0:SEQ, HALF:D] = high.astype(BF)
    normed[SEQ:ROWS, :] = jnp.zeros((ROWS - SEQ, D), BF)
    scaled = (out_grad[0].astype(F32) * ffn_scale[...]).astype(BF)
    grad_mlp[0:SEQ, :] = scaled
    grad_mlp[SEQ:ROWS, :] = jnp.zeros((ROWS - SEQ, D), BF)

    @pl.when(step == 0)
    def _():
        sums[...] = jnp.zeros_like(sums)

    sums[0:1, :] += column_sum(scaled.astype(F32))


def start(place, images, masked, out_grad, token, gain, shift, ffn_scale):
    count = images.shape[0]
    return call(
        start_kernel,
        "start",
        (count,),
        [image_of(D), image_of(1), image_of(D)] + [whole((1, D))] * 4,
        [rows_of(D), rows_of(D), whole((8, D))],
        [like((count * ROWS, D), BF), like((count * ROWS, D), BF), like((8, D), F32)],
        prefetch=1,
    )(place, hbm(images), masked, hbm(out_grad), token, gain, shift, ffn_scale)


def table_lines(block, few):
    both = block.astype(F32)
    both = both[0 : 2 * few] + both[2 * few : 4 * few]
    lines = [jnp.concatenate([both[2 * i : 2 * i + 1], both[2 * i + 1 : 2 * i + 2]], axis=1) for i in range(few)]
    return lines


def bias_kernel(spots_across, edge_rows, first, second, bias, ones_down, ones_across):
    few = bias.shape[0]
    lines = table_lines(jnp.where(pl.program_id(0) == 0, first[0], second[0]), few)

    @pl.when(pl.program_id(0) == 0)
    def _():
        where_across = lax.broadcasted_iota(jnp.int32, (REACH, ROWS), 0)
        hot = (spots_across[...] == where_across).astype(F32)
        ones_across[...] = hot.astype(BF)
        ones_down[...] = hot.T.astype(BF)

    table_high, table_low = split_two(jnp.concatenate(lines + [jnp.zeros((8 - few, TABLE), F32)], axis=0))
    reach = lax.broadcasted_iota(jnp.int32, (ROWS, TABLE), 1)
    picked = []
    for edge in range(SEQ - VALID):
        hot = (edge_rows[:, edge : edge + 1] == reach).astype(BF)
        picked.append(nt(hot, table_high) + nt(hot, table_low))
    key = lax.broadcasted_iota(jnp.int32, (ROWS, ROWS), 0)
    query = lax.broadcasted_iota(jnp.int32, (ROWS, ROWS), 1)
    for head in range(few):
        line = lines[head]
        spread = []
        for chunk in range(REACH // 128):
            turned = pltpu.roll(jnp.broadcast_to(line, (8, TABLE)), (TABLE - CENTRE + chunk * 128) % TABLE, 1)
            turned = jnp.broadcast_to(turned[0:1], (128, TABLE))
            spread.append(pltpu.roll(turned, 0, 1, stride=1, stride_axis=0)[:, :REACH])
        spread = jnp.concatenate(spread, axis=0)
        high, low = split_two(spread)
        middle = nn(nn(ones_down[...], high).astype(BF), ones_across[...])
        middle += nn(nn(ones_down[...], low).astype(BF), ones_across[...])
        value = jnp.where(key == 0, line[:, 730:731], middle)
        value = jnp.where(query == 0, jnp.where(key == 0, line[:, 731:732], line[:, 729:730]), value)
        for edge in range(SEQ - VALID):
            value = jnp.where(query == VALID + edge, picked[edge][:, head : head + 1], value)
        bias[head] = jnp.where(key >= VALID, NEG, value)


def small_spec(block):
    return pl.BlockSpec((1, 16, HALF), lambda *_: (block, 0, 0))


def bias_of(spots_across, edge_rows, sources, block, few, half):
    return call(
        bias_kernel,
        "bias",
        (2,),
        [whole(spots_across.shape), whole(edge_rows.shape)] + [small_spec(block)] * 2,
        pl.BlockSpec((few, ROWS, ROWS), lambda i: (i, 0, 0)),
        like((2 * few, ROWS, ROWS), F32),
        scratch=[pltpu.VMEM((ROWS, REACH), BF), pltpu.VMEM((REACH, ROWS), BF)],
        turn=str(half),
    )(spots_across, edge_rows, *sources)


def table_kernel(spots_across, edge_rows, grad_a, grad_b, out):
    each = grad_a.shape[0]
    across = spots_across[...]
    ones_turned = ((REACH - 1) - across == lax.broadcasted_iota(jnp.int32, (REACH, ROWS), 0)).astype(BF)
    ones_turned = jnp.where(across >= 0, ones_turned, jnp.zeros_like(ones_turned))
    where_across = lax.broadcasted_iota(jnp.int32, (REACH, ROWS), 0)
    ones_down = (across == where_across).astype(F32).T.astype(BF)
    reach = lax.broadcasted_iota(jnp.int32, (ROWS, TABLE), 1)
    line = lax.broadcasted_iota(jnp.int32, (1, TABLE), 1)
    key = lax.broadcasted_iota(jnp.int32, (ROWS, 1), 0)
    for head in range(2 * each):
        grads = grad_a if head < each else grad_b
        grad = grads[head % each]
        high, low = split_two(grad)
        both = nn(nn(ones_turned, high).astype(BF), ones_down)
        both += nn(nn(ones_turned, low).astype(BF), ones_down)
        total = jnp.zeros((1, TABLE), F32)
        for chunk in range(REACH // 128):
            rows = both[chunk * 128 : chunk * 128 + 128]
            wide = jnp.concatenate([rows, jnp.zeros((128, TABLE - REACH), F32)], axis=1)
            added = column_sum(pltpu.roll(wide, 0, 1, stride=1, stride_axis=0))
            shift = (TABLE - (REACH - 1 - CENTRE) + chunk * 128) % TABLE
            total += pltpu.roll(jnp.broadcast_to(added, (8, TABLE)), shift, 1)[0:1]
        first = grad[:, 0:1]
        total += jnp.where(line == 729, column_sum(jnp.where(key > 0, first, 0.0)), 0.0)
        total += jnp.where(line == 731, grad[0:1, 0:1], 0.0)
        top = lax.broadcasted_iota(jnp.int32, (1, ROWS), 1)
        row = jnp.where((top > 0) & (top < VALID), grad[0:1, :], 0.0)
        total += jnp.where(line == 730, jnp.sum(row, axis=1, keepdims=True), 0.0)
        for edge in range(SEQ - VALID):
            spot = edge_rows[:, edge : edge + 1] == reach
            total += column_sum(jnp.where(spot, grad[:, VALID + edge : VALID + edge + 1], 0.0))
        out[head : head + 1, :] = total


def table_of(spots_across, edge_rows, grad_a, grad_b):
    heads = grad_a.shape[0] * 2
    return call(
        table_kernel,
        "table",
        (1,),
        [
            whole(spots_across.shape),
            whole(edge_rows.shape),
            whole(grad_a.shape),
            whole(grad_b.shape),
        ],
        whole((heads, TABLE)),
        like((heads, TABLE), F32),
    )(spots_across, edge_rows, grad_a, grad_b)


def project_kernel(has_own, heads, place, *refs):
    own = refs[0] if has_own else None
    pieces = refs[1 if has_own else 0 :]
    normed, small_low, small_high, outs, weights = pieces[2:]
    kind = pl.program_id(0)
    part = pieces[0].shape[3]
    skipped = 1 if has_own else 0
    if has_own:
        for head in range(heads):
            for plane in range(4):
                rows = own[kind * heads + head, plane * part : plane * part + part, :]
                low, high = swap_halves(place[0], rows)
                slot = jnp.bitwise_xor(place[1], plane)
                at = pl.ds(pl.multiple_of(head * HEAD_DIM + slot * part, part), part)
                weights[0, at, 0:HALF] = low
                weights[0, at, HALF:D] = high
    for core in range(2):
        for plane in range(4):
            piece = pieces[core]
            for group in range(piece.shape[1]):
                for head in range(heads):
                    at = ((group + skipped) * heads + head) * HEAD_DIM + plane * part
                    weights[0, at : at + part, core * HALF : core * HALF + HALF] = piece[
                        plane, group, kind * heads + head
                    ]

    @pl.when(kind < 3)
    def _():
        lane = lax.broadcasted_iota(jnp.int32, (8, HALF), 1)

        def shift_of(ref):
            block = ref[0].astype(F32)
            queries = block[4 * heads : 4 * heads + 1] + block[4 * heads + 2 : 4 * heads + 3]
            values = block[4 * heads + 1 : 4 * heads + 2] + block[4 * heads + 3 : 4 * heads + 4]
            row = jnp.broadcast_to(jnp.where(kind == 0, queries, values), (8, HALF))
            return jnp.where(lane < heads * HEAD_DIM, row, 0.0)

        scale = jnp.where(kind == 0, HEAD_DIM ** (-0.5), 1.0)
        shift = shift_of(small_low) + pltpu.roll(shift_of(small_high), heads * HEAD_DIM, 1)
        shift = turn(place[1], shift, part)[0:1] * jnp.where(kind == 1, 0.0, 1.0)
        outs[0] = ((nt(normed[...], weights[0]) + shift) * scale).astype(BF)


def project(place, own, pieces, normed, sources, block, heads, half):
    total = normed.shape[0]
    operands = ([] if own is None else [own]) + list(pieces) + [normed]
    return call(
        partial(project_kernel, own is not None, heads),
        "project",
        (4,),
        [once(value.shape) for value in operands] + [small_spec(block)] * 2,
        [
            pl.BlockSpec((1, total, HALF), lambda t, *_: (jnp.minimum(t, 2), 0, 0)),
            pl.BlockSpec((1, HALF, D), lambda t, *_: (t, 0, 0)),
        ],
        [like((3, total, HALF), BF), in_hbm((4, HALF, D), BF)],
        prefetch=1,
        turn=str(half),
    )(place, *operands, *sources)


def unit_kernel(own_at, far_at, row, *refs):
    pieces, out = refs[:-1], refs[-1]
    for core in range(2):
        for plane in range(4):
            far, near = pieces[core], pieces[2 + core]
            four = [far[plane, 0, own_at], far[plane, 0, far_at], near[plane, 0, 0], near[plane, 1, 0]]
            x, y = divmod(plane, 2)
            for z in range(4):
                rows = four[z].astype(F32)[row : row + 1, HALF - 128 : HALF]
                out[2 * core + x, 4 * y + z : 4 * y + z + 1, :] = rows


def units_of(far, near, heads):
    last = 4 * heads
    return call(
        partial(unit_kernel, 1, 0, last),
        "units",
        (1,),
        [pl.BlockSpec((4, 1, 2, 16, HALF), lambda i: (0, 0, last // 2, 0, 0))] * 2
        + [pl.BlockSpec((4, 2, 1, 16, HALF), lambda i: (0, 0, last, 0, 0))] * 2,
        whole((4, 8, 128)),
        like((4, 8, 128), F32),
    )(*far, *near)


PAIRS = [slice(pair * 128, pair * 128 + 128) for pair in range(HALF // 128)]


def one_side(pair, side):
    lane = lax.broadcasted_iota(jnp.int32, pair.shape, 1)
    return jnp.where((lane >= 64) if side else (lane < 64), pair, jnp.zeros_like(pair))


def attend_kernel(projected, bias, attended, probs):
    scores = []
    for index, cols in enumerate(PAIRS):
        for side in range(2):
            queries = one_side(projected[0, :, cols], side)
            scores.append(nt(projected[1, :, cols], queries) + bias[index * 2 + side])
    soft = []
    for head, score in enumerate(scores):
        expo = jnp.exp(score - jnp.max(score, axis=0, keepdims=True))
        soft.append((expo * (1.0 / jnp.sum(expo, axis=0, keepdims=True))).astype(BF))
        probs[0, head] = soft[head]
    for index, cols in enumerate(PAIRS):
        turned = projected[2, :, cols].T
        parts = [nn(turned[side * 64 : side * 64 + 64, :], soft[index * 2 + side]) for side in range(2)]
        attended[:, cols] = jnp.concatenate(parts, axis=0).T.astype(BF)


def attend(projected, bias, half):
    total = projected.shape[1]
    count, heads = total // ROWS, bias.shape[0]
    return call(
        attend_kernel,
        "attend",
        (count,),
        [three_rows(), once(bias.shape)],
        [rows_of(HALF), pl.BlockSpec((1, heads, ROWS, ROWS), lambda i: (i, 0, 0, 0))],
        [like((total, HALF), BF), in_hbm((count, heads, ROWS, ROWS), BF)],
        turn=str(half),
    )(projected, bias)


def attend_back_kernel(projected, grad_att, probs, grads, grad_bias):
    scale = HEAD_DIM ** (-0.5)

    @pl.when(pl.program_id(0) == 0)
    def _():
        grad_bias[...] = jnp.zeros_like(grad_bias)

    grad_probs = []
    for cols in PAIRS:
        for side in range(2):
            grad_probs.append(nt(projected[2, :, cols], one_side(grad_att[:, cols], side)))
    grad_scores = []
    for head, grad in enumerate(grad_probs):
        wide = probs[0, head].astype(F32)
        centre = jnp.sum(wide * grad, axis=0, keepdims=True)
        grad_scores.append((wide * (grad - centre)).astype(BF))
        grad_bias[head] += grad_scores[head].astype(F32)
    first = lax.broadcasted_iota(jnp.int32, (ROWS, 128), 1) < 64
    for index, cols in enumerate(PAIRS):
        heads = (2 * index, 2 * index + 1)
        turned = projected[1, :, cols].T
        by_value = [nn(probs[0, head], grad_att[:, cols]) for head in heads]
        by_key = [nn(grad_scores[head], projected[0, :, cols]) for head in heads]
        by_query = [nn(turned[64 * (head % 2) : 64 * (head % 2) + 64, :], grad_scores[head]) for head in heads]
        grads[2, :, cols] = jnp.where(first, by_value[0], by_value[1]).astype(BF)
        grads[1, :, cols] = jnp.where(first, by_key[0], by_key[1]).astype(BF)
        grads[0, :, cols] = (jnp.concatenate(by_query, axis=0).T * scale).astype(BF)


def attend_back(projected, grad_att, probs, half):
    total = projected.shape[1]
    count, heads = probs.shape[:2]
    return call(
        attend_back_kernel,
        "attend_back",
        (count,),
        [three_rows(), rows_of(HALF), pl.BlockSpec((1, heads, ROWS, ROWS), lambda i: (i, 0, 0, 0))],
        [three_rows(), whole((heads, ROWS, ROWS))],
        [like((3, total, HALF), BF), like((heads, ROWS, ROWS), F32)],
        turn=str(half),
    )(projected, grad_att, hbm(probs))


def branch_kernel(
    place, att_a, att_b, out_a, out_b, images, masked, token, out_bias, attn_scale, gain, shift, branch, normed, every
):
    @pl.when(pl.program_id(0) == 0)
    def _():
        every[0:HALF, :] = out_a[0]
        every[HALF:D, :] = out_b[0]

    mixed = nn(jnp.concatenate([att_a[...], att_b[...]], axis=1), every[...])
    low, high = swap_halves(place[0], mixed)
    rows = jnp.concatenate([low, high], axis=1) + out_bias[...]
    branch[...] = rows
    hidden = jnp.where(masked[0] > 0.0, token[...], images[0].astype(F32))
    middle = hidden + attn_scale[...] * rows[0:SEQ]
    normal, _ = norm_stats(middle)
    normed[0:SEQ, :] = (normal * gain[...] + shift[...]).astype(BF)
    normed[SEQ:ROWS, :] = jnp.zeros((ROWS - SEQ, D), BF)


def out_weight_spec():
    return pl.BlockSpec((1, HALF, D), lambda i, *_: (3, 0, 0), pipeline_mode=pl.Buffered(1))


def branch_of(place, att_a, att_b, w_a, w_b, images, masked, vectors):
    count = images.shape[0]
    return call(
        branch_kernel,
        "branch",
        (count,),
        [rows_of(HALF), rows_of(HALF), out_weight_spec(), out_weight_spec(), image_of(D), image_of(1)]
        + [whole((1, D))] * len(vectors),
        [rows_of(D), rows_of(D)],
        [like((count * ROWS, D), F32), like((count * ROWS, D), BF)],
        scratch=[pltpu.VMEM((D, D), BF)],
        prefetch=1,
    )(place, att_a, att_b, *hbm(w_a, w_b, images), masked, *vectors)


def gelu_both(value):
    cdf = 0.5 * (1.0 + lax.erf(value * (0.5**0.5)))
    pdf = jnp.exp(value * value * -0.5) * 0.3989422804014327
    return value * cdf, cdf + value * pdf


def feed_kernel(first, half, pieces, bias, normed, grad_mlp, *rest):
    if not first:
        mlp_in, grad_in = rest[:2]
        rest = rest[2:]
    mlp, grad_normed, out, bias_grad, up, down, act, pre = rest
    planes, some, twice, _ = pieces.shape
    part = twice // 2
    slots = planes * some
    units = slots * part
    for slot in range(slots):
        at = slice(slot * part, slot * part + part)
        up[at, :] = pieces[slot // some, slot % some, 0:part]
        down[at, :] = pieces[slot // some, slot % some, part:twice]
    unit = lax.broadcasted_iota(jnp.int32, (slots, units), 1)
    owner = jnp.zeros_like(unit)
    for slot in range(1, slots):
        owner += (unit >= slot * part).astype(jnp.int32)
    is_own = owner == lax.broadcasted_iota(jnp.int32, (slots, units), 0)
    lane = (unit - owner * part + half * part)[0:1]
    hot = (lax.broadcasted_iota(jnp.int32, (128, units), 0) == lane).astype(BF)
    rows = jnp.concatenate([bias[0], bias[1]], axis=0).astype(BF)
    shift = column_sum(jnp.where(is_own, nn(rows, hot), 0.0))
    tiles = normed.shape[0] // ROWS

    def tile(index, total):
        at = pl.ds(pl.multiple_of(index * ROWS, ROWS), ROWS)
        value = nt(normed[at, :], up[...]) + shift
        active, slope = gelu_both(value)
        act[at, :] = active.astype(BF)
        grad = (nt(grad_mlp[at, :], down[...]) * slope).astype(BF)
        pre[at, :] = grad
        return total + column_sum(grad.astype(F32))

    unit_grad = lax.fori_loop(0, tiles, tile, jnp.zeros((1, units), F32), unroll=UNROLL)
    unit_high, unit_low = split_two(jnp.where(is_own, unit_grad, 0.0))
    grads = nt(unit_high, hot) + nt(unit_low, hot)
    bias_grad[0] = grads[0 : slots // 2]
    bias_grad[1] = grads[slots // 2 : slots]
    if first:
        mlp[...] = nn(act[...], down[...])
        grad_normed[...] = nn(pre[...], up[...])
    else:
        mlp[...] = mlp_in[...] + nn(act[...], down[...])
        grad_normed[...] = grad_in[...] + nn(pre[...], up[...])
    grad_up = tn(pre[...], normed[...]).astype(BF)
    grad_down = tn(act[...], grad_mlp[...]).astype(BF)
    for slot in range(slots):
        out[slot, 0:part, :] = grad_up[slot * part : slot * part + part, :]
        out[slot, part : 2 * part, :] = grad_down[slot * part : slot * part + part, :]


def feed(half, core, pieces, bias, normed, grad_mlp, carried):
    total = normed.shape[0]
    planes, some, twice, _ = pieces.shape
    slots, part = planes * some, twice // 2
    units = slots * part
    first = carried is None
    in_specs = [once(pieces.shape), pl.BlockSpec((2, slots // 2, 128), lambda i: (core, 0, 0))]
    in_specs += [once((total, D))] * 2
    operands = [pieces, bias, normed, grad_mlp]
    aliases = {}
    if not first:
        in_specs += [once((total, D))] * 2
        operands += list(carried)
        aliases = {4: 0, 5: 1}
    return call(
        partial(feed_kernel, first, half),
        "feed",
        (1,),
        in_specs,
        [once((total, D))] * 2 + [once((slots, twice, D)), whole((2, slots // 2, 128))],
        [
            like((total, D), F32),
            like((total, D), F32),
            like((slots, twice, D), BF),
            like((2, slots // 2, 128), F32),
        ],
        scratch=[
            pltpu.VMEM((units, D), BF),
            pltpu.VMEM((units, D), BF),
            pltpu.VMEM((total, units), BF),
            pltpu.VMEM((total, units), BF),
        ],
        aliases=aliases,
        turn=f"{half}{core}",
    )(*operands)


def middle_kernel(
    place,
    mlp_ref,
    grad_normed,
    branch,
    images,
    masked,
    out_grad,
    out_a,
    out_b,
    token,
    attn_scale,
    gain,
    ffn_scale,
    down_bias,
    output,
    grad_middle,
    grad_branch,
    grad_a,
    grad_b,
    sums,
    every,
):
    step = pl.program_id(0)

    @pl.when(step == 0)
    def _():
        sums[...] = jnp.zeros_like(sums)
        every[0:HALF, :] = out_a[0]
        every[HALF:D, :] = out_b[0]

    hidden = jnp.where(masked[0] > 0.0, token[...], images[0].astype(F32))
    side = branch[0:SEQ, :]
    middle = hidden + attn_scale[...] * side
    mlp = mlp_ref[0:SEQ, :] + down_bias[...]
    output[0] = (middle + ffn_scale[...] * mlp).astype(BF)
    grad_out = out_grad[0].astype(F32)
    sums[0:1, :] += column_sum(grad_out * mlp)
    normal, inv_std = norm_stats(middle)
    grad_two = grad_normed[0:SEQ, :]
    sums[1:2, :] += column_sum(grad_two * normal)
    sums[2:3, :] += column_sum(grad_two)
    grad = grad_out + norm_back(grad_two, normal, inv_std, gain[...])
    grad_middle[0:SEQ, :] = grad
    grad_middle[SEQ:ROWS, :] = jnp.zeros((ROWS - SEQ, D), F32)
    sums[3:4, :] += column_sum(grad * side)
    low_branch = (grad * attn_scale[...]).astype(BF)
    sums[4:5, :] += column_sum(low_branch.astype(F32))
    low, high = swap_halves(place[0], low_branch)
    grad_branch[0:SEQ, 0:HALF] = low
    grad_branch[0:SEQ, HALF:D] = high
    grad_branch[SEQ:ROWS, :] = jnp.zeros((ROWS - SEQ, D), BF)
    both = nt(grad_branch[...], every[...])
    grad_a[...] = both[:, 0:HALF].astype(BF)
    grad_b[...] = both[:, HALF:D].astype(BF)


def middle_of(place, mlp, grad_normed, branch, images, masked, out_grad, w_a, w_b, vectors):
    count = images.shape[0]
    total = count * ROWS
    return call(
        middle_kernel,
        "middle",
        (count,),
        [rows_of(D)] * 3
        + [image_of(D), image_of(1), image_of(D), out_weight_spec(), out_weight_spec()]
        + [whole((1, D))] * len(vectors),
        [image_of(D), rows_of(D), rows_of(D), rows_of(HALF), rows_of(HALF), whole((8, D))],
        [
            like((count, SEQ, D), BF),
            like((total, D), F32),
            like((total, D), BF),
            like((total, HALF), BF),
            like((total, HALF), BF),
            like((8, D), F32),
        ],
        scratch=[pltpu.VMEM((D, D), BF)],
        prefetch=1,
    )(place, mlp, grad_normed, branch, hbm(images), masked, *hbm(out_grad, w_a, w_b), *vectors)


def weight_kernel(place, grads, attended, normed, grad_branch, mine, other, sums):
    kind = pl.program_id(0)
    planes, groups, heads, part, _ = mine.shape

    def put(left, right):
        grad = tn(left, right).astype(BF)
        for plane in range(planes):
            for group in range(groups):
                for head in range(heads):
                    at = (group * heads + head) * HEAD_DIM + plane * part
                    mine[plane, group, head] = grad[at : at + part, 0:HALF]
                    other[plane, group, head] = grad[at : at + part, HALF:D]

    @pl.when(kind < 3)
    def _():
        put(grads[0], normed[...])
        total = jnp.broadcast_to(column_sum(grads[0].astype(F32)), (8, HALF))
        sums[0] = turn(place[1], total, part)

    @pl.when(kind == 3)
    def _():
        put(attended[...], grad_branch[...])


def weights_of(place, grads, attended, normed, grad_branch, shape, half):
    total = normed.shape[0]
    planes, groups, blocks, part, _ = shape
    out = pl.BlockSpec((planes, groups, blocks // 4, part, HALF), lambda t, *_: (0, 0, t, 0, 0))
    return call(
        weight_kernel,
        "weights",
        (4,),
        [
            pl.BlockSpec((1, total, HALF), lambda t, *_: (jnp.minimum(t, 2), 0, 0)),
            once((total, HALF)),
            once((total, D)),
            once((total, D)),
        ],
        [out, out, pl.BlockSpec((1, 8, HALF), lambda t, *_: (jnp.minimum(t, 2), 0, 0))],
        [like(shape, BF), like(shape, BF), like((3, 8, HALF), F32)],
        prefetch=1,
        turn=str(half),
    )(place, grads, attended, normed, grad_branch)


def end_kernel(
    place, back_a, back_b, w_a, w_b, grad_middle, images, masked, token, gain, images_grad, sums, every
):
    step = pl.program_id(0)

    @pl.when(step == 0)
    def _():
        sums[...] = jnp.zeros_like(sums)
        for index, ref in enumerate((w_a, w_b)):
            for kind in range(3):
                at = (3 * index + kind) * HALF
                every[at : at + HALF, :] = ref[kind]

    total = nn(jnp.concatenate([ref[kind] for ref in (back_a, back_b) for kind in range(3)], axis=1), every[...])
    low, high = swap_halves(place[0], total)
    grad_one = jnp.concatenate([low, high], axis=1)[0:SEQ]
    is_masked = masked[0] > 0.0
    hidden = jnp.where(is_masked, token[...], images[0].astype(F32))
    normal, inv_std = norm_stats(hidden)
    sums[0:1, :] += column_sum(grad_one * normal)
    sums[1:2, :] += column_sum(grad_one)
    grad = grad_middle[0:SEQ, :] + norm_back(grad_one, normal, inv_std, gain[...])
    images_grad[0] = jnp.where(is_masked, 0.0, grad).astype(BF)
    sums[2:3, :] += column_sum(jnp.where(is_masked, grad, 0.0))


def end_of(place, grads_a, grads_b, w_a, w_b, grad_middle, images, masked, vectors):
    count = images.shape[0]
    return call(
        end_kernel,
        "end",
        (count,),
        [three_rows()] * 2
        + [pl.BlockSpec((3, HALF, D), lambda i, *_: (0, 0, 0), pipeline_mode=pl.Buffered(1))] * 2
        + [rows_of(D), image_of(D), image_of(1)]
        + [whole((1, D))] * len(vectors),
        [image_of(D), whole((8, D))],
        [like((count, SEQ, D), BF), like((8, D), F32)],
        scratch=[pltpu.VMEM((6 * HALF, D), BF)],
        prefetch=1,
    )(place, grads_a, grads_b, *hbm(w_a, w_b), grad_middle, hbm(images), masked, *vectors)


def rows_kernel(heads, first, middle, last, table, shift_a, shift_b, unit_am, unit_ao, unit_bm, unit_bo, keep, send):
    lane = lax.broadcasted_iota(jnp.int32, (8, HALF), 1)
    for out, unit_a, unit_b in ((keep, unit_am, unit_bm), (send, unit_ao, unit_bo)):
        out[...] = jnp.zeros_like(out)
        out[0:1, :] = first[0:1, :]
        out[1:6, :] = middle[0:5, :]
        out[6:9, :] = last[0:3, :]
        at = 9
        for group in range(4):
            out[at : at + heads, :] = table[group * heads : group * heads + heads, :]
            at += heads
            for kind in (0, 2):
                row = (shift_a if group < 2 else shift_b)[kind]
                row = row if group % 2 == 0 else pltpu.roll(row, HALF - heads * HEAD_DIM, 1)
                out[at : at + 1, 0:HALF] = jnp.where(lane < heads * HEAD_DIM, row, 0.0)[0:1]
                at += 1
        for x in range(2):
            out[at + 8 * x : at + 8 * x + 8, 0:128] = unit_a[x] + unit_b[x]


def rows_of_sums(heads, operands):
    tall = 9 + 4 * (heads + 2) + 16
    return call(
        partial(rows_kernel, heads),
        "rows",
        (1,),
        [whole(value.shape) for value in operands],
        [whole((tall, D))] * 2,
        [like((tall, D), F32)] * 2,
    )(*operands)


def order_kernel(place, own, other, qkv_grad, out_grad, wide):
    core, plane_here = place[0], place[1]
    planes, blocks, part, _ = own.shape
    heads = blocks // 4
    for plane in range(planes):
        slot = jnp.bitwise_xor(plane_here, plane)
        for block in range(blocks):
            at = block * HEAD_DIM + plane * part
            for source, side in ((own, core), (other, 1 - core)):
                columns = pl.ds(pl.multiple_of(side * HALF, HALF), HALF)
                wide[at : at + part, columns] = source[slot, block].astype(F32)
    size = heads * HEAD_DIM
    for kind in range(3):
        qkv_grad[kind] = wide[kind * size : kind * size + size, :]
    out_grad[...] = wide[3 * size : 4 * size, :]


def order(place, gathered):
    planes, blocks, part, _ = gathered[0].shape
    size = blocks // 4 * HEAD_DIM
    return call(
        order_kernel,
        "order",
        (1,),
        [whole(gathered[0].shape)] * 2,
        [whole((3, size, D)), whole((size, D))],
        [like((3, size, D), F32), like((size, D), F32)],
        scratch=[pltpu.VMEM((4 * size, D), F32)],
        prefetch=1,
    )(place, *gathered)


class Butterfly:
    def __init__(self, mesh):
        self.dp, self.head = mesh.shape["dp"], mesh.shape["head"]
        self.far, self.near = 2, 1
        self.core, self.x, self.y = (self.head << bit for bit in range(3))

    def swap(self, value, mask):
        size = self.dp * self.head
        return lax.ppermute(value, BOTH, [(i, i ^ mask) for i in range(size)])


def after(done, *values):
    held = lax.optimization_barrier((done,) + values)[1:]
    return held if len(values) > 1 else held[0]


def tie(*values):
    return lax.optimization_barrier(values)


def add_low(own, come):
    return (own.astype(F32) + come.astype(F32)).astype(own.dtype)


def line(vector):
    return vector.reshape(1, -1)


class Layer:
    def __init__(self, place, args, masked, heads, groups):
        self.place, self.args, self.masked = place, args, masked
        self.heads, self.groups = heads, groups
        self.weights, self.streams, self.carried = [None, None], [None, None], None
        self.rel_bias, self.sources, self.block = [None, None], [None, None], 0

    def lines(self, *names):
        return [line(self.args[name]) for name in names]

    def start(self):
        a = self.args
        self.normed_one, self.grad_mlp, self.sums_start = start(
            self.place,
            a["images"],
            self.masked,
            a["out_grad"],
            *self.lines("mask_token", "attn_gain", "attn_shift", "ffn_scale"),
        )
        return self.sums_start

    def spots(self):
        rel_index = self.args["rel_index"]
        positions = jnp.arange(SEQ, dtype=jnp.int32)
        column = rel_index[:, 1]
        patch = (positions >= 1) & (positions < VALID)
        corner = jnp.min(jnp.where(patch, column, TABLE))
        spots = jnp.where(patch, column - corner, -1)
        spots = jnp.pad(spots, (0, ROWS - SEQ), constant_values=-1)
        edges = jnp.pad(rel_index[VALID:, :].T, ((0, ROWS - SEQ), (0, 8 - (SEQ - VALID))))
        self.where = (spots[None, :], edges)

    def bias(self, half):
        self.rel_bias[half] = bias_of(*self.where, self.sources[half], self.block, self.heads, half)

    def project(self, half, own, pieces):
        projected, self.weights[half] = project(
            self.place, own, pieces, self.normed_one, self.sources[half], self.block, self.heads, half
        )
        self.streams[half] = [projected]
        return projected

    def attend(self, half):
        self.streams[half] += attend(self.streams[half][0], self.rel_bias[half], half)
        return self.streams[half][1]

    def branch(self):
        self.side, self.normed_two = branch_of(
            self.place,
            self.streams[0][1],
            self.streams[1][1],
            self.weights[0],
            self.weights[1],
            self.args["images"],
            self.masked,
            self.lines("mask_token", "out_bias", "attn_scale", "ffn_gain", "ffn_shift"),
        )
        return self.normed_two

    def feed(self, half, core, pieces, bias):
        *self.carried, grads, unit_grads = feed(
            half, core, pieces, bias, self.normed_two, self.grad_mlp, self.carried
        )
        return grads, unit_grads

    def middle(self):
        self.output, self.grad_middle, self.grad_branch, *self.grad_att, self.sums_middle = middle_of(
            self.place,
            *self.carried,
            self.side,
            self.args["images"],
            self.masked,
            self.args["out_grad"],
            self.weights[0],
            self.weights[1],
            self.lines("mask_token", "attn_scale", "ffn_gain", "ffn_scale", "down_bias"),
        )
        self.back, self.grad_bias, self.shift_sums = [None, None], [None, None], [None, None]
        return self.grad_att[0]

    def attend_back(self, half):
        projected, _, probs = self.streams[half]
        self.back[half], self.grad_bias[half] = attend_back(projected, self.grad_att[half], probs, half)
        return self.grad_bias[half]

    def weight_grads(self, half):
        mine, other, self.shift_sums[half] = weights_of(
            self.place,
            self.back[half],
            self.streams[half][1],
            self.normed_one,
            self.grad_branch,
            (4, self.groups // 2, 4 * self.heads, HEAD_DIM // 4, HALF),
            half,
        )
        return mine, other

    def table(self):
        self.grad_table = table_of(*self.where, *self.grad_bias)
        return self.grad_table

    def end(self):
        self.images_grad, self.sums_end = end_of(
            self.place,
            self.back[0],
            self.back[1],
            self.weights[0],
            self.weights[1],
            self.grad_middle,
            self.args["images"],
            self.masked,
            self.lines("mask_token", "attn_gain"),
        )
        return self.sums_end

    def vectors(self):
        heads, groups = self.heads, self.groups
        rows = jnp.concatenate([self.sums_start[0:1], self.sums_middle[0:5], self.sums_end[0:3]], axis=0)
        width = heads * HEAD_DIM
        slots = []
        for group in range(groups):
            half, at = divmod(group, groups // 2)
            slots.append(self.grad_table[group * heads : group * heads + heads])
            sums = self.shift_sums[half][:, 0, at * width : at * width + width]
            slots += [jnp.pad(sums[kind : kind + 1], ((0, 0), (0, D - width))) for kind in (0, 2)]
        return rows, slots


def run_butterfly(net, layer, own_stack, small, shares):
    heads, groups = layer.heads, layer.groups
    dp_here = lax.axis_index("dp")
    core = dp_here % 2
    x_here, y_here = dp_here // 2 % 2, dp_here // 4
    plane = x_here * 2 + y_here
    layer.place = jnp.stack([core, plane]).astype(jnp.int32)
    part = HEAD_DIM // 4
    swap = net.swap
    own_units = shares.shape[1]
    half_units = own_units // 2
    blocks = 4 * heads
    thirds = (net.far, net.near, net.far + net.near)
    planes = (net.y, net.x, net.x + net.y)

    def around(value, masks):
        return [swap(value, mask) for mask in masks]

    def total(*values):
        return sum(value.astype(F32) for value in values).astype(values[0].dtype)

    mine = lax.dynamic_slice(own_stack, (0, plane * part, core * HALF), (blocks, part, HALF))
    mine = jnp.concatenate([mine, small], axis=0)
    far, near, third = around(mine, thirds)
    layer.spots()
    layer.masked, layer.place, *layer.where = tie(layer.masked, layer.place, *layer.where)
    done = layer.start()
    far, near, third = after(done, far, near, third)
    layer.sources, layer.block = [(mine, far), (near, third)], blocks

    far_own = jnp.concatenate([far, small], axis=0)[None]
    come_a = around(far_own, planes)
    ffn = shares.reshape(2, 2, half_units, D).transpose(1, 0, 2, 3).reshape(2, 2 * half_units, D)
    ffn = after(far, ffn)
    ffn_a, ffn_b = ffn[0], ffn[1]
    far_fa = swap(ffn_a, net.far)
    layer.bias(0)
    layer.rel_bias[0], near, third, far_fa, *come_a = tie(layer.rel_bias[0], near, third, far_fa, *come_a)
    pieces_a = jnp.stack([far_own] + come_a)
    cross_a = swap(pieces_a, net.core)
    rest = jnp.stack([near, third])
    come_b = around(rest, planes)
    ffn_a = jnp.stack([ffn_a, far_fa])
    near_fa = swap(ffn_a, net.near)
    layer.bias(1)
    layer.rel_bias[1], cross_a, near_fa = tie(layer.rel_bias[1], cross_a, near_fa)
    ffn_a = jnp.concatenate([ffn_a, near_fa])
    come_fa = around(ffn_a, planes[:2])
    layer.project(0, own_stack, (pieces_a, cross_a))
    layer.streams[0][0], ffn_b, ffn_a, *come_b = tie(layer.streams[0][0], ffn_b, ffn_a, *come_b)
    come_fa += around(ffn_a, planes[2:])
    pieces_b = jnp.stack([rest] + come_b)
    cross_b = swap(pieces_b, net.core)
    far_fb = swap(ffn_b, net.far)
    layer.attend(0)
    layer.streams[0][1], cross_b, far_fb = tie(layer.streams[0][1], cross_b, far_fb)
    ffn_b = jnp.stack([ffn_b, far_fb])
    near_fb = swap(ffn_b, net.near)
    layer.project(1, None, (pieces_b, cross_b))
    biases = units_of((pieces_a, cross_a), (pieces_b, cross_b), heads)
    layer.attend(1)
    layer.streams[1][1], biases, near_fb = tie(layer.streams[1][1], biases, near_fb)
    ffn_b = jnp.concatenate([ffn_b, near_fb])
    come_fb = around(ffn_b, planes[:2])
    layer.branch()
    layer.normed_two, ffn_b, *come_fa = tie(layer.normed_two, ffn_b, *come_fa)
    pieces_fa = jnp.stack([ffn_a] + come_fa)
    cross_fa = swap(pieces_fa, net.core)
    come_fb += around(ffn_b, planes[2:])
    grads_am, unit_am = layer.feed(0, 0, pieces_fa, biases)
    layer.carried[0], cross_fa = tie(layer.carried[0], cross_fa)
    grads_ao, unit_ao = layer.feed(0, 1, cross_fa, biases)
    layer.carried[0], *come_fb = tie(layer.carried[0], *come_fb)
    ffn_b = jnp.stack([ffn_b] + come_fb)

    def parts_of(own, come):
        own, come = [v.reshape(2, 2, 2, 2, 2 * half_units, D) for v in (own, come)]
        return (
            add_low(own[..., :half_units, :], come[..., :half_units, :]),
            add_low(own[..., half_units:, :], come[..., half_units:, :]),
        )

    come_a = swap(grads_ao, net.core)
    cross_fb = swap(ffn_b, net.core)
    grads_bm, unit_bm = layer.feed(1, 0, ffn_b, biases)
    layer.carried[0], come_a, cross_fb = tie(layer.carried[0], come_a, cross_fb)
    up_a, down_a = parts_of(grads_am, come_a)
    come_up_a, come_down_a = swap(up_a[1], net.x), swap(down_a[:, 1], net.y)
    grads_bo, unit_bo = layer.feed(1, 1, cross_fb, biases)
    come_b = swap(grads_bo, net.core)
    layer.middle()
    layer.grad_att[1], come_up_a, come_down_a, come_b = tie(layer.grad_att[1], come_up_a, come_down_a, come_b)
    up_a, down_a = add_low(up_a[0], come_up_a), add_low(down_a[:, 0], come_down_a)
    come_up_a, come_down_a = swap(up_a[1], net.y), swap(down_a[1], net.x)
    up_b, down_b = parts_of(grads_bm, come_b)
    come_up, come_down = swap(up_b[1], net.x), swap(down_b[:, 1], net.y)
    layer.attend_back(1)
    attn_b = layer.weight_grads(1)
    layer.grad_att[0], come_up_a, come_down_a, come_up, come_down, *attn_b = tie(
        layer.grad_att[0], come_up_a, come_down_a, come_up, come_down, *attn_b
    )
    come_attn_b = swap(attn_b[1], net.core)
    sum_a = jnp.concatenate([add_low(up_a[0], come_up_a), add_low(down_a[0], come_down_a)], axis=-2)
    come_a = swap(sum_a[1], net.near)
    up_b, down_b = add_low(up_b[0], come_up), add_low(down_b[:, 0], come_down)
    come_up, come_down = swap(up_b[1], net.y), swap(down_b[1], net.x)
    layer.attend_back(0)
    layer.back[0], come_a, come_up, come_down, come_attn_b = tie(
        layer.back[0], come_a, come_up, come_down, come_attn_b
    )
    sum_a = add_low(sum_a[0], come_a)
    sum_b = jnp.concatenate([add_low(up_b[0], come_up), add_low(down_b[0], come_down)], axis=-2)
    come_b = swap(sum_b[1], net.near)
    attn_b = [total(attn_b[0][slot], come_attn_b[slot]) for slot in range(4)]
    come_attn_b = [swap(value, mask) for value, mask in zip(attn_b[1:], planes)]
    attn_a = layer.weight_grads(0)
    layer.grad_bias[0], *attn_a = tie(layer.grad_bias[0], *attn_a)
    come_attn_a = swap(attn_a[1], net.core)
    layer.table()
    layer.grad_table, layer.grad_middle, come_b, come_attn_a, *come_attn_b = tie(
        layer.grad_table, layer.grad_middle, come_b, come_attn_a, *come_attn_b
    )
    attn_a = add_low(*attn_a[:1], come_attn_a).reshape(2, 2, 2, 4 * heads, part, HALF)
    come_plane = [swap(attn_a[0, 1], net.y), swap(attn_a[1, 0], net.x), swap(attn_a[1, 1], net.x + net.y)]
    attn_b = total(attn_b[0], *come_attn_b)
    come_attn_b = swap(attn_b, net.near)
    sum_b = add_low(sum_b[0], come_b)
    come_both = swap(jnp.stack([sum_a[1], sum_b[1]]), net.far)
    layer.end()
    layer.sums_end, come_attn_b, come_both = tie(layer.sums_end, come_attn_b, come_both)
    sum_a, sum_b = add_low(sum_a[0], come_both[0]), add_low(sum_b[0], come_both[1])

    unit_am, unit_ao, unit_bm, unit_bo = after(layer.sums_end, unit_am, unit_ao, unit_bm, unit_bo)
    extra = heads + 2
    fixed = 9
    wide = fixed + 4 * extra
    state, sent = rows_of_sums(
        heads,
        [layer.sums_start, layer.sums_middle, layer.sums_end, layer.grad_table]
        + layer.shift_sums
        + [unit_am, unit_ao, unit_bm, unit_bo],
    )
    come = swap(sent, net.core)
    come, come_attn_b, *come_plane = tie(come, come_attn_b, *come_plane)
    state = state + come
    attn = total(attn_a[0, 0], come_attn_b, *come_plane)

    fixed_wide, each = state[:wide], groups
    sent = [jnp.concatenate([fixed_wide, state[wide + at * each : wide + at * each + each]]) for at in (1, 2, 3)]
    last, *come = tie(swap(attn[1], net.far), *[swap(v, mask) for v, mask in zip(sent, planes)])
    state = state[: wide + each] + come[0] + come[1] + come[2]
    own = add_low(attn[0], last)
    last = [swap(own, mask) for mask in planes]
    sent = []
    for at in (1, 2, 3):
        group = state[fixed + at * extra : fixed + at * extra + extra]
        sent.append(jnp.concatenate([state[:fixed], group, state[wide + at : wide + at + 1]]))
    state = jnp.concatenate([state[: fixed + extra], state[wide : wide + 1]])
    *last, come_far, come_near, come_third = tie(*last, *[swap(v, mask) for v, mask in zip(sent, thirds)])
    own = jnp.stack([own] + last)
    other = swap(own, net.core)
    state = state + come_far + come_near + come_third
    rows, slots, units = state[:fixed], state[fixed : fixed + extra], state[fixed + extra, :own_units]
    gathered = [own, other]

    own_ffn = jnp.stack([sum_a, sum_b]).reshape(2, 2, half_units, D).transpose(1, 0, 2, 3)
    own_ffn = own_ffn.reshape(2, own_units, D).astype(F32)
    return gathered, own_ffn, units, rows, slots


def run_plain(layer, own_stack, small, shares, up_bias):
    heads, groups = layer.heads, layer.groups
    layer.place = jnp.zeros((2,), jnp.int32)
    part = HEAD_DIM // 4
    blocks = 4 * heads
    attn = lax.all_gather(own_stack, "head", axis=0, tiled=False)
    attn = attn.reshape(2, groups // 2, blocks, 4, part, 2, HALF).transpose(0, 5, 3, 1, 2, 4, 6)
    ffn = lax.all_gather(shares, BOTH, axis=1, tiled=True)
    half_units = ffn.shape[1] // 64
    ffn = ffn.reshape(2, 2, 2, 4, 4, half_units, D).transpose(1, 2, 3, 4, 0, 5, 6)
    ffn = ffn.reshape(2, 2, 4, 4, 2 * half_units, D)
    small = lax.all_gather(small, "head", axis=0, tiled=False)
    layer.sources = [(small[0], small[1]), (small[2], small[3])]
    biases = lax.all_gather(up_bias, BOTH, axis=0, tiled=True).reshape(2, 4, 8, half_units)
    biases = jnp.concatenate([biases[0], biases[1]], axis=-1)
    biases = jnp.pad(biases, ((0, 0), (0, 0), (0, 128 - 2 * half_units)))
    layer.start()
    layer.spots()
    for half in range(2):
        layer.bias(half)
        layer.project(half, None, (attn[half, 0], attn[half, 1]))
        layer.attend(half)
    layer.branch()
    ffn_grads, unit_grads = [], []
    for half in range(2):
        for core in range(2):
            grads, units = layer.feed(half, core, ffn[half, core], biases)
            ffn_grads.append(grads)
            unit_grads.append(units[..., half * half_units : half * half_units + half_units])
    layer.middle()
    attn_grads = []
    for half in range(2):
        layer.attend_back(half)
        attn_grads.append(jnp.stack(layer.weight_grads(half)))
    layer.table()
    layer.end()
    parts = jnp.stack(attn_grads).astype(F32)
    parts = parts.transpose(0, 3, 4, 2, 5, 1, 6).reshape(groups, blocks, HEAD_DIM, D)
    own = lax.psum_scatter(parts, "head", scatter_dimension=0, tiled=True)
    own = lax.psum(own, "dp").reshape(blocks, 4, part, 2, HALF)
    both = jnp.stack(ffn_grads).astype(F32).reshape(2, 2, 16, 2, half_units, D).transpose(3, 0, 1, 2, 4, 5)
    own_ffn = lax.psum_scatter(both.reshape(2, -1, D), BOTH, scatter_dimension=1, tiled=True)
    units = lax.psum_scatter(jnp.stack(unit_grads).reshape(-1), BOTH, scatter_dimension=0, tiled=True)
    rows, slots = layer.vectors()
    slots = jnp.concatenate(slots).reshape(groups, -1, D)
    slots = lax.psum_scatter(slots, "head", scatter_dimension=0, tiled=True)[0]
    return own.transpose(3, 1, 0, 2, 4), own_ffn, units, lax.psum(rows, BOTH), lax.psum(slots, "dp")


NAMES = (
    "images",
    "mask_ids",
    "rel_index",
    "out_grad",
    "mask_token",
    "attn_gain",
    "attn_shift",
    "qkv_weight",
    "qv_bias",
    "rel_table",
    "out_weight",
    "out_bias",
    "attn_scale",
    "ffn_gain",
    "ffn_shift",
    "up_weight",
    "up_bias",
    "down_weight",
    "down_bias",
    "ffn_scale",
)


def on_device(mesh, *arrays):
    args = dict(zip(NAMES, arrays))
    rel_table, up_weight = args["rel_table"], args["up_weight"]
    table_rows, heads = rel_table.shape
    own_units = up_weight.shape[1]
    positions = jnp.arange(SEQ, dtype=jnp.int32)
    masked = jnp.any(args["mask_ids"][:, :, None] == positions, axis=1).astype(F32)[:, :, None]
    net = Butterfly(mesh)
    layer = Layer(None, args, masked, heads, net.head)

    own_stack = jnp.concatenate([jnp.swapaxes(args["qkv_weight"], 1, 2), args["out_weight"][None]], axis=0)
    own_stack = own_stack.reshape(4 * heads, HEAD_DIM, D)
    up_bias = args["up_bias"].astype(F32)
    lines = jnp.pad(rel_table.T, ((0, 0), (0, TABLE - table_rows))).reshape(2 * heads, HALF)
    shifts = jnp.pad(args["qv_bias"], ((0, 0), (0, HALF - heads * HEAD_DIM)))
    high_lines, high_shifts = lax.reduce_precision(lines, 8, 7), lax.reduce_precision(shifts, 8, 7)
    beside = jnp.pad(up_bias[None], ((0, 1), (HALF - 128, 128 - own_units)))
    small = jnp.concatenate(
        [high_lines, lines - high_lines, high_shifts + beside, shifts - high_shifts], axis=0
    ).astype(BF)[None]
    shares = jnp.stack([up_weight.T, args["down_weight"]])
    if net.dp == 8 and net.head == 4:
        gathered, own_ffn, units, rows, slots = run_butterfly(net, layer, own_stack, small, shares)
    else:
        gathered, own_ffn, units, rows, slots = run_plain(layer, own_stack, small, shares, up_bias)
    qkv_weight_grad, out_weight_grad = order(layer.place, gathered)
    (
        down_bias_grad,
        ffn_scale_grad,
        ffn_gain_grad,
        ffn_shift_grad,
        attn_scale_grad,
        out_bias_grad,
        attn_gain_grad,
        attn_shift_grad,
        mask_token_grad,
    ) = rows
    return (
        layer.output,
        layer.images_grad,
        mask_token_grad,
        attn_gain_grad,
        attn_shift_grad,
        jnp.swapaxes(qkv_weight_grad, 1, 2),
        slots[heads : heads + 2, : heads * HEAD_DIM],
        slots[:heads, :table_rows].T,
        out_weight_grad,
        out_bias_grad,
        attn_scale_grad,
        ffn_gain_grad,
        ffn_shift_grad,
        own_ffn[0].T,
        units,
        own_ffn[1],
        down_bias_grad,
        ffn_scale_grad,
    )


def solution(mesh):
    in_specs = (
        P(("dp", "head"), None, None),
        P(("dp", "head"), None),
        P(),
        P(("dp", "head"), None, None),
        P(),
        P(),
        P(),
        P(None, None, "head"),
        P(None, "head"),
        P(None, "head"),
        P("head", None),
        P(),
        P(),
        P(),
        P(),
        P(None, ("dp", "head")),
        P(("dp", "head")),
        P(("dp", "head"), None),
        P(),
        P(),
    )
    out_specs = (
        P(("dp", "head"), None, None),
        P(("dp", "head"), None, None),
        P(),
        P(),
        P(),
        P(None, None, "head"),
        P(None, "head"),
        P(None, "head"),
        P("head", None),
        P(),
        P(),
        P(),
        P(),
        P(None, ("dp", "head")),
        P(("dp", "head")),
        P(("dp", "head"), None),
        P(),
        P(),
    )
    return jax.shard_map(
        partial(on_device, mesh), mesh=mesh, in_specs=in_specs, out_specs=out_specs, check_vma=False
    )
```

```python
from functools import partial

import jax
import jax.numpy as jnp
from jax import lax
from jax.experimental import pallas as pl
from jax.experimental.pallas import tpu as pltpu
from jax.sharding import PartitionSpec as P

HEAD_DIM = 64
SEQ = 200
VALID = 197
ROWS = 208
D = 768
HALF = 384
TABLE = 768
REACH = 384
CENTRE = 364
EPS = 1e-06
NEG = -1000000000.0
BOTH = ("dp", "head")
BF = jnp.bfloat16
F32 = jnp.float32
MIB = 1 << 20
UNROLL = 5
WEIGHT = dict(
    start=16, bias0=1, bias1=1, project0=1, project1=1, attend0=1, attend1=1, units=1, branch=1,
    feed00=64, feed01=1, feed10=64, feed11=64, middle=44, attend_back1=36, weights1=20, attend_back0=36,
    weights0=20, end=1, table=36, order=8, rows=1,
)
GRANTS = dict(
    start=8, bias=10, project=16, attend=20, branch=14, feed=26,
    middle=20, attend_back=18, weights=16, end=20, table=14, order=10, units=6, rows=6,
)


def nn(a, b):
    return lax.dot_general(a, b, (((1,), (0,)), ((), ())), preferred_element_type=F32)


def nt(a, b):
    return lax.dot_general(a, b, (((1,), (1,)), ((), ())), preferred_element_type=F32)


def tn(a, b):
    return lax.dot_general(a, b, (((0,), (0,)), ((), ())), preferred_element_type=F32)


def norm_stats(rows):
    row_mean = jnp.mean(rows, axis=-1, keepdims=True)
    centered = rows - row_mean
    inv_std = lax.rsqrt(jnp.mean(centered * centered, axis=-1, keepdims=True) + EPS)
    return centered * inv_std, inv_std


def norm_back(grad_normed, normal, inv_std, gain):
    scaled = grad_normed * gain
    return inv_std * (
        scaled
        - jnp.mean(scaled, axis=-1, keepdims=True)
        - normal * jnp.mean(scaled * normal, axis=-1, keepdims=True)
    )


def swap_halves(core, value):
    low, high = value[:, :HALF], value[:, HALF:]
    first = core == 0
    return jnp.where(first, low, high), jnp.where(first, high, low)


def turn(plane, value, part):
    width = value.shape[1]
    lane = lax.broadcasted_iota(jnp.int32, value.shape, 1)
    for bit in range(2):
        step = part << bit
        other = jnp.where((lane & step) != 0, pltpu.roll(value, step, 1), pltpu.roll(value, width - step, 1))
        value = jnp.where((plane >> bit) % 2 == 1, other, value)
    return value


def column_sum(value):
    return jnp.sum(value, axis=0, keepdims=True)


def split_two(value):
    high = value.astype(BF)
    return high, (value - high.astype(F32)).astype(BF)


def call(kernel, name, grid, in_specs, out_specs, out_shape, scratch=(), prefetch=0, aliases=None, turn=""):
    vmem, time = GRANTS[name], WEIGHT[name + turn]
    return pl.pallas_call(
        kernel,
        name=name,
        grid_spec=pltpu.PrefetchScalarGridSpec(
            num_scalar_prefetch=prefetch,
            grid=grid,
            in_specs=in_specs,
            out_specs=out_specs,
            scratch_shapes=list(scratch),
        ),
        out_shape=out_shape,
        input_output_aliases=aliases or {},
        compiler_params=pltpu.CompilerParams(vmem_limit_bytes=vmem * MIB),
        cost_estimate=pl.CostEstimate(flops=int(time * 1e9), bytes_accessed=MIB, transcendentals=0),
    )


def whole(shape):
    count = len(shape)
    return pl.BlockSpec(shape, lambda *_: (0,) * count)


def once(shape):
    count = len(shape)
    return pl.BlockSpec(shape, lambda *_: (0,) * count, pipeline_mode=pl.Buffered(1))


def three_rows():
    return pl.BlockSpec((3, ROWS, HALF), lambda i, *_: (0, i, 0))


def hbm(*values):
    held = [pltpu.with_memory_space_constraint(value, pltpu.HBM) for value in values]
    return held if len(held) > 1 else held[0]


def in_hbm(shape, dtype):
    return pltpu.HBM(shape, dtype)


def rows_of(width):
    return pl.BlockSpec((ROWS, width), lambda i, *_: (i, 0))


def image_of(width):
    return pl.BlockSpec((1, SEQ, width), lambda i, *_: (i, 0, 0))


def like(shape, dtype):
    return jax.ShapeDtypeStruct(shape, dtype)


def start_kernel(place, images, masked, out_grad, token, gain, shift, ffn_scale, normed, grad_mlp, sums):
    step = pl.program_id(0)
    hidden = jnp.where(masked[0] > 0.0, token[...], images[0].astype(F32))
    normal, _ = norm_stats(hidden)
    rows = normal * gain[...] + shift[...]
    low, high = swap_halves(place[0], rows)
    normed[0:SEQ, 0:HALF] = low.astype(BF)
    normed[0:SEQ, HALF:D] = high.astype(BF)
    normed[SEQ:ROWS, :] = jnp.zeros((ROWS - SEQ, D), BF)
    scaled = (out_grad[0].astype(F32) * ffn_scale[...]).astype(BF)
    grad_mlp[0:SEQ, :] = scaled
    grad_mlp[SEQ:ROWS, :] = jnp.zeros((ROWS - SEQ, D), BF)

    @pl.when(step == 0)
    def _():
        sums[...] = jnp.zeros_like(sums)

    sums[0:1, :] += column_sum(scaled.astype(F32))


def start(place, images, masked, out_grad, token, gain, shift, ffn_scale):
    count = images.shape[0]
    return call(
        start_kernel,
        "start",
        (count,),
        [image_of(D), image_of(1), image_of(D)] + [whole((1, D))] * 4,
        [rows_of(D), rows_of(D), whole((8, D))],
        [like((count * ROWS, D), BF), like((count * ROWS, D), BF), like((8, D), F32)],
        prefetch=1,
    )(place, hbm(images), masked, hbm(out_grad), token, gain, shift, ffn_scale)


def table_lines(block, few):
    both = block.astype(F32)
    both = both[0 : 2 * few] + both[2 * few : 4 * few]
    lines = [jnp.concatenate([both[2 * i : 2 * i + 1], both[2 * i + 1 : 2 * i + 2]], axis=1) for i in range(few)]
    return lines


def bias_kernel(spots_across, edge_rows, first, second, bias, ones_down, ones_across):
    few = bias.shape[0]
    lines = table_lines(jnp.where(pl.program_id(0) == 0, first[0], second[0]), few)

    @pl.when(pl.program_id(0) == 0)
    def _():
        where_across = lax.broadcasted_iota(jnp.int32, (REACH, ROWS), 0)
        hot = (spots_across[...] == where_across).astype(F32)
        ones_across[...] = hot.astype(BF)
        ones_down[...] = hot.T.astype(BF)

    table_high, table_low = split_two(jnp.concatenate(lines + [jnp.zeros((8 - few, TABLE), F32)], axis=0))
    reach = lax.broadcasted_iota(jnp.int32, (ROWS, TABLE), 1)
    picked = []
    for edge in range(SEQ - VALID):
        hot = (edge_rows[:, edge : edge + 1] == reach).astype(BF)
        picked.append(nt(hot, table_high) + nt(hot, table_low))
    key = lax.broadcasted_iota(jnp.int32, (ROWS, ROWS), 0)
    query = lax.broadcasted_iota(jnp.int32, (ROWS, ROWS), 1)
    for head in range(few):
        line = lines[head]
        spread = []
        for chunk in range(REACH // 128):
            turned = pltpu.roll(jnp.broadcast_to(line, (8, TABLE)), (TABLE - CENTRE + chunk * 128) % TABLE, 1)
            turned = jnp.broadcast_to(turned[0:1], (128, TABLE))
            spread.append(pltpu.roll(turned, 0, 1, stride=1, stride_axis=0)[:, :REACH])
        spread = jnp.concatenate(spread, axis=0)
        high, low = split_two(spread)
        middle = nn(nn(ones_down[...], high).astype(BF), ones_across[...])
        middle += nn(nn(ones_down[...], low).astype(BF), ones_across[...])
        value = jnp.where(key == 0, line[:, 730:731], middle)
        value = jnp.where(query == 0, jnp.where(key == 0, line[:, 731:732], line[:, 729:730]), value)
        for edge in range(SEQ - VALID):
            value = jnp.where(query == VALID + edge, picked[edge][:, head : head + 1], value)
        bias[head] = jnp.where(key >= VALID, NEG, value)


def small_spec(block):
    return pl.BlockSpec((1, 16, HALF), lambda *_: (block, 0, 0))


def bias_of(spots_across, edge_rows, sources, block, few, half):
    return call(
        bias_kernel,
        "bias",
        (2,),
        [whole(spots_across.shape), whole(edge_rows.shape)] + [small_spec(block)] * 2,
        pl.BlockSpec((few, ROWS, ROWS), lambda i: (i, 0, 0)),
        like((2 * few, ROWS, ROWS), F32),
        scratch=[pltpu.VMEM((ROWS, REACH), BF), pltpu.VMEM((REACH, ROWS), BF)],
        turn=str(half),
    )(spots_across, edge_rows, *sources)


def table_kernel(spots_across, edge_rows, grads, out):
    across = spots_across[...]
    ones_turned = ((REACH - 1) - across == lax.broadcasted_iota(jnp.int32, (REACH, ROWS), 0)).astype(BF)
    ones_turned = jnp.where(across >= 0, ones_turned, jnp.zeros_like(ones_turned))
    where_across = lax.broadcasted_iota(jnp.int32, (REACH, ROWS), 0)
    ones_down = (across == where_across).astype(F32).T.astype(BF)
    reach = lax.broadcasted_iota(jnp.int32, (ROWS, TABLE), 1)
    line = lax.broadcasted_iota(jnp.int32, (1, TABLE), 1)
    key = lax.broadcasted_iota(jnp.int32, (ROWS, 1), 0)
    for head in range(grads.shape[0]):
        grad = grads[head]
        high, low = split_two(grad)
        both = nn(nn(ones_turned, high).astype(BF), ones_down)
        both += nn(nn(ones_turned, low).astype(BF), ones_down)
        total = jnp.zeros((1, TABLE), F32)
        for chunk in range(REACH // 128):
            rows = both[chunk * 128 : chunk * 128 + 128]
            wide = jnp.concatenate([rows, jnp.zeros((128, TABLE - REACH), F32)], axis=1)
            added = column_sum(pltpu.roll(wide, 0, 1, stride=1, stride_axis=0))
            shift = (TABLE - (REACH - 1 - CENTRE) + chunk * 128) % TABLE
            total += pltpu.roll(jnp.broadcast_to(added, (8, TABLE)), shift, 1)[0:1]
        first = grad[:, 0:1]
        total += jnp.where(line == 729, column_sum(jnp.where(key > 0, first, 0.0)), 0.0)
        total += jnp.where(line == 731, grad[0:1, 0:1], 0.0)
        top = lax.broadcasted_iota(jnp.int32, (1, ROWS), 1)
        row = jnp.where((top > 0) & (top < VALID), grad[0:1, :], 0.0)
        total += jnp.where(line == 730, jnp.sum(row, axis=1, keepdims=True), 0.0)
        for edge in range(SEQ - VALID):
            spot = edge_rows[:, edge : edge + 1] == reach
            total += column_sum(jnp.where(spot, grad[:, VALID + edge : VALID + edge + 1], 0.0))
        out[head : head + 1, :] = total


def table_of(spots_across, edge_rows, grads):
    heads = grads.shape[0]
    return call(
        table_kernel,
        "table",
        (1,),
        [
            whole(spots_across.shape),
            whole(edge_rows.shape),
            whole(grads.shape),
        ],
        whole((heads, TABLE)),
        like((heads, TABLE), F32),
    )(spots_across, edge_rows, grads)


def project_kernel(has_own, heads, place, *refs):
    own = refs[0] if has_own else None
    pieces = refs[1 if has_own else 0 :]
    normed, small_low, small_high, outs, weights = pieces[2:]
    kind = pl.program_id(0)
    part = pieces[0].shape[3]
    skipped = 1 if has_own else 0
    if has_own:
        for head in range(heads):
            for plane in range(4):
                rows = own[kind * heads + head, plane * part : plane * part + part, :]
                low, high = swap_halves(place[0], rows)
                slot = jnp.bitwise_xor(place[1], plane)
                at = pl.ds(pl.multiple_of(head * HEAD_DIM + slot * part, part), part)
                weights[0, at, 0:HALF] = low
                weights[0, at, HALF:D] = high
    for core in range(2):
        for plane in range(4):
            piece = pieces[core]
            for group in range(piece.shape[1]):
                for head in range(heads):
                    at = ((group + skipped) * heads + head) * HEAD_DIM + plane * part
                    weights[0, at : at + part, core * HALF : core * HALF + HALF] = piece[
                        plane, group, kind * heads + head
                    ]

    @pl.when(kind < 3)
    def _():
        lane = lax.broadcasted_iota(jnp.int32, (8, HALF), 1)

        def shift_of(ref):
            block = ref[0].astype(F32)
            queries = block[4 * heads : 4 * heads + 1] + block[4 * heads + 2 : 4 * heads + 3]
            values = block[4 * heads + 1 : 4 * heads + 2] + block[4 * heads + 3 : 4 * heads + 4]
            row = jnp.broadcast_to(jnp.where(kind == 0, queries, values), (8, HALF))
            return jnp.where(lane < heads * HEAD_DIM, row, 0.0)

        scale = jnp.where(kind == 0, HEAD_DIM ** (-0.5), 1.0)
        shift = shift_of(small_low) + pltpu.roll(shift_of(small_high), heads * HEAD_DIM, 1)
        shift = turn(place[1], shift, part)[0:1] * jnp.where(kind == 1, 0.0, 1.0)
        outs[0] = ((nt(normed[...], weights[0]) + shift) * scale).astype(BF)


def project(place, own, pieces, normed, sources, block, heads, half):
    total = normed.shape[0]
    operands = ([] if own is None else [own]) + list(pieces) + [normed]
    return call(
        partial(project_kernel, own is not None, heads),
        "project",
        (4,),
        [once(value.shape) for value in operands] + [small_spec(block)] * 2,
        [
            pl.BlockSpec((1, total, HALF), lambda t, *_: (jnp.minimum(t, 2), 0, 0)),
            pl.BlockSpec((1, HALF, D), lambda t, *_: (t, 0, 0)),
        ],
        [like((3, total, HALF), BF), in_hbm((4, HALF, D), BF)],
        prefetch=1,
        turn=str(half),
    )(place, *operands, *sources)


def unit_kernel(own_at, far_at, row, *refs):
    pieces, out = refs[:-1], refs[-1]
    for core in range(2):
        for plane in range(4):
            far, near = pieces[core], pieces[2 + core]
            four = [far[plane, 0, own_at], far[plane, 0, far_at], near[plane, 0, 0], near[plane, 1, 0]]
            x, y = divmod(plane, 2)
            for z in range(4):
                rows = four[z].astype(F32)[row : row + 1, HALF - 128 : HALF]
                out[2 * core + x, 4 * y + z : 4 * y + z + 1, :] = rows


def units_of(far, near, heads):
    last = 4 * heads
    return call(
        partial(unit_kernel, 1, 0, last),
        "units",
        (1,),
        [pl.BlockSpec((4, 1, 2, 16, HALF), lambda i: (0, 0, last // 2, 0, 0))] * 2
        + [pl.BlockSpec((4, 2, 1, 16, HALF), lambda i: (0, 0, last, 0, 0))] * 2,
        whole((4, 8, 128)),
        like((4, 8, 128), F32),
    )(*far, *near)


PAIRS = [slice(pair * 128, pair * 128 + 128) for pair in range(HALF // 128)]


def one_side(pair, side):
    lane = lax.broadcasted_iota(jnp.int32, pair.shape, 1)
    return jnp.where((lane >= 64) if side else (lane < 64), pair, jnp.zeros_like(pair))


def attend_kernel(projected, bias, attended, probs):
    scores = []
    for index, cols in enumerate(PAIRS):
        for side in range(2):
            queries = one_side(projected[0, :, cols], side)
            scores.append(nt(projected[1, :, cols], queries) + bias[index * 2 + side])
    soft = []
    for head, score in enumerate(scores):
        expo = jnp.exp(score - jnp.max(score, axis=0, keepdims=True))
        soft.append((expo * (1.0 / jnp.sum(expo, axis=0, keepdims=True))).astype(BF))
        probs[0, head] = soft[head]
    for index, cols in enumerate(PAIRS):
        turned = projected[2, :, cols].T
        parts = [nn(turned[side * 64 : side * 64 + 64, :], soft[index * 2 + side]) for side in range(2)]
        attended[:, cols] = jnp.concatenate(parts, axis=0).T.astype(BF)


def attend(projected, bias, half):
    total = projected.shape[1]
    count, heads = total // ROWS, bias.shape[0]
    return call(
        attend_kernel,
        "attend",
        (count,),
        [three_rows(), once(bias.shape)],
        [rows_of(HALF), pl.BlockSpec((1, heads, ROWS, ROWS), lambda i: (i, 0, 0, 0))],
        [like((total, HALF), BF), in_hbm((count, heads, ROWS, ROWS), BF)],
        turn=str(half),
    )(projected, bias)


def attend_back_kernel(projected, grad_att, probs, grads, grad_bias):
    scale = HEAD_DIM ** (-0.5)

    @pl.when(pl.program_id(0) == 0)
    def _():
        grad_bias[...] = jnp.zeros_like(grad_bias)

    grad_probs = []
    for cols in PAIRS:
        for side in range(2):
            grad_probs.append(nt(projected[2, :, cols], one_side(grad_att[:, cols], side)))
    grad_scores = []
    for head, grad in enumerate(grad_probs):
        wide = probs[0, head].astype(F32)
        centre = jnp.sum(wide * grad, axis=0, keepdims=True)
        grad_scores.append((wide * (grad - centre)).astype(BF))
        grad_bias[head] += grad_scores[head].astype(F32)
    first = lax.broadcasted_iota(jnp.int32, (ROWS, 128), 1) < 64
    for index, cols in enumerate(PAIRS):
        heads = (2 * index, 2 * index + 1)
        turned = projected[1, :, cols].T
        by_value = [nn(probs[0, head], grad_att[:, cols]) for head in heads]
        by_key = [nn(grad_scores[head], projected[0, :, cols]) for head in heads]
        by_query = [nn(turned[64 * (head % 2) : 64 * (head % 2) + 64, :], grad_scores[head]) for head in heads]
        grads[2, :, cols] = jnp.where(first, by_value[0], by_value[1]).astype(BF)
        grads[1, :, cols] = jnp.where(first, by_key[0], by_key[1]).astype(BF)
        grads[0, :, cols] = (jnp.concatenate(by_query, axis=0).T * scale).astype(BF)


def attend_back(projected, grad_att, probs, half):
    total = projected.shape[1]
    count, heads = probs.shape[:2]
    return call(
        attend_back_kernel,
        "attend_back",
        (count,),
        [three_rows(), rows_of(HALF), pl.BlockSpec((1, heads, ROWS, ROWS), lambda i: (i, 0, 0, 0))],
        [three_rows(), whole((heads, ROWS, ROWS))],
        [like((3, total, HALF), BF), like((heads, ROWS, ROWS), F32)],
        turn=str(half),
    )(projected, grad_att, hbm(probs))


def branch_kernel(
    place, att_a, att_b, out_a, out_b, images, masked, token, out_bias, attn_scale, gain, shift, branch, normed, every
):
    @pl.when(pl.program_id(0) == 0)
    def _():
        every[0:HALF, :] = out_a[0]
        every[HALF:D, :] = out_b[0]

    mixed = nn(jnp.concatenate([att_a[...], att_b[...]], axis=1), every[...])
    low, high = swap_halves(place[0], mixed)
    rows = jnp.concatenate([low, high], axis=1) + out_bias[...]
    branch[...] = rows
    hidden = jnp.where(masked[0] > 0.0, token[...], images[0].astype(F32))
    middle = hidden + attn_scale[...] * rows[0:SEQ]
    normal, _ = norm_stats(middle)
    normed[0:SEQ, :] = (normal * gain[...] + shift[...]).astype(BF)
    normed[SEQ:ROWS, :] = jnp.zeros((ROWS - SEQ, D), BF)


def out_weight_spec():
    return pl.BlockSpec((1, HALF, D), lambda i, *_: (3, 0, 0), pipeline_mode=pl.Buffered(1))


def branch_of(place, att_a, att_b, w_a, w_b, images, masked, vectors):
    count = images.shape[0]
    return call(
        branch_kernel,
        "branch",
        (count,),
        [rows_of(HALF), rows_of(HALF), out_weight_spec(), out_weight_spec(), image_of(D), image_of(1)]
        + [whole((1, D))] * len(vectors),
        [rows_of(D), rows_of(D)],
        [like((count * ROWS, D), F32), like((count * ROWS, D), BF)],
        scratch=[pltpu.VMEM((D, D), BF)],
        prefetch=1,
    )(place, att_a, att_b, *hbm(w_a, w_b, images), masked, *vectors)


def gelu_both(value):
    cdf = 0.5 * (1.0 + lax.erf(value * (0.5**0.5)))
    pdf = jnp.exp(value * value * -0.5) * 0.3989422804014327
    return value * cdf, cdf + value * pdf


def feed_kernel(first, half, pieces, bias, normed, grad_mlp, *rest):
    if not first:
        mlp_in, grad_in = rest[:2]
        rest = rest[2:]
    mlp, grad_normed, out, bias_grad, up, down, act, pre = rest
    planes, some, twice, _ = pieces.shape
    part = twice // 2
    slots = planes * some
    units = slots * part
    for slot in range(slots):
        at = slice(slot * part, slot * part + part)
        up[at, :] = pieces[slot // some, slot % some, 0:part]
        down[at, :] = pieces[slot // some, slot % some, part:twice]
    unit = lax.broadcasted_iota(jnp.int32, (slots, units), 1)
    owner = jnp.zeros_like(unit)
    for slot in range(1, slots):
        owner += (unit >= slot * part).astype(jnp.int32)
    is_own = owner == lax.broadcasted_iota(jnp.int32, (slots, units), 0)
    lane = (unit - owner * part + half * part)[0:1]
    hot = (lax.broadcasted_iota(jnp.int32, (128, units), 0) == lane).astype(BF)
    rows = jnp.concatenate([bias[0], bias[1]], axis=0).astype(BF)
    shift = column_sum(jnp.where(is_own, nn(rows, hot), 0.0))
    tiles = normed.shape[0] // ROWS

    def tile(index, total):
        at = pl.ds(pl.multiple_of(index * ROWS, ROWS), ROWS)
        value = nt(normed[at, :], up[...]) + shift
        active, slope = gelu_both(value)
        act[at, :] = active.astype(BF)
        grad = (nt(grad_mlp[at, :], down[...]) * slope).astype(BF)
        pre[at, :] = grad
        return total + column_sum(grad.astype(F32))

    unit_grad = lax.fori_loop(0, tiles, tile, jnp.zeros((1, units), F32), unroll=UNROLL)
    unit_high, unit_low = split_two(jnp.where(is_own, unit_grad, 0.0))
    grads = nt(unit_high, hot) + nt(unit_low, hot)
    bias_grad[0] = grads[0 : slots // 2]
    bias_grad[1] = grads[slots // 2 : slots]
    if first:
        mlp[...] = nn(act[...], down[...])
        grad_normed[...] = nn(pre[...], up[...])
    else:
        mlp[...] = mlp_in[...] + nn(act[...], down[...])
        grad_normed[...] = grad_in[...] + nn(pre[...], up[...])
    grad_up = tn(pre[...], normed[...]).astype(BF)
    grad_down = tn(act[...], grad_mlp[...]).astype(BF)
    for slot in range(slots):
        out[slot, 0:part, :] = grad_up[slot * part : slot * part + part, :]
        out[slot, part : 2 * part, :] = grad_down[slot * part : slot * part + part, :]


def feed(half, core, pieces, bias, normed, grad_mlp, carried):
    total = normed.shape[0]
    planes, some, twice, _ = pieces.shape
    slots, part = planes * some, twice // 2
    units = slots * part
    first = carried is None
    in_specs = [once(pieces.shape), pl.BlockSpec((2, slots // 2, 128), lambda i: (core, 0, 0))]
    in_specs += [once((total, D))] * 2
    operands = [pieces, bias, normed, grad_mlp]
    aliases = {}
    if not first:
        in_specs += [once((total, D))] * 2
        operands += list(carried)
        aliases = {4: 0, 5: 1}
    return call(
        partial(feed_kernel, first, half),
        "feed",
        (1,),
        in_specs,
        [once((total, D))] * 2 + [once((slots, twice, D)), whole((2, slots // 2, 128))],
        [
            like((total, D), F32),
            like((total, D), F32),
            like((slots, twice, D), BF),
            like((2, slots // 2, 128), F32),
        ],
        scratch=[
            pltpu.VMEM((units, D), BF),
            pltpu.VMEM((units, D), BF),
            pltpu.VMEM((total, units), BF),
            pltpu.VMEM((total, units), BF),
        ],
        aliases=aliases,
        turn=f"{half}{core}",
    )(*operands)


def middle_kernel(
    place,
    mlp_ref,
    grad_normed,
    branch,
    images,
    masked,
    out_grad,
    out_a,
    out_b,
    token,
    attn_scale,
    gain,
    ffn_scale,
    down_bias,
    output,
    grad_middle,
    grad_branch,
    grad_a,
    grad_b,
    sums,
    every,
):
    step = pl.program_id(0)

    @pl.when(step == 0)
    def _():
        sums[...] = jnp.zeros_like(sums)
        every[0:HALF, :] = out_a[0]
        every[HALF:D, :] = out_b[0]

    hidden = jnp.where(masked[0] > 0.0, token[...], images[0].astype(F32))
    side = branch[0:SEQ, :]
    middle = hidden + attn_scale[...] * side
    mlp = mlp_ref[0:SEQ, :] + down_bias[...]
    output[0] = (middle + ffn_scale[...] * mlp).astype(BF)
    grad_out = out_grad[0].astype(F32)
    sums[0:1, :] += column_sum(grad_out * mlp)
    normal, inv_std = norm_stats(middle)
    grad_two = grad_normed[0:SEQ, :]
    sums[1:2, :] += column_sum(grad_two * normal)
    sums[2:3, :] += column_sum(grad_two)
    grad = grad_out + norm_back(grad_two, normal, inv_std, gain[...])
    grad_middle[0:SEQ, :] = grad
    grad_middle[SEQ:ROWS, :] = jnp.zeros((ROWS - SEQ, D), F32)
    sums[3:4, :] += column_sum(grad * side)
    low_branch = (grad * attn_scale[...]).astype(BF)
    sums[4:5, :] += column_sum(low_branch.astype(F32))
    low, high = swap_halves(place[0], low_branch)
    grad_branch[0:SEQ, 0:HALF] = low
    grad_branch[0:SEQ, HALF:D] = high
    grad_branch[SEQ:ROWS, :] = jnp.zeros((ROWS - SEQ, D), BF)
    both = nt(grad_branch[...], every[...])
    grad_a[...] = both[:, 0:HALF].astype(BF)
    grad_b[...] = both[:, HALF:D].astype(BF)


def middle_of(place, mlp, grad_normed, branch, images, masked, out_grad, w_a, w_b, vectors):
    count = images.shape[0]
    total = count * ROWS
    return call(
        middle_kernel,
        "middle",
        (count,),
        [rows_of(D)] * 3
        + [image_of(D), image_of(1), image_of(D), out_weight_spec(), out_weight_spec()]
        + [whole((1, D))] * len(vectors),
        [image_of(D), rows_of(D), rows_of(D), rows_of(HALF), rows_of(HALF), whole((8, D))],
        [
            like((count, SEQ, D), BF),
            like((total, D), F32),
            like((total, D), BF),
            like((total, HALF), BF),
            like((total, HALF), BF),
            like((8, D), F32),
        ],
        scratch=[pltpu.VMEM((D, D), BF)],
        prefetch=1,
    )(place, mlp, grad_normed, branch, hbm(images), masked, *hbm(out_grad, w_a, w_b), *vectors)


def weight_kernel(place, grads, attended, normed, grad_branch, mine, other, sums):
    kind = pl.program_id(0)
    planes, groups, heads, part, _ = mine.shape

    def put(left, right):
        grad = tn(left, right).astype(BF)
        for plane in range(planes):
            for group in range(groups):
                for head in range(heads):
                    at = (group * heads + head) * HEAD_DIM + plane * part
                    mine[plane, group, head] = grad[at : at + part, 0:HALF]
                    other[plane, group, head] = grad[at : at + part, HALF:D]

    @pl.when(kind < 3)
    def _():
        put(grads[0], normed[...])
        total = jnp.broadcast_to(column_sum(grads[0].astype(F32)), (8, HALF))
        sums[0] = turn(place[1], total, part)

    @pl.when(kind == 3)
    def _():
        put(attended[...], grad_branch[...])


def weights_of(place, grads, attended, normed, grad_branch, shape, half):
    total = normed.shape[0]
    planes, groups, blocks, part, _ = shape
    out = pl.BlockSpec((planes, groups, blocks // 4, part, HALF), lambda t, *_: (0, 0, t, 0, 0))
    return call(
        weight_kernel,
        "weights",
        (4,),
        [
            pl.BlockSpec((1, total, HALF), lambda t, *_: (jnp.minimum(t, 2), 0, 0)),
            once((total, HALF)),
            once((total, D)),
            once((total, D)),
        ],
        [out, out, pl.BlockSpec((1, 8, HALF), lambda t, *_: (jnp.minimum(t, 2), 0, 0))],
        [like(shape, BF), like(shape, BF), like((3, 8, HALF), F32)],
        prefetch=1,
        turn=str(half),
    )(place, grads, attended, normed, grad_branch)


def end_kernel(
    place, back_a, back_b, w_a, w_b, grad_middle, images, masked, token, gain, images_grad, sums, every
):
    step = pl.program_id(0)

    @pl.when(step == 0)
    def _():
        sums[...] = jnp.zeros_like(sums)
        for index, ref in enumerate((w_a, w_b)):
            for kind in range(3):
                at = (3 * index + kind) * HALF
                every[at : at + HALF, :] = ref[kind]

    total = nn(jnp.concatenate([ref[kind] for ref in (back_a, back_b) for kind in range(3)], axis=1), every[...])
    low, high = swap_halves(place[0], total)
    grad_one = jnp.concatenate([low, high], axis=1)[0:SEQ]
    is_masked = masked[0] > 0.0
    hidden = jnp.where(is_masked, token[...], images[0].astype(F32))
    normal, inv_std = norm_stats(hidden)
    sums[0:1, :] += column_sum(grad_one * normal)
    sums[1:2, :] += column_sum(grad_one)
    grad = grad_middle[0:SEQ, :] + norm_back(grad_one, normal, inv_std, gain[...])
    images_grad[0] = jnp.where(is_masked, 0.0, grad).astype(BF)
    sums[2:3, :] += column_sum(jnp.where(is_masked, grad, 0.0))


def end_of(place, grads_a, grads_b, w_a, w_b, grad_middle, images, masked, vectors):
    count = images.shape[0]
    return call(
        end_kernel,
        "end",
        (count,),
        [three_rows()] * 2
        + [pl.BlockSpec((3, HALF, D), lambda i, *_: (0, 0, 0), pipeline_mode=pl.Buffered(1))] * 2
        + [rows_of(D), image_of(D), image_of(1)]
        + [whole((1, D))] * len(vectors),
        [image_of(D), whole((8, D))],
        [like((count, SEQ, D), BF), like((8, D), F32)],
        scratch=[pltpu.VMEM((6 * HALF, D), BF)],
        prefetch=1,
    )(place, grads_a, grads_b, *hbm(w_a, w_b), grad_middle, hbm(images), masked, *vectors)


def rows_kernel(heads, first, middle, last, table_a, table_b, shift_a, shift_b, unit_am, unit_ao, unit_bm, unit_bo, keep, send):
    lane = lax.broadcasted_iota(jnp.int32, (8, HALF), 1)
    for out, unit_a, unit_b in ((keep, unit_am, unit_bm), (send, unit_ao, unit_bo)):
        out[...] = jnp.zeros_like(out)
        out[0:1, :] = first[0:1, :]
        out[1:6, :] = middle[0:5, :]
        out[6:9, :] = last[0:3, :]
        at = 9
        for group in range(4):
            table, low = table_a if group < 2 else table_b, group % 2 * heads
            out[at : at + heads, :] = table[low : low + heads, :]
            at += heads
            for kind in (0, 2):
                row = (shift_a if group < 2 else shift_b)[kind]
                row = row if group % 2 == 0 else pltpu.roll(row, HALF - heads * HEAD_DIM, 1)
                out[at : at + 1, 0:HALF] = jnp.where(lane < heads * HEAD_DIM, row, 0.0)[0:1]
                at += 1
        for x in range(2):
            out[at + 8 * x : at + 8 * x + 8, 0:128] = unit_a[x] + unit_b[x]


def rows_of_sums(heads, operands):
    tall = 9 + 4 * (heads + 2) + 16
    return call(
        partial(rows_kernel, heads),
        "rows",
        (1,),
        [whole(value.shape) for value in operands],
        [whole((tall, D))] * 2,
        [like((tall, D), F32)] * 2,
    )(*operands)


def order_kernel(place, own, other, qkv_grad, out_grad, wide):
    core, plane_here = place[0], place[1]
    planes, blocks, part, _ = own.shape
    heads = blocks // 4
    for plane in range(planes):
        slot = jnp.bitwise_xor(plane_here, plane)
        for block in range(blocks):
            at = block * HEAD_DIM + plane * part
            for source, side in ((own, core), (other, 1 - core)):
                columns = pl.ds(pl.multiple_of(side * HALF, HALF), HALF)
                wide[at : at + part, columns] = source[slot, block].astype(F32)
    size = heads * HEAD_DIM
    for kind in range(3):
        qkv_grad[kind] = wide[kind * size : kind * size + size, :]
    out_grad[...] = wide[3 * size : 4 * size, :]


def order(place, gathered):
    planes, blocks, part, _ = gathered[0].shape
    size = blocks // 4 * HEAD_DIM
    return call(
        order_kernel,
        "order",
        (1,),
        [whole(gathered[0].shape)] * 2,
        [whole((3, size, D)), whole((size, D))],
        [like((3, size, D), F32), like((size, D), F32)],
        scratch=[pltpu.VMEM((4 * size, D), F32)],
        prefetch=1,
    )(place, *gathered)


class Butterfly:
    def __init__(self, mesh):
        self.dp, self.head = mesh.shape["dp"], mesh.shape["head"]
        self.far, self.near = 2, 1
        self.core, self.x, self.y = (self.head << bit for bit in range(3))

    def swap(self, value, mask):
        size = self.dp * self.head
        return lax.ppermute(value, BOTH, [(i, i ^ mask) for i in range(size)])


def after(done, *values):
    held = lax.optimization_barrier((done,) + values)[1:]
    return held if len(values) > 1 else held[0]


def tie(*values):
    return lax.optimization_barrier(values)


def add_low(own, come):
    return (own.astype(F32) + come.astype(F32)).astype(own.dtype)


def line(vector):
    return vector.reshape(1, -1)


class Layer:
    def __init__(self, place, args, masked, heads, groups):
        self.place, self.args, self.masked = place, args, masked
        self.heads, self.groups = heads, groups
        self.weights, self.streams, self.carried = [None, None], [None, None], None
        self.rel_bias, self.sources, self.block = [None, None], [None, None], 0

    def lines(self, *names):
        return [line(self.args[name]) for name in names]

    def start(self):
        a = self.args
        self.normed_one, self.grad_mlp, self.sums_start = start(
            self.place,
            a["images"],
            self.masked,
            a["out_grad"],
            *self.lines("mask_token", "attn_gain", "attn_shift", "ffn_scale"),
        )
        return self.sums_start

    def spots(self):
        rel_index = self.args["rel_index"]
        positions = jnp.arange(SEQ, dtype=jnp.int32)
        column = rel_index[:, 1]
        patch = (positions >= 1) & (positions < VALID)
        corner = jnp.min(jnp.where(patch, column, TABLE))
        spots = jnp.where(patch, column - corner, -1)
        spots = jnp.pad(spots, (0, ROWS - SEQ), constant_values=-1)
        edges = jnp.pad(rel_index[VALID:, :].T, ((0, ROWS - SEQ), (0, 8 - (SEQ - VALID))))
        self.where = (spots[None, :], edges)

    def bias(self, half):
        self.rel_bias[half] = bias_of(*self.where, self.sources[half], self.block, self.heads, half)

    def project(self, half, own, pieces):
        projected, self.weights[half] = project(
            self.place, own, pieces, self.normed_one, self.sources[half], self.block, self.heads, half
        )
        self.streams[half] = [projected]
        return projected

    def attend(self, half):
        self.streams[half] += attend(self.streams[half][0], self.rel_bias[half], half)
        return self.streams[half][1]

    def branch(self):
        self.side, self.normed_two = branch_of(
            self.place,
            self.streams[0][1],
            self.streams[1][1],
            self.weights[0],
            self.weights[1],
            self.args["images"],
            self.masked,
            self.lines("mask_token", "out_bias", "attn_scale", "ffn_gain", "ffn_shift"),
        )
        return self.normed_two

    def feed(self, half, core, pieces, bias):
        *self.carried, grads, unit_grads = feed(
            half, core, pieces, bias, self.normed_two, self.grad_mlp, self.carried
        )
        return grads, unit_grads

    def middle(self):
        self.output, self.grad_middle, self.grad_branch, *self.grad_att, self.sums_middle = middle_of(
            self.place,
            *self.carried,
            self.side,
            self.args["images"],
            self.masked,
            self.args["out_grad"],
            self.weights[0],
            self.weights[1],
            self.lines("mask_token", "attn_scale", "ffn_gain", "ffn_scale", "down_bias"),
        )
        self.back, self.grad_bias, self.shift_sums = [None, None], [None, None], [None, None]
        self.grad_table = [None, None]
        return self.grad_att[0]

    def attend_back(self, half):
        projected, _, probs = self.streams[half]
        self.back[half], self.grad_bias[half] = attend_back(projected, self.grad_att[half], probs, half)
        return self.grad_bias[half]

    def weight_grads(self, half):
        mine, other, self.shift_sums[half] = weights_of(
            self.place,
            self.back[half],
            self.streams[half][1],
            self.normed_one,
            self.grad_branch,
            (4, self.groups // 2, 4 * self.heads, HEAD_DIM // 4, HALF),
            half,
        )
        return mine, other

    def table(self, half):
        self.grad_table[half] = table_of(*self.where, self.grad_bias[half])

    def end(self):
        self.images_grad, self.sums_end = end_of(
            self.place,
            self.back[0],
            self.back[1],
            self.weights[0],
            self.weights[1],
            self.grad_middle,
            self.args["images"],
            self.masked,
            self.lines("mask_token", "attn_gain"),
        )
        return self.sums_end

    def vectors(self):
        heads, groups = self.heads, self.groups
        rows = jnp.concatenate([self.sums_start[0:1], self.sums_middle[0:5], self.sums_end[0:3]], axis=0)
        width = heads * HEAD_DIM
        slots = []
        for group in range(groups):
            half, at = divmod(group, groups // 2)
            slots.append(self.grad_table[half][at * heads : at * heads + heads])
            sums = self.shift_sums[half][:, 0, at * width : at * width + width]
            slots += [jnp.pad(sums[kind : kind + 1], ((0, 0), (0, D - width))) for kind in (0, 2)]
        return rows, slots


def run_butterfly(net, layer, own_stack, small, shares):
    heads, groups = layer.heads, layer.groups
    dp_here = lax.axis_index("dp")
    core = dp_here % 2
    x_here, y_here = dp_here // 2 % 2, dp_here // 4
    plane = x_here * 2 + y_here
    layer.place = jnp.stack([core, plane]).astype(jnp.int32)
    part = HEAD_DIM // 4
    swap = net.swap
    own_units = shares.shape[1]
    half_units = own_units // 2
    blocks = 4 * heads
    thirds = (net.far, net.near, net.far + net.near)
    planes = (net.y, net.x, net.x + net.y)

    def around(value, masks):
        return [swap(value, mask) for mask in masks]

    def total(*values):
        return sum(value.astype(F32) for value in values).astype(values[0].dtype)

    mine = lax.dynamic_slice(own_stack, (0, plane * part, core * HALF), (blocks, part, HALF))
    mine = jnp.concatenate([mine, small], axis=0)
    far, near, third = around(mine, thirds)
    layer.spots()
    layer.masked, layer.place, *layer.where = tie(layer.masked, layer.place, *layer.where)
    done = layer.start()
    far, near, third = after(done, far, near, third)
    layer.sources, layer.block = [(mine, far), (near, third)], blocks

    far_own = jnp.concatenate([far, small], axis=0)[None]
    come_a = around(far_own, planes)
    ffn = shares.reshape(2, 2, half_units, D).transpose(1, 0, 2, 3).reshape(2, 2 * half_units, D)
    ffn = after(far, ffn)
    ffn_a, ffn_b = ffn[0], ffn[1]
    far_fa = swap(ffn_a, net.far)
    layer.bias(0)
    layer.rel_bias[0], near, third, far_fa, *come_a = tie(layer.rel_bias[0], near, third, far_fa, *come_a)
    pieces_a = jnp.stack([far_own] + come_a)
    cross_a = swap(pieces_a, net.core)
    rest = jnp.stack([near, third])
    come_b = around(rest, planes)
    ffn_a = jnp.stack([ffn_a, far_fa])
    near_fa = swap(ffn_a, net.near)
    layer.bias(1)
    layer.rel_bias[1], cross_a, near_fa = tie(layer.rel_bias[1], cross_a, near_fa)
    ffn_a = jnp.concatenate([ffn_a, near_fa])
    come_fa = around(ffn_a, planes[:2])
    layer.project(0, own_stack, (pieces_a, cross_a))
    layer.streams[0][0], ffn_b, ffn_a, *come_b = tie(layer.streams[0][0], ffn_b, ffn_a, *come_b)
    come_fa += around(ffn_a, planes[2:])
    pieces_b = jnp.stack([rest] + come_b)
    cross_b = swap(pieces_b, net.core)
    far_fb = swap(ffn_b, net.far)
    layer.attend(0)
    layer.streams[0][1], cross_b, far_fb = tie(layer.streams[0][1], cross_b, far_fb)
    ffn_b = jnp.stack([ffn_b, far_fb])
    near_fb = swap(ffn_b, net.near)
    layer.project(1, None, (pieces_b, cross_b))
    biases = units_of((pieces_a, cross_a), (pieces_b, cross_b), heads)
    layer.attend(1)
    layer.streams[1][1], biases, near_fb = tie(layer.streams[1][1], biases, near_fb)
    ffn_b = jnp.concatenate([ffn_b, near_fb])
    come_fb = around(ffn_b, planes[:2])
    layer.branch()
    layer.normed_two, ffn_b, *come_fa = tie(layer.normed_two, ffn_b, *come_fa)
    pieces_fa = jnp.stack([ffn_a] + come_fa)
    cross_fa = swap(pieces_fa, net.core)
    come_fb += around(ffn_b, planes[2:])
    grads_am, unit_am = layer.feed(0, 0, pieces_fa, biases)
    layer.carried[0], cross_fa = tie(layer.carried[0], cross_fa)
    grads_ao, unit_ao = layer.feed(0, 1, cross_fa, biases)
    layer.carried[0], *come_fb = tie(layer.carried[0], *come_fb)
    ffn_b = jnp.stack([ffn_b] + come_fb)

    def parts_of(own, come):
        own, come = [v.reshape(2, 2, 2, 2, 2 * half_units, D) for v in (own, come)]
        return (
            add_low(own[..., :half_units, :], come[..., :half_units, :]),
            add_low(own[..., half_units:, :], come[..., half_units:, :]),
        )

    come_a = swap(grads_ao, net.core)
    cross_fb = swap(ffn_b, net.core)
    grads_bm, unit_bm = layer.feed(1, 0, ffn_b, biases)
    layer.carried[0], come_a, cross_fb = tie(layer.carried[0], come_a, cross_fb)
    up_a, down_a = parts_of(grads_am, come_a)
    come_up_a, come_down_a = swap(up_a[1], net.x), swap(down_a[:, 1], net.y)
    grads_bo, unit_bo = layer.feed(1, 1, cross_fb, biases)
    come_b = swap(grads_bo, net.core)
    layer.middle()
    layer.grad_att[1], come_up_a, come_down_a, come_b = tie(layer.grad_att[1], come_up_a, come_down_a, come_b)
    up_a, down_a = add_low(up_a[0], come_up_a), add_low(down_a[:, 0], come_down_a)
    come_up_a, come_down_a = swap(up_a[1], net.y), swap(down_a[1], net.x)
    up_b, down_b = parts_of(grads_bm, come_b)
    come_up, come_down = swap(up_b[1], net.x), swap(down_b[:, 1], net.y)
    layer.attend_back(1)
    attn_b = layer.weight_grads(1)
    layer.table(1)
    layer.grad_table[1], layer.grad_att[0], come_up_a, come_down_a, come_up, come_down, *attn_b = tie(
        layer.grad_table[1], layer.grad_att[0], come_up_a, come_down_a, come_up, come_down, *attn_b
    )
    come_attn_b = swap(attn_b[1], net.core)
    sum_a = jnp.concatenate([add_low(up_a[0], come_up_a), add_low(down_a[0], come_down_a)], axis=-2)
    come_a = swap(sum_a[1], net.near)
    up_b, down_b = add_low(up_b[0], come_up), add_low(down_b[:, 0], come_down)
    come_up, come_down = swap(up_b[1], net.y), swap(down_b[1], net.x)
    layer.attend_back(0)
    layer.back[0], come_a, come_up, come_down, come_attn_b = tie(
        layer.back[0], come_a, come_up, come_down, come_attn_b
    )
    sum_a = add_low(sum_a[0], come_a)
    sum_b = jnp.concatenate([add_low(up_b[0], come_up), add_low(down_b[0], come_down)], axis=-2)
    come_b = swap(sum_b[1], net.near)
    attn_b = [total(attn_b[0][slot], come_attn_b[slot]) for slot in range(4)]
    come_attn_b = [swap(value, mask) for value, mask in zip(attn_b[1:], planes)]
    attn_a = layer.weight_grads(0)
    layer.grad_bias[0], *attn_a = tie(layer.grad_bias[0], *attn_a)
    come_attn_a = swap(attn_a[1], net.core)
    layer.table(0)
    layer.grad_table[0], layer.grad_middle, come_b, come_attn_a, *come_attn_b = tie(
        layer.grad_table[0], layer.grad_middle, come_b, come_attn_a, *come_attn_b
    )
    attn_a = add_low(*attn_a[:1], come_attn_a).reshape(2, 2, 2, 4 * heads, part, HALF)
    come_plane = [swap(attn_a[0, 1], net.y), swap(attn_a[1, 0], net.x), swap(attn_a[1, 1], net.x + net.y)]
    attn_b = total(attn_b[0], *come_attn_b)
    come_attn_b = swap(attn_b, net.near)
    sum_b = add_low(sum_b[0], come_b)
    come_both = swap(jnp.stack([sum_a[1], sum_b[1]]), net.far)
    layer.end()
    layer.sums_end, come_attn_b, come_both = tie(layer.sums_end, come_attn_b, come_both)
    sum_a, sum_b = add_low(sum_a[0], come_both[0]), add_low(sum_b[0], come_both[1])

    unit_am, unit_ao, unit_bm, unit_bo = after(layer.sums_end, unit_am, unit_ao, unit_bm, unit_bo)
    extra = heads + 2
    fixed = 9
    wide = fixed + 4 * extra
    state, sent = rows_of_sums(
        heads,
        [layer.sums_start, layer.sums_middle, layer.sums_end]
        + layer.grad_table
        + layer.shift_sums
        + [unit_am, unit_ao, unit_bm, unit_bo],
    )
    come = swap(sent, net.core)
    come, come_attn_b, *come_plane = tie(come, come_attn_b, *come_plane)
    state = state + come
    attn = total(attn_a[0, 0], come_attn_b, *come_plane)

    fixed_wide, each = state[:wide], groups
    sent = [jnp.concatenate([fixed_wide, state[wide + at * each : wide + at * each + each]]) for at in (1, 2, 3)]
    last, *come = tie(swap(attn[1], net.far), *[swap(v, mask) for v, mask in zip(sent, planes)])
    state = state[: wide + each] + come[0] + come[1] + come[2]
    own = add_low(attn[0], last)
    last = [swap(own, mask) for mask in planes]
    sent = []
    for at in (1, 2, 3):
        group = state[fixed + at * extra : fixed + at * extra + extra]
        sent.append(jnp.concatenate([state[:fixed], group, state[wide + at : wide + at + 1]]))
    state = jnp.concatenate([state[: fixed + extra], state[wide : wide + 1]])
    *last, come_far, come_near, come_third = tie(*last, *[swap(v, mask) for v, mask in zip(sent, thirds)])
    own = jnp.stack([own] + last)
    other = swap(own, net.core)
    state = state + come_far + come_near + come_third
    rows, slots, units = state[:fixed], state[fixed : fixed + extra], state[fixed + extra, :own_units]
    gathered = [own, other]

    own_ffn = jnp.stack([sum_a, sum_b]).reshape(2, 2, half_units, D).transpose(1, 0, 2, 3)
    own_ffn = own_ffn.reshape(2, own_units, D).astype(F32)
    return gathered, own_ffn, units, rows, slots


def run_plain(layer, own_stack, small, shares, up_bias):
    heads, groups = layer.heads, layer.groups
    layer.place = jnp.zeros((2,), jnp.int32)
    part = HEAD_DIM // 4
    blocks = 4 * heads
    attn = lax.all_gather(own_stack, "head", axis=0, tiled=False)
    attn = attn.reshape(2, groups // 2, blocks, 4, part, 2, HALF).transpose(0, 5, 3, 1, 2, 4, 6)
    ffn = lax.all_gather(shares, BOTH, axis=1, tiled=True)
    half_units = ffn.shape[1] // 64
    ffn = ffn.reshape(2, 2, 2, 4, 4, half_units, D).transpose(1, 2, 3, 4, 0, 5, 6)
    ffn = ffn.reshape(2, 2, 4, 4, 2 * half_units, D)
    small = lax.all_gather(small, "head", axis=0, tiled=False)
    layer.sources = [(small[0], small[1]), (small[2], small[3])]
    biases = lax.all_gather(up_bias, BOTH, axis=0, tiled=True).reshape(2, 4, 8, half_units)
    biases = jnp.concatenate([biases[0], biases[1]], axis=-1)
    biases = jnp.pad(biases, ((0, 0), (0, 0), (0, 128 - 2 * half_units)))
    layer.start()
    layer.spots()
    for half in range(2):
        layer.bias(half)
        layer.project(half, None, (attn[half, 0], attn[half, 1]))
        layer.attend(half)
    layer.branch()
    ffn_grads, unit_grads = [], []
    for half in range(2):
        for core in range(2):
            grads, units = layer.feed(half, core, ffn[half, core], biases)
            ffn_grads.append(grads)
            unit_grads.append(units[..., half * half_units : half * half_units + half_units])
    layer.middle()
    attn_grads = []
    for half in range(2):
        layer.attend_back(half)
        attn_grads.append(jnp.stack(layer.weight_grads(half)))
    layer.table(0)
    layer.table(1)
    layer.end()
    parts = jnp.stack(attn_grads).astype(F32)
    parts = parts.transpose(0, 3, 4, 2, 5, 1, 6).reshape(groups, blocks, HEAD_DIM, D)
    own = lax.psum_scatter(parts, "head", scatter_dimension=0, tiled=True)
    own = lax.psum(own, "dp").reshape(blocks, 4, part, 2, HALF)
    both = jnp.stack(ffn_grads).astype(F32).reshape(2, 2, 16, 2, half_units, D).transpose(3, 0, 1, 2, 4, 5)
    own_ffn = lax.psum_scatter(both.reshape(2, -1, D), BOTH, scatter_dimension=1, tiled=True)
    units = lax.psum_scatter(jnp.stack(unit_grads).reshape(-1), BOTH, scatter_dimension=0, tiled=True)
    rows, slots = layer.vectors()
    slots = jnp.concatenate(slots).reshape(groups, -1, D)
    slots = lax.psum_scatter(slots, "head", scatter_dimension=0, tiled=True)[0]
    return own.transpose(3, 1, 0, 2, 4), own_ffn, units, lax.psum(rows, BOTH), lax.psum(slots, "dp")


NAMES = (
    "images",
    "mask_ids",
    "rel_index",
    "out_grad",
    "mask_token",
    "attn_gain",
    "attn_shift",
    "qkv_weight",
    "qv_bias",
    "rel_table",
    "out_weight",
    "out_bias",
    "attn_scale",
    "ffn_gain",
    "ffn_shift",
    "up_weight",
    "up_bias",
    "down_weight",
    "down_bias",
    "ffn_scale",
)


def on_device(mesh, *arrays):
    args = dict(zip(NAMES, arrays))
    rel_table, up_weight = args["rel_table"], args["up_weight"]
    table_rows, heads = rel_table.shape
    own_units = up_weight.shape[1]
    positions = jnp.arange(SEQ, dtype=jnp.int32)
    masked = jnp.any(args["mask_ids"][:, :, None] == positions, axis=1).astype(F32)[:, :, None]
    net = Butterfly(mesh)
    layer = Layer(None, args, masked, heads, net.head)

    own_stack = jnp.concatenate([jnp.swapaxes(args["qkv_weight"], 1, 2), args["out_weight"][None]], axis=0)
    own_stack = own_stack.reshape(4 * heads, HEAD_DIM, D)
    up_bias = args["up_bias"].astype(F32)
    lines = jnp.pad(rel_table.T, ((0, 0), (0, TABLE - table_rows))).reshape(2 * heads, HALF)
    shifts = jnp.pad(args["qv_bias"], ((0, 0), (0, HALF - heads * HEAD_DIM)))
    high_lines, high_shifts = lax.reduce_precision(lines, 8, 7), lax.reduce_precision(shifts, 8, 7)
    beside = jnp.pad(up_bias[None], ((0, 1), (HALF - 128, 128 - own_units)))
    small = jnp.concatenate(
        [high_lines, lines - high_lines, high_shifts + beside, shifts - high_shifts], axis=0
    ).astype(BF)[None]
    shares = jnp.stack([up_weight.T, args["down_weight"]])
    if net.dp == 8 and net.head == 4:
        gathered, own_ffn, units, rows, slots = run_butterfly(net, layer, own_stack, small, shares)
    else:
        gathered, own_ffn, units, rows, slots = run_plain(layer, own_stack, small, shares, up_bias)
    qkv_weight_grad, out_weight_grad = order(layer.place, gathered)
    (
        down_bias_grad,
        ffn_scale_grad,
        ffn_gain_grad,
        ffn_shift_grad,
        attn_scale_grad,
        out_bias_grad,
        attn_gain_grad,
        attn_shift_grad,
        mask_token_grad,
    ) = rows
    return (
        layer.output,
        layer.images_grad,
        mask_token_grad,
        attn_gain_grad,
        attn_shift_grad,
        jnp.swapaxes(qkv_weight_grad, 1, 2),
        slots[heads : heads + 2, : heads * HEAD_DIM],
        slots[:heads, :table_rows].T,
        out_weight_grad,
        out_bias_grad,
        attn_scale_grad,
        ffn_gain_grad,
        ffn_shift_grad,
        own_ffn[0].T,
        units,
        own_ffn[1],
        down_bias_grad,
        ffn_scale_grad,
    )


def solution(mesh):
    in_specs = (
        P(("dp", "head"), None, None),
        P(("dp", "head"), None),
        P(),
        P(("dp", "head"), None, None),
        P(),
        P(),
        P(),
        P(None, None, "head"),
        P(None, "head"),
        P(None, "head"),
        P("head", None),
        P(),
        P(),
        P(),
        P(),
        P(None, ("dp", "head")),
        P(("dp", "head")),
        P(("dp", "head"), None),
        P(),
        P(),
    )
    out_specs = (
        P(("dp", "head"), None, None),
        P(("dp", "head"), None, None),
        P(),
        P(),
        P(),
        P(None, None, "head"),
        P(None, "head"),
        P(None, "head"),
        P("head", None),
        P(),
        P(),
        P(),
        P(),
        P(None, ("dp", "head")),
        P(("dp", "head")),
        P(("dp", "head"), None),
        P(),
        P(),
    )
    return jax.shard_map(
        partial(on_device, mesh), mesh=mesh, in_specs=in_specs, out_specs=out_specs, check_vma=False
    )
```
